256 devices in a mesh: band: 4 (over x), gvec: 16 (over z, core), dom: 4 (over y).
Axes of the slice: x: 4, y: 4, z: 8, core: 2. Of those that a mesh axis runs over, the one named last changes fastest.
Arguments:
- coeffs: bfloat16 [16, 128, 128, 128], P(('band', 'dom'), 'gvec'), may hold values from -1.5 to 1.5
- v_local: bfloat16 [128, 128, 128], P(None, 'gvec'), may hold values from -4 to 4
- atom_pos: float32 [3, 262144], P(None, ('band', 'gvec', 'dom')), may hold values from -32 to 160
- atom_charge: float32 [262144], P(('band', 'gvec', 'dom')), may hold values from -1 to 1
- near_list: int32 [4096], P(('band', 'gvec', 'dom')), may hold values from 0 to 1023, as said below
- live_count: int32 [256], P(('band', 'gvec', 'dom')), may hold values from 0 to 16, as said below
Outputs:
- waves_new: bfloat16 [16, 128, 128, 128], P(('band', 'dom'), 'gvec')
- energies: float32 [16], P(('band', 'dom'))
- resid_ratio: float32 [16], P(('band', 'dom'))
- atom_force: float32 [3, 262144], P(None, ('band', 'gvec', 'dom'))
- totals: float32 [8], replicated
The draws below stay inside these ranges and needn't reach their ends.
Inputs may be any that keep to these rules, and one draw needn't show every extreme that they name: `live_count`: the counts of all devices sum to exactly 1024; some device has all 16 slots live; a device's live slots are its first ones. `near_list`: indices of the device's own atoms; the 16 entries of one device's block are distinct.
All inputs are finite; a program needn't handle non-finite values.
Results may differ from the reference program's by a relative error of at most 0.0045.
Values may be sent and summed in bfloat16 or wider, within the bound.
No kernel may reach another device: no remote copies, remote signals or barrier semaphores. Data moves between devices by JAX's collectives and lax.ppermute only.
A program may use at most 64 MiB of HBM per device.

```python
import jax
import jax.numpy as jnp
from jax import lax

GRID = 128
CAP = 16
ATOMS_DEV = 1024
BANDS = 16
NCH = 4096
LIVE = 1024
NATOMS = 262144


def draw_live_count(key, part):
    owners = NCH // CAP
    key_level, key_leader, key_order = jax.random.split(key, 3)
    levels = jax.random.randint(key_level, (owners,), 0, 3)
    leader = jax.random.randint(key_leader, (), 0, owners)
    levels = jnp.where(jnp.arange(owners) == leader, 3, levels)
    shuffle = jax.random.permutation(key_order, NCH)
    scores = jnp.repeat(levels, CAP) * NCH + shuffle
    _, chosen = lax.top_k(scores, LIVE)
    counts = jnp.zeros((owners,), jnp.int32).at[chosen // CAP].add(1)
    return counts.astype(jnp.int32)


def draw_near_list(key, part):
    owners = NCH // CAP
    key_lists = jax.random.split(key, owners)

    def pick_atoms(key_one):
        return jax.random.permutation(key_one, ATOMS_DEV)[:CAP]
    lists = jax.vmap(pick_atoms)(key_lists)
    return lists.reshape(-1).astype(jnp.int32)


def block_scale(key, dims, cuts, least, high):
    level, own = 1.0, jax.random.fold_in(key, 6)
    for axis_at, shards_of in cuts:
        draws = jnp.exp(jax.random.uniform(jax.random.fold_in(own, axis_at), (shards_of,), jnp.float32, least / len(cuts), high / len(cuts)))
        level = level * jnp.repeat(draws, dims[axis_at] // shards_of).reshape([-1 if axis == axis_at else 1 for axis in range(len(dims))])
    return level


def scatter_about(key, shape, spread, most, cuts=(), kind=jnp.bfloat16):
    result = jax.random.normal(key, shape, jnp.float32) * spread
    if len(cuts) > 0:
        result = block_scale(key, shape, cuts, -0.22, 0.18) * result
    return jnp.clip(result, min=-most, max=most).astype(kind)


def setup_inputs(seed: int = 0) -> dict:
    splits = jax.random.split(jax.random.key(seed), 7)
    return {
        "coeffs": scatter_about(splits[0], (BANDS, GRID, GRID, GRID), 0.25, 1.5, ((0, 16), (1, 16))),
        "v_local": scatter_about(splits[1], (GRID, GRID, GRID), 1.0, 4.0, ((1, 16),)),
        "atom_pos": jnp.clip(-32.0 + 192.0 * jax.random.uniform(splits[2], (3, NATOMS), jnp.float32) ** block_scale(splits[2], (3, NATOMS), ((1, 256),), -0.2, 0.2), -32.0, 160.0),
        "atom_charge": jnp.clip(jax.random.uniform(splits[3], (NATOMS,), jnp.float32, -1.0, 1.0) * block_scale(splits[3], (NATOMS,), ((0, 256),), -0.4, 0.0), -1.0, 1.0),
        "near_list": draw_near_list(jax.random.fold_in(splits[6], 71), 0),
        "live_count": draw_live_count(jax.random.fold_in(splits[6], 71), 0),
    }


sigma_fractions = (1.0 / 32.0, 1.0 / 16.0, 1.0 / 8.0, 1.0 / 4.0)
kernel_weights = (1.0, 0.5, 0.25, 0.125)
force_unit = 1.0 / 4096.0
step_size = 0.5

def cosine_table(length):
    points = jnp.arange(length).astype(jnp.float32)
    angles = jnp.pi * (points[:, None] + 0.5) * points[None, :] / length
    scales = jnp.where(points == 0.0, jnp.sqrt(1.0 / length), jnp.sqrt(2.0 / length))
    return (jnp.cos(angles) * scales[None, :]).astype(jnp.bfloat16)

def occupancy(band_index, band_total):
    shifted = band_index.astype(jnp.float32) - 0.5 * band_total
    return 2.0 / (1.0 + jnp.exp(shifted / (0.125 * band_total)))

def kernels(points, centres, extent):
    values = []
    slopes = []
    for fraction in sigma_fractions:
        exponent = 0.5 / (extent * fraction) ** 2
        offset = points[:, None] - centres[None, :]
        gauss_value = jnp.exp(-exponent * offset * offset)
        values.append(gauss_value)
        slopes.append(2.0 * exponent * offset * gauss_value)
    return (jnp.concatenate(values, axis=1), jnp.concatenate(slopes, axis=1))

def charge_work(charges, density, x_start, y_start, extent, block_width):
    x_count, y_count, z_count = density.shape
    density_rows = density.reshape(x_count * y_count, z_count).astype(jnp.bfloat16)
    x_points = (x_start + jnp.arange(x_count)).astype(jnp.float32)
    y_points = (y_start + jnp.arange(y_count)).astype(jnp.float32)
    z_points = jnp.arange(z_count).astype(jnp.float32)
    weights = jnp.array(kernel_weights, jnp.float32)
    slot_total = charges.shape[1]
    blocks = charges.reshape(4, slot_total // block_width, block_width).transpose(1, 0, 2)

    def one_block(potential, block_now):
        x_value, x_slope = kernels(x_points, block_now[0], extent)
        y_value, y_slope = kernels(y_points, block_now[1], extent)
        z_value, z_slope = kernels(z_points, block_now[2], extent)
        scaled = (weights[:, None] * block_now[3][None, :]).reshape(-1)
        plane = (x_value[:, None, :] * y_value[None, :, :]).reshape(x_count * y_count, -1).astype(jnp.bfloat16)
        depth = (scaled[None, :] * z_value).astype(jnp.bfloat16)
        potential = potential + lax.dot_general(plane, depth, (((1,), (1,)), ((), ())), preferred_element_type=jnp.float32)
        tables = jnp.concatenate([z_value, z_slope], axis=1).astype(jnp.bfloat16)
        projected = jnp.dot(density_rows, tables, preferred_element_type=jnp.float32).reshape(x_count, y_count, 2, -1)
        grid_part = projected[:, :, 0, :]
        slope_part = projected[:, :, 1, :]
        along_y = lax.optimization_barrier(jnp.sum(grid_part * y_value[None], axis=1))
        slope_y = lax.optimization_barrier(jnp.sum(grid_part * y_slope[None], axis=1))
        depth_y = lax.optimization_barrier(jnp.sum(slope_part * y_value[None], axis=1))
        force_x = lax.optimization_barrier(jnp.sum(x_slope * along_y, axis=0))
        force_y = lax.optimization_barrier(jnp.sum(x_value * slope_y, axis=0))
        force_z = lax.optimization_barrier(jnp.sum(x_value * depth_y, axis=0))
        stacked = jnp.stack([force_x, force_y, force_z]) * scaled[None, :]
        forces = -force_unit * lax.optimization_barrier(jnp.sum(stacked.reshape(3, len(kernel_weights), -1), axis=1))
        return (potential, forces)
    start = jnp.zeros((x_count * y_count, z_count), jnp.float32)
    potential, forces = lax.scan(one_block, start, blocks)
    return (potential.reshape(x_count, y_count, z_count), forces.transpose(1, 0, 2).reshape(3, slot_total))

def stress_terms(weighted, x_wave, y_wave):
    over_z = lax.optimization_barrier(jnp.sum(weighted, axis=2))
    over_y = lax.optimization_barrier(jnp.sum(weighted, axis=1))
    over_x = lax.optimization_barrier(jnp.sum(weighted, axis=0))
    stress_xx = jnp.sum(x_wave * x_wave * lax.optimization_barrier(jnp.sum(over_z, axis=1)))
    stress_yy = jnp.sum(y_wave * y_wave * lax.optimization_barrier(jnp.sum(over_z, axis=0)))
    stress_zz = jnp.sum(y_wave * y_wave * lax.optimization_barrier(jnp.sum(over_y, axis=0)))
    stress_xy = jnp.sum(x_wave[:, None] * y_wave[None, :] * over_z)
    stress_xz = jnp.sum(x_wave[:, None] * y_wave[None, :] * over_y)
    stress_yz = jnp.sum(y_wave[:, None] * y_wave[None, :] * over_x)
    return jnp.stack([stress_xx, stress_yy, stress_zz, stress_xy, stress_xz, stress_yz])

def forward_band(coeff_band, cosine_wide):
    sectioned = jnp.einsum('aql,zl->aqz', coeff_band.astype(jnp.float32), cosine_wide).astype(jnp.bfloat16)
    sectioned = jnp.einsum('aqz,yq->ayz', sectioned.astype(jnp.float32), cosine_wide).astype(jnp.bfloat16)
    return jnp.einsum('ayz,xa->xyz', sectioned.astype(jnp.float32), cosine_wide).astype(jnp.bfloat16)

def backward_band(applied, cosine_wide):
    sectioned = jnp.einsum('xyz,xa->ayz', applied.astype(jnp.float32), cosine_wide).astype(jnp.bfloat16)
    sectioned = jnp.einsum('ayz,yq->aqz', sectioned.astype(jnp.float32), cosine_wide).astype(jnp.bfloat16)
    return jnp.einsum('aqz,zl->aql', sectioned.astype(jnp.float32), cosine_wide)

def reference(coeffs, v_local, atom_pos, atom_charge, near_list, live_count):
    cosines = cosine_table(GRID)
    cosine_wide = cosines.astype(jnp.float32)
    occupied = occupancy(jnp.arange(BANDS), BANDS)

    def add_band(density, inputs):
        coeff_band, weight = inputs
        real_space = forward_band(coeff_band, cosine_wide).astype(jnp.float32)
        return (density + weight * real_space * real_space, None)
    density, _ = lax.scan(add_band, jnp.zeros((GRID, GRID, GRID), jnp.float32), (coeffs, occupied))
    owners = jnp.arange(NCH) // CAP
    slot_index = jnp.arange(NCH) % CAP
    live_mask = (slot_index < live_count[owners]).astype(jnp.float32)
    atom_index = (owners * ATOMS_DEV + near_list).astype(jnp.int32)
    picked = jnp.concatenate([atom_pos[:, atom_index], (atom_charge[atom_index] * live_mask)[None, :]], axis=0)
    target = jnp.where(live_mask > 0.5, jnp.cumsum(live_mask) - 1.0, 1.0 * LIVE).astype(jnp.int32)
    charges = jnp.zeros((4, LIVE), jnp.float32).at[:, target].set(picked, mode='drop')
    potential, forces = charge_work(charges, density, 0, 0, GRID, min(256, LIVE))
    padded = forces[:, jnp.minimum(target, LIVE - 1)] * live_mask[None, :]
    atom_force = jnp.zeros((3, NATOMS), jnp.float32).at[:, atom_index].add(padded)
    embedding = jnp.sum(density * potential) / GRID ** 3
    rounded = lax.optimization_barrier(potential.astype(jnp.bfloat16))
    field_total = v_local.astype(jnp.float32) + rounded.astype(jnp.float32)
    wave_index = jnp.arange(GRID).astype(jnp.float32) * (jnp.pi / GRID)
    kinetic = 0.5 * (wave_index[:, None, None] ** 2 + wave_index[None, :, None] ** 2 + wave_index[None, None, :] ** 2)

    def update_band(weighted, inputs):
        coeff_band, weight = inputs
        real_space = forward_band(coeff_band, cosine_wide)
        applied = (field_total * real_space.astype(jnp.float32)).astype(jnp.bfloat16)
        wave_field = backward_band(applied, cosine_wide)
        coeff_wide = coeff_band.astype(jnp.float32)
        image = kinetic * coeff_wide + wave_field
        norm_sq = jnp.sum(coeff_wide * coeff_wide)
        energy = jnp.sum(coeff_wide * image) / norm_sq
        residual = image - energy * coeff_wide
        ratio_band = jnp.sum(residual * residual) / norm_sq
        updated = (coeff_wide - step_size * residual / (1.0 + kinetic)).astype(jnp.bfloat16)
        return (weighted + weight * coeff_wide * coeff_wide, (updated, energy, ratio_band))
    weighted, outputs = lax.scan(update_band, jnp.zeros((GRID, GRID, GRID), jnp.float32), (coeffs, occupied))
    waves_new, energies, resid_ratio = outputs
    stress = stress_terms(weighted, wave_index, wave_index) / GRID ** 3
    band_energy = jnp.sum(occupied * energies) / BANDS
    totals = jnp.concatenate([stress, jnp.stack([embedding, band_energy])])
    return (waves_new, energies, resid_ratio, atom_force, totals)
```

```python
import jax
import jax.numpy as jnp
from jax import lax
from jax.sharding import PartitionSpec as P

sigma_fractions = (1.0 / 32.0, 1.0 / 16.0, 1.0 / 8.0, 1.0 / 4.0)
kernel_weights = (1.0, 0.5, 0.25, 0.125)
force_unit = 1.0 / 4096.0
step_size = 0.5


def cosine_table(length):
    points = jnp.arange(length).astype(jnp.float32)
    angles = jnp.pi * (points[:, None] + 0.5) * points[None, :] / length
    scales = jnp.where(points == 0.0, jnp.sqrt(1.0 / length), jnp.sqrt(2.0 / length))
    return (jnp.cos(angles) * scales[None, :]).astype(jnp.bfloat16)


def occupancy(band_index, band_total):
    shifted = band_index.astype(jnp.float32) - 0.5 * band_total
    return 2.0 / (1.0 + jnp.exp(shifted / (0.125 * band_total)))


def kernels(points, centres, extent):
    values = []
    slopes = []
    for fraction in sigma_fractions:
        exponent = 0.5 / (extent * fraction) ** 2
        offset = points[:, None] - centres[None, :]
        gauss_value = jnp.exp(-exponent * offset * offset)
        values.append(gauss_value)
        slopes.append(2.0 * exponent * offset * gauss_value)
    return (jnp.concatenate(values, axis=1), jnp.concatenate(slopes, axis=1))


def charge_work(charges, density, x_start, y_start, extent, block_width):
    x_count, y_count, z_count = density.shape
    density_rows = density.reshape(x_count * y_count, z_count).astype(jnp.bfloat16)
    x_points = (x_start + jnp.arange(x_count)).astype(jnp.float32)
    y_points = (y_start + jnp.arange(y_count)).astype(jnp.float32)
    z_points = jnp.arange(z_count).astype(jnp.float32)
    weights = jnp.array(kernel_weights, jnp.float32)
    slot_total = charges.shape[1]
    blocks = charges.reshape(4, slot_total // block_width, block_width).transpose(1, 0, 2)

    def one_block(potential, block_now):
        x_value, x_slope = kernels(x_points, block_now[0], extent)
        y_value, y_slope = kernels(y_points, block_now[1], extent)
        z_value, z_slope = kernels(z_points, block_now[2], extent)
        scaled = (weights[:, None] * block_now[3][None, :]).reshape(-1)
        plane = (
            (x_value[:, None, :] * y_value[None, :, :])
            .reshape(x_count * y_count, -1)
            .astype(jnp.bfloat16)
        )
        depth = (scaled[None, :] * z_value).astype(jnp.bfloat16)
        potential = potential + lax.dot_general(
            plane, depth, (((1,), (1,)), ((), ())), preferred_element_type=jnp.float32
        )
        tables = jnp.concatenate([z_value, z_slope], axis=1).astype(jnp.bfloat16)
        projected = jnp.dot(density_rows, tables, preferred_element_type=jnp.float32).reshape(
            x_count, y_count, 2, -1
        )
        grid_part = projected[:, :, 0, :]
        slope_part = projected[:, :, 1, :]
        along_y = jnp.sum(grid_part * y_value[None], axis=1)
        slope_y = jnp.sum(grid_part * y_slope[None], axis=1)
        depth_y = jnp.sum(slope_part * y_value[None], axis=1)
        force_x = jnp.sum(x_slope * along_y, axis=0)
        force_y = jnp.sum(x_value * slope_y, axis=0)
        force_z = jnp.sum(x_value * depth_y, axis=0)
        stacked = jnp.stack([force_x, force_y, force_z]) * scaled[None, :]
        forces = -force_unit * jnp.sum(stacked.reshape(3, len(kernel_weights), -1), axis=1)
        return (potential, forces)

    start = jnp.zeros((x_count * y_count, z_count), jnp.float32)
    potential, forces = lax.scan(one_block, start, blocks)
    return (
        potential.reshape(x_count, y_count, z_count),
        forces.transpose(1, 0, 2).reshape(3, slot_total),
    )


def stress_terms(weighted, x_wave, y_wave):
    over_z = jnp.sum(weighted, axis=2)
    over_y = jnp.sum(weighted, axis=1)
    over_x = jnp.sum(weighted, axis=0)
    stress_xx = jnp.sum(x_wave * x_wave * jnp.sum(over_z, axis=1))
    stress_yy = jnp.sum(y_wave * y_wave * jnp.sum(over_z, axis=0))
    stress_zz = jnp.sum(y_wave * y_wave * jnp.sum(over_y, axis=0))
    stress_xy = jnp.sum(x_wave[:, None] * y_wave[None, :] * over_z)
    stress_xz = jnp.sum(x_wave[:, None] * y_wave[None, :] * over_y)
    stress_yz = jnp.sum(y_wave[:, None] * y_wave[None, :] * over_x)
    return jnp.stack([stress_xx, stress_yy, stress_zz, stress_xy, stress_xz, stress_yz])


def spread_out(block, axes):
    copies = lax.axis_size(axes)
    many = jnp.broadcast_to(block[None], (copies,) + block.shape)
    got = lax.all_to_all(many, axes, split_axis=0, concat_axis=0, tiled=True)
    return got.reshape((copies * block.shape[0],) + block.shape[1:])


def per_device(coeffs, v_local, atom_pos, atom_charge, near_list, live_count):
    local_bands, x_local, extent, _ = coeffs.shape
    cosines = cosine_table(extent)
    gvec_id = lax.axis_index("gvec")
    group_id = lax.axis_index(("band", "dom"))
    groups = lax.axis_size(("band", "dom"))
    band_total = local_bands * groups
    cell_count = float(extent**3)
    band_ids = group_id * local_bands + jnp.arange(local_bands)
    weight = occupancy(band_ids, band_total)
    capacity = near_list.shape[0]
    live_mask = (jnp.arange(capacity) < live_count[0]).astype(jnp.float32)
    picked_pos = jnp.take(atom_pos, near_list, axis=1)
    picked_charge = jnp.take(atom_charge, near_list) * live_mask
    own_block = jnp.concatenate([picked_pos, picked_charge[None, :]], axis=0)
    all_blocks = spread_out(own_block.reshape(1, 4 * capacity), ("band", "gvec", "dom"))
    charges = all_blocks.reshape(-1, 4, capacity).transpose(1, 0, 2).reshape(4, -1)
    block_width = min(1024, charges.shape[1])
    sectioned = jnp.einsum(
        "naql,zl->naqz", coeffs, cosines, preferred_element_type=jnp.float32
    ).astype(jnp.bfloat16)
    sectioned = jnp.einsum(
        "naqz,yq->nayz", sectioned, cosines, preferred_element_type=jnp.float32
    ).astype(jnp.bfloat16)
    exchanged = lax.all_to_all(sectioned, "gvec", split_axis=2, concat_axis=1, tiled=True)
    real_space = jnp.einsum(
        "nayz,xa->nxyz", exchanged, cosines, preferred_element_type=jnp.float32
    ).astype(jnp.bfloat16)
    x_share = extent // groups
    y_share = exchanged.shape[2]
    x_start = group_id * x_share
    y_start = gvec_id * y_share
    wide_real = real_space.astype(jnp.float32)
    partial_value = jnp.sum(weight[:, None, None, None] * wide_real * wide_real, axis=0)
    shares = lax.all_to_all(
        partial_value.astype(jnp.bfloat16), ("band", "dom"), split_axis=0, concat_axis=0, tiled=True
    )
    density = jnp.sum(
        shares.reshape((groups, x_share) + shares.shape[1:]).astype(jnp.float32), axis=0
    )
    potential, forces = charge_work(charges, density, x_start, y_start, extent, block_width)
    slab_field = spread_out(potential.astype(jnp.bfloat16), ("band", "dom"))
    field_total = v_local.astype(jnp.float32) + slab_field.astype(jnp.float32)
    applied = (field_total[None] * wide_real).astype(jnp.bfloat16)
    embedding = jnp.sum(density * potential) / cell_count
    owners = lax.axis_size(("band", "gvec", "dom"))
    outgoing = forces.reshape(3, owners, capacity).transpose(1, 0, 2).reshape(owners, 3 * capacity)
    arrived = lax.all_to_all(
        outgoing, ("band", "gvec", "dom"), split_axis=0, concat_axis=0, tiled=True
    )
    mine = jnp.sum(arrived, axis=0).reshape(3, capacity)
    atom_force = jnp.zeros((3, atom_pos.shape[1]), jnp.float32).at[:, near_list].add(mine)
    back_one = jnp.einsum(
        "nxyz,xa->nayz", applied, cosines, preferred_element_type=jnp.float32
    ).astype(jnp.bfloat16)
    returned = lax.all_to_all(back_one, "gvec", split_axis=1, concat_axis=2, tiled=True)
    back_two = jnp.einsum(
        "nayz,yq->naqz", returned, cosines, preferred_element_type=jnp.float32
    ).astype(jnp.bfloat16)
    wave_field = jnp.einsum("naqz,zl->naql", back_two, cosines, preferred_element_type=jnp.float32)
    wave_step = jnp.pi / extent
    x_wave = (gvec_id * x_local + jnp.arange(x_local)).astype(jnp.float32) * wave_step
    y_wave = jnp.arange(extent).astype(jnp.float32) * wave_step
    kinetic = 0.5 * (
        x_wave[:, None, None] ** 2 + y_wave[None, :, None] ** 2 + y_wave[None, None, :] ** 2
    )
    coeff_wide = coeffs.astype(jnp.float32)
    image = kinetic[None] * coeff_wide + wave_field
    norm_sq = jnp.sum(coeff_wide * coeff_wide)
    intersection = jnp.sum(coeff_wide * image)
    local_energy = intersection / jnp.maximum(norm_sq, 1e-30)
    local_resid = jnp.sum((image - local_energy * coeff_wide) ** 2)
    weighted = jnp.sum(weight[:, None, None, None] * coeff_wide * coeff_wide, axis=0)
    stress_local = stress_terms(weighted, x_wave, y_wave) / cell_count
    local_totals = jnp.concatenate([stress_local, embedding[None]])
    partials = jnp.concatenate(
        [jnp.stack([norm_sq, intersection, local_resid]), local_totals]
    )
    gathered = spread_out(
        jnp.pad(partials, (0, 128 - partials.shape[0]))[None, :], ("band", "gvec", "dom")
    )
    by_group = gathered.reshape(
        lax.axis_size("band"), lax.axis_size("gvec"), lax.axis_size("dom"), -1
    ).transpose(0, 2, 1, 3).reshape(groups, -1, gathered.shape[-1])
    norm_all = jnp.sum(by_group[:, :, 0], axis=1)
    energy_all = jnp.sum(by_group[:, :, 1], axis=1) / norm_all
    each_energy = by_group[:, :, 1] / jnp.maximum(by_group[:, :, 0], 1e-30)
    resid_all = jnp.sum(
        by_group[:, :, 2] + by_group[:, :, 0] * (each_energy - energy_all[:, None]) ** 2, axis=1
    )
    spread = (jnp.arange(band_total) == group_id).astype(jnp.float32)
    energies = jnp.sum(spread * energy_all)[None]
    resid_ratio = jnp.sum(spread * (resid_all / norm_all))[None]
    residual = image - energies[:, None, None, None] * coeff_wide
    waves_new = (coeff_wide - step_size * residual / (1.0 + kinetic[None])).astype(jnp.bfloat16)
    band_energy = jnp.sum(occupancy(jnp.arange(band_total), band_total) * energy_all) / band_total
    summed = jnp.sum(by_group[:, :, 3:10], axis=(0, 1))
    totals = jnp.concatenate([summed, band_energy[None]])
    return (waves_new, energies, resid_ratio, atom_force, totals)


def solution(mesh):
    return jax.shard_map(
        per_device,
        mesh=mesh,
        in_specs=(
            P(("band", "dom"), "gvec", None, None),
            P(None, "gvec", None),
            P(None, ("band", "gvec", "dom")),
            P(("band", "gvec", "dom")),
            P(("band", "gvec", "dom")),
            P(("band", "gvec", "dom")),
        ),
        out_specs=(
            P(("band", "dom"), "gvec", None, None),
            P(("band", "dom")),
            P(("band", "dom")),
            P(None, ("band", "gvec", "dom")),
            P(),
        ),
        check_vma=False,
    )
```

```python
import jax
import jax.numpy as jnp
import numpy as np
from jax import lax
from jax.experimental import pallas as pl
from jax.experimental.pallas import tpu as pltpu
from jax.sharding import PartitionSpec as P

GRID = 128
CAP = 16
BANDS = 16
SHARES = 16
OWNERS = 256
LIVE = 1024
ATOMS = 1024
SIGMA_FRACTIONS = (1.0 / 32.0, 1.0 / 16.0, 1.0 / 8.0, 1.0 / 4.0)
KERNEL_WEIGHTS = (1.0, 0.5, 0.25, 0.125)
EXPONENTS = tuple(0.5 / (GRID * fraction) ** 2 for fraction in SIGMA_FRACTIONS)
FORCE_UNIT = 1.0 / 4096.0
STEP_SIZE = 0.5
WAVE_STEP = float(np.pi / GRID)
CELLS = float(GRID**3)
DEAD_MARK = 4096.0
SCALAR_LANE = 96
f32 = jnp.float32
bf16 = jnp.bfloat16
EVERY = ("gvec", "band", "dom")
GROUP = ("band", "dom")


def cosine_table():
    points = np.arange(GRID).astype(np.float32)
    angles = np.float32(np.pi) * (points[:, None] + np.float32(0.5)) * points[None, :]
    angles = (angles / np.float32(GRID)).astype(np.float32)
    scales = np.where(
        points == 0, np.sqrt(np.float32(1.0 / GRID)), np.sqrt(np.float32(2.0 / GRID))
    ).astype(np.float32)
    return jnp.asarray(np.cos(angles).astype(np.float32) * scales[None, :], bf16)


def dot_nn(a, b):
    return lax.dot_general(a, b, (((1,), (0,)), ((), ())), preferred_element_type=f32)


def dot_nt(a, b):
    return lax.dot_general(a, b, (((1,), (1,)), ((), ())), preferred_element_type=f32)


def iota(shape, dim):
    return lax.broadcasted_iota(jnp.int32, shape, dim)


def occupancy(band):
    return 2.0 / (1.0 + jnp.exp((band.astype(f32) - 0.5 * BANDS) / (0.125 * BANDS)))


def near_one_hot(near_ref):
    slot = iota((128, 128), 0) % CAP
    wanted = jnp.zeros((128, 128), jnp.int32)
    for s in range(CAP):
        wanted = jnp.where(slot == s, near_ref[s], wanted)
    lanes = iota((128, 128), 1)
    parts = [
        jnp.where(wanted == lanes + 128 * t, 1.0, 0.0).astype(bf16) for t in range(ATOMS // 128)
    ]
    return jnp.concatenate(parts, axis=1)


def halves(value):
    high = value.astype(bf16).astype(f32)
    return high, value - high


def pick_kernel(near_ref, count_ref, pos_ref, charge_ref, out_ref):
    one_hot = near_one_hot(near_ref)
    wide = jnp.concatenate([pos_ref[...], charge_ref[...]], axis=0)
    high, low = halves(wide)
    both = jnp.concatenate([high, low], axis=0).astype(bf16)
    picked = dot_nt(both, one_hot)
    lane = iota((8, 128), 1)
    row = jnp.sum(jnp.where(lane // CAP == iota((8, 128), 0), picked, 0.0), axis=0, keepdims=True)
    lane_row = iota((1, 128), 1)
    dead = (lane_row < CAP) & (lane_row >= count_ref[0])
    row = jnp.where(dead, DEAD_MARK, row)
    out_ref[...] = jnp.broadcast_to(row[None], out_ref.shape)


def section_kernel(coeffs_ref, table_ref, out_ref, wide_ref):
    table = table_ref[...]
    along_z = dot_nt(coeffs_ref[...].reshape(1024, GRID), table).astype(bf16)
    for a in range(8):
        wide_ref[:, a, :] = dot_nn(table, along_z[a * GRID : (a + 1) * GRID])
    out_ref[:, :64, :] = wide_ref[...].reshape(SHARES, 64, GRID).astype(bf16)
    out_ref[:, 64:, :] = jnp.zeros((SHARES, 16, GRID), bf16)


def stats_kernel(where_ref, coeffs_ref, out_ref):
    first = where_ref[0] * 8
    q_wave = iota((GRID, GRID), 0).astype(f32) * WAVE_STEP
    l_wave = iota((1, GRID), 1).astype(f32) * WAVE_STEP
    sums = [jnp.zeros((1, GRID), f32) for _ in range(7)]
    for a in range(8):
        a_wave = (first + a).astype(f32) * WAVE_STEP
        value = coeffs_ref[a].astype(f32)
        square = value * value
        scaled = square * q_wave
        flat = jnp.sum(square, axis=0, keepdims=True)
        once = jnp.sum(scaled, axis=0, keepdims=True)
        twice = jnp.sum(scaled * q_wave, axis=0, keepdims=True)
        terms = (
            flat,
            a_wave * a_wave * flat,
            twice,
            l_wave * l_wave * flat,
            a_wave * once,
            a_wave * l_wave * flat,
            l_wave * once,
        )
        sums = [total + term for total, term in zip(sums, terms)]
    lane = iota((1, GRID), 1)
    weight = occupancy(jnp.full((1, 1), where_ref[1], jnp.int32)) / CELLS
    row = jnp.where(lane == SCALAR_LANE, jnp.sum(sums[0]), 0.0)
    for i in range(1, 7):
        value = jnp.sum(sums[i], axis=1, keepdims=True) * weight
        row = jnp.where(lane == SCALAR_LANE + 2 + i, value, row)
    out_ref[...] = row


def gauss_values(offset):
    wide = jnp.exp(-EXPONENTS[3] * offset * offset)
    values = [wide]
    for _ in range(3):
        square = values[0] * values[0]
        values.insert(0, square * square)
    return values


def slot_place(blocks):
    lane = iota((OWNERS, 128), 1)
    live = jnp.where((blocks < 1000.0) & (lane < CAP), 1.0, 0.0).astype(bf16)
    return live


def place_by_row(live):
    ones = jnp.ones((128, 128), bf16)
    counts = dot_nn(live, ones)
    before = jnp.where(iota((OWNERS, OWNERS), 1) < iota((OWNERS, OWNERS), 0), 1.0, 0.0).astype(bf16)
    starts = dot_nn(before, counts.astype(bf16))
    return counts, starts


def place_by_lane(live):
    ones = jnp.ones((128, 128), bf16)
    counts = dot_nt(ones, live)
    before = jnp.where(iota((OWNERS, OWNERS), 0) < iota((OWNERS, OWNERS), 1), 1.0, 0.0).astype(bf16)
    starts = dot_nn(counts.astype(bf16), before)
    return counts, starts


def slot_masks(live):
    counts, starts = place_by_lane(live)
    place = iota((LIVE, OWNERS), 0).astype(f32)
    start_row = starts[:1]
    owner = (place >= start_row) & (place < start_row + counts[:1])
    owner = jnp.where(owner, 1.0, 0.0).astype(bf16)
    coarse = jnp.floor(starts * 0.125)
    fine = starts - 8.0 * coarse
    own_start = 8.0 * dot_nt(owner, coarse.astype(bf16)) + dot_nt(owner, fine.astype(bf16))
    slot = iota((LIVE, 128), 0).astype(f32) - own_start
    chosen = slot == (iota((LIVE, 128), 1) % CAP).astype(f32)
    return owner, chosen


def field_kernel(
    where_ref, got_ref, local_ref, table_ref, back_ref, density_ref, slots_ref, energy_ref,
    local_wide, back_wide, gx_ref, depth_ref,
):
    table = table_ref[...]
    got = got_ref[...].astype(f32)
    blocks = got[:, 64:, :].reshape(OWNERS, 128)
    owner, chosen = slot_masks(slot_place(blocks))
    rows = jnp.where(chosen, dot_nn(owner, blocks.astype(bf16)), 0.0).astype(bf16)
    pick = jnp.where(iota((8, 128), 1) // CAP == iota((8, 128), 0), 1.0, 0.0).astype(bf16)
    slots = dot_nt(pick, rows)
    slots = slots[:4] + slots[4:]
    slots_ref[...] = jnp.concatenate([slots, slots], axis=0)
    points = iota((GRID, LIVE), 0).astype(f32)
    y_points = (where_ref[0] * 8 + iota((8, LIVE), 0)).astype(f32)
    gx_values = gauss_values(points - slots[0:1])
    gy_values = gauss_values(y_points - slots[1:2])
    gz_values = gauss_values(points - slots[2:3])
    for k in range(4):
        gx_ref[k] = gx_values[k].astype(bf16)
        depth_ref[k] = gz_values[k] * (slots[3:4] * KERNEL_WEIGHTS[k])
    local_wide[...] = local_ref[...].astype(f32)
    weight = occupancy(jnp.full((1, 1), where_ref[1], jnp.int32))
    energy = jnp.zeros((1, GRID), f32)
    for y in range(8):
        potential = jnp.zeros((GRID, GRID), f32)
        for k in range(4):
            plane = (depth_ref[k] * gy_values[k][y : y + 1]).astype(bf16)
            potential = potential + dot_nt(gx_ref[k], plane)
        mine = got[:, y * 8 : (y + 1) * 8, :].reshape(GRID, GRID).astype(bf16)
        real = dot_nn(table, mine).astype(bf16).astype(f32)
        density = weight * real * real
        density_ref[y] = density
        energy = energy + jnp.sum(density * potential, axis=0, keepdims=True)
        field = local_wide[:, y, :] + potential.astype(bf16).astype(f32)
        applied = (field * real).astype(bf16)
        back = lax.dot_general(
            table, applied, (((0,), (0,)), ((), ())), preferred_element_type=f32
        )
        back_wide[:, y * 8 : (y + 1) * 8, :] = back.reshape(SHARES, 8, GRID)
    back_ref[...] = back_wide[...].astype(bf16)
    total = jnp.sum(energy, axis=1, keepdims=True) / CELLS
    energy_ref[...] = jnp.where(iota((1, GRID), 1) == SCALAR_LANE + 9, total, 0.0)


def force_kernel(
    where_ref, got_ref, density_ref, slots_ref, out_ref,
    turned_ref, x_ref, gz_ref, hz_ref, gy_ref, hy_ref, sum_ref,
):
    for y in range(8):
        turned_ref[y] = density_ref[y].T.astype(bf16)
    slots = slots_ref[...]
    points = iota((GRID, LIVE), 0).astype(f32)
    x_offset = points - slots[0:1]
    y_offset = (where_ref[0] * 8 + iota((8, LIVE), 0)).astype(f32) - slots[1:2]
    z_offset = points - slots[2:3]
    gx_values = gauss_values(x_offset)
    gy_values = gauss_values(y_offset)
    gz_values = gauss_values(z_offset)
    for k in range(4):
        slope = 2.0 * EXPONENTS[k]
        x_ref[k, 0] = gx_values[k].astype(bf16)
        x_ref[k, 1] = (slope * x_offset * gx_values[k]).astype(bf16)
        gy_ref[k] = gy_values[k]
        hy_ref[k] = slope * y_offset * gy_values[k]
        scale = KERNEL_WEIGHTS[k] * slots[3:4]
        gz_ref[k] = gz_values[k] * scale
        hz_ref[k] = slope * z_offset * gz_values[k] * scale

    @pl.loop(0, LIVE // 128)
    def _(chunk):
        lanes = pl.ds(pl.multiple_of(chunk * 128, 128), 128)
        force_x = jnp.zeros((1, 128), f32)
        force_y = jnp.zeros((1, 128), f32)
        force_z = jnp.zeros((1, 128), f32)
        for k in range(4):
            both = jnp.concatenate([x_ref[k, 0, :, lanes], x_ref[k, 1, :, lanes]], axis=1)
            value_y = gy_ref[k, :, lanes]
            slope_y = hy_ref[k, :, lanes]
            with_x = jnp.zeros((GRID, 128), f32)
            with_y = jnp.zeros((GRID, 128), f32)
            with_z = jnp.zeros((GRID, 128), f32)
            for y in range(8):
                part = dot_nn(turned_ref[y], both)
                with_x = with_x + part[:, 128:] * value_y[y : y + 1]
                with_y = with_y + part[:, :128] * slope_y[y : y + 1]
                with_z = with_z + part[:, :128] * value_y[y : y + 1]
            value_z = gz_ref[k, :, lanes]
            force_x = force_x + jnp.sum(with_x * value_z, axis=0, keepdims=True)
            force_y = force_y + jnp.sum(with_y * value_z, axis=0, keepdims=True)
            force_z = force_z + jnp.sum(with_z * hz_ref[k, :, lanes], axis=0, keepdims=True)
        sum_ref[0:1, lanes] = force_x
        sum_ref[1:2, lanes] = force_y
        sum_ref[2:3, lanes] = force_z

    forces = sum_ref[0:3, :] * -FORCE_UNIT
    high, low = halves(forces)
    stacked = jnp.concatenate([high, low, jnp.zeros((2, LIVE), f32)], axis=0)
    live = slot_place(got_ref[:, 64:, :].astype(f32).reshape(OWNERS, 128))
    owner, chosen = slot_masks(live)
    spread = jnp.where(iota((8, 128), 1) // CAP == iota((8, 128), 0), 1.0, 0.0).astype(bf16)
    per_slot = lax.dot_general(
        stacked.astype(bf16), spread, (((0,), (0,)), ((), ())), preferred_element_type=f32
    )
    per_slot = jnp.where(chosen, per_slot, 0.0).astype(bf16)
    counts, starts = place_by_row(live)
    place = iota((OWNERS, 128), 1).astype(f32)
    total = jnp.zeros((OWNERS, 128), f32)
    for t in range(LIVE // 128):
        here = place + (128.0 * t)
        held = jnp.where((here >= starts) & (here < starts + counts), 1.0, 0.0).astype(bf16)
        total = total + dot_nn(held, per_slot[t * 128 : (t + 1) * 128])
    out_ref[...] = total


def wave_tables(where_ref):
    q_wave = iota((GRID, GRID), 0).astype(f32) * WAVE_STEP
    l_wave = iota((GRID, GRID), 1).astype(f32) * WAVE_STEP
    return q_wave * q_wave + l_wave * l_wave


def kinetic_of(where_ref, plane_waves, a):
    a_wave = (where_ref[0] * 8 + a).astype(f32) * WAVE_STEP
    return 0.5 * (a_wave * a_wave + plane_waves)


def image_kernel(
    where_ref, got_ref, coeffs_ref, table_ref, force_ref, stats_ref, energy_ref,
    image_ref, out_ref, wide_ref,
):
    table = table_ref[...]
    wide_ref[...] = got_ref[...].astype(f32).reshape(GRID, 8, GRID)
    plane_waves = wave_tables(where_ref)
    overlap = jnp.zeros((1, GRID), f32)
    norm = jnp.zeros((1, GRID), f32)
    for a in range(8):
        along_y = lax.dot_general(
            table, wide_ref[:, a, :].astype(bf16), (((0,), (0,)), ((), ())),
            preferred_element_type=f32,
        ).astype(bf16)
        coeff = coeffs_ref[a].astype(f32)
        image = kinetic_of(where_ref, plane_waves, a) * coeff + dot_nn(along_y, table)
        image_ref[a] = image
        overlap = overlap + jnp.sum(coeff * image, axis=0, keepdims=True)
        norm = norm + jnp.sum(coeff * coeff, axis=0, keepdims=True)
    overlap = jnp.sum(overlap, axis=1, keepdims=True)
    norm = jnp.sum(norm, axis=1, keepdims=True)
    mean = overlap / jnp.maximum(norm, 1e-30)
    spread = jnp.zeros((1, GRID), f32)
    for a in range(8):
        residual = image_ref[a] - mean * coeffs_ref[a].astype(f32)
        spread = spread + jnp.sum(residual * residual, axis=0, keepdims=True)
    spread = jnp.sum(spread, axis=1, keepdims=True)
    lane = iota((1, GRID), 1)
    row = stats_ref[...] + energy_ref[...]
    row = jnp.where(lane == SCALAR_LANE + 1, overlap, row)
    row = jnp.where(lane == SCALAR_LANE + 2, spread, row)
    out_ref[...] = force_ref[...] + row


def final_kernel(
    where_ref, near_ref, count_ref, got_ref, image_ref, coeffs_ref,
    waves_ref, force_ref, energy_ref, ratio_ref, totals_ref,
):
    got = got_ref[...]
    by_band = jnp.sum(got.reshape(SHARES, BANDS, 128), axis=0)
    column = lambda i: slice(SCALAR_LANE + i, SCALAR_LANE + i + 1)
    norms = by_band[:, column(0)]
    energies = by_band[:, column(1)] / norms
    band = iota((BANDS, 1), 0)
    own = band == where_ref[1]
    energy = jnp.sum(jnp.where(own, energies, 0.0), axis=0, keepdims=True)
    norm = jnp.sum(jnp.where(own, norms, 0.0), axis=0, keepdims=True)
    part_norm = got[:, column(0)]
    part_energy = got[:, column(1)] / jnp.maximum(part_norm, 1e-30)
    shift = part_energy - energy
    spread = got[:, column(2)] + part_norm * shift * shift
    own_rows = iota((OWNERS, 1), 0) % BANDS == where_ref[1]
    squares = jnp.sum(jnp.where(own_rows, spread, 0.0), axis=0, keepdims=True)
    energy_ref[...] = energy
    ratio_ref[...] = squares / norm
    everything = jnp.sum(by_band, axis=0, keepdims=True)
    band_energy = jnp.sum(occupancy(band) * energies, axis=0, keepdims=True) / BANDS
    totals_ref[...] = jnp.concatenate(
        [everything[:, SCALAR_LANE + 3 : SCALAR_LANE + 10], band_energy], axis=1
    )
    plane_waves = wave_tables(where_ref)
    for a in range(8):
        coeff = coeffs_ref[a].astype(f32)
        residual = image_ref[a] - energy * coeff
        kinetic = kinetic_of(where_ref, plane_waves, a)
        waves_ref[a] = (coeff - STEP_SIZE * residual / (1.0 + kinetic)).astype(bf16)
    lane = iota((8, 128), 1)
    wanted = (lane // CAP) % 3 == iota((8, 128), 0)
    wanted = wanted & (lane < SCALAR_LANE) & (lane % CAP < count_ref[0])
    split = jnp.where(wanted, everything, 0.0)
    high, rest = halves(split)
    middle, low = halves(rest)
    pieces = jnp.concatenate([high, middle, low, jnp.zeros_like(low)], axis=0).astype(bf16)
    placed = dot_nn(pieces, near_one_hot(near_ref))
    forces = placed[0:8] + placed[8:16] + placed[16:24]
    force_ref[...] = forces[:3]


VMEM = pl.BlockSpec(memory_space=pltpu.VMEM)
SMEM = pl.BlockSpec(memory_space=pltpu.SMEM)


def call(kernel, inputs, outputs, scratch=(), cost=2000000000):
    specs = [SMEM if x.dtype == jnp.int32 else VMEM for x in inputs]
    shapes = [jax.ShapeDtypeStruct(*out) for out in outputs]
    return pl.pallas_call(
        kernel,
        out_shape=shapes,
        in_specs=specs,
        out_specs=[VMEM] * len(shapes),
        scratch_shapes=[pltpu.VMEM(*one) for one in scratch],
        compiler_params=pltpu.CompilerParams(vmem_limit_bytes=40 * 1024 * 1024),
        cost_estimate=pl.CostEstimate(flops=cost, bytes_accessed=1000000, transcendentals=0),
    )(*inputs)


def exchange(block, axes):
    return lax.all_to_all(block, axes, split_axis=0, concat_axis=0, tiled=True)


def per_device(coeffs, v_local, atom_pos, atom_charge, near_list, live_count):
    table = cosine_table()
    coeffs = coeffs[0]
    where = jnp.stack([lax.axis_index("gvec"), lax.axis_index(GROUP)]).astype(jnp.int32)
    (own,) = call(
        pick_kernel,
        [near_list, live_count, atom_pos, atom_charge.reshape(1, ATOMS)],
        [((SHARES, 1, 128), f32)],
    )
    group = exchange(own, GROUP)
    (sections,) = call(
        section_kernel,
        [coeffs, table],
        [((SHARES, 80, GRID), bf16)],
        [((GRID, 8, GRID), f32)],
    )
    blocks = jnp.broadcast_to(group.reshape(1, SHARES, 128), (SHARES, SHARES, 128)).astype(bf16)
    sections = lax.dynamic_update_slice(sections, blocks, (0, 64, 0))
    got = exchange(sections, "gvec")
    (stats,) = call(stats_kernel, [where, coeffs], [((1, 128), f32)])
    back, density, slots, energy = call(
        field_kernel,
        [where, got, v_local, table],
        [
            ((SHARES, 64, GRID), bf16),
            ((8, GRID, GRID), f32),
            ((8, LIVE), f32),
            ((1, 128), f32),
        ],
        [
            ((GRID, 8, GRID), f32),
            ((SHARES, 64, GRID), f32),
            ((4, GRID, LIVE), bf16),
            ((4, GRID, LIVE), f32),
        ],
    )
    returned = exchange(back, "gvec")
    (forces,) = call(
        force_kernel,
        [where, got, density, slots],
        [((OWNERS, 128), f32)],
        [
            ((8, GRID, GRID), bf16),
            ((4, 2, GRID, LIVE), bf16),
            ((4, GRID, LIVE), f32),
            ((4, GRID, LIVE), f32),
            ((4, 8, LIVE), f32),
            ((4, 8, LIVE), f32),
            ((8, LIVE), f32),
        ],
    )
    image, message = call(
        image_kernel,
        [where, returned, coeffs, table, forces, stats, energy],
        [((8, GRID, GRID), f32), ((OWNERS, 128), f32)],
        [((GRID, 8, GRID), f32)],
    )
    arrived = exchange(message.reshape(OWNERS, 1, 128), EVERY).reshape(OWNERS, 128)
    waves, atom_force, energies, ratio, totals = call(
        final_kernel,
        [where, near_list, live_count, arrived, image, coeffs],
        [
            ((8, GRID, GRID), bf16),
            ((3, ATOMS), f32),
            ((1, 1), f32),
            ((1, 1), f32),
            ((1, 8), f32),
        ],
    )
    return (waves[None], energies.reshape(1), ratio.reshape(1), atom_force, totals.reshape(8))


def solution(mesh):
    return jax.shard_map(
        per_device,
        mesh=mesh,
        in_specs=(
            P(("band", "dom"), "gvec", None, None),
            P(None, "gvec", None),
            P(None, ("band", "gvec", "dom")),
            P(("band", "gvec", "dom")),
            P(("band", "gvec", "dom")),
            P(("band", "gvec", "dom")),
        ),
        out_specs=(
            P(("band", "dom"), "gvec", None, None),
            P(("band", "dom")),
            P(("band", "dom")),
            P(None, ("band", "gvec", "dom")),
            P(),
        ),
        check_vma=False,
    )
```

```python
import jax
import jax.numpy as jnp
import numpy as np
from jax import lax
from jax.experimental import pallas as pl
from jax.experimental.pallas import tpu as pltpu
from jax.sharding import PartitionSpec as P

GRID = 128
CAP = 16
BANDS = 16
SHARES = 16
OWNERS = 256
LIVE = 1024
ATOMS = 1024
SIGMA_FRACTIONS = (1.0 / 32.0, 1.0 / 16.0, 1.0 / 8.0, 1.0 / 4.0)
KERNEL_WEIGHTS = (1.0, 0.5, 0.25, 0.125)
EXPONENTS = tuple(0.5 / (GRID * fraction) ** 2 for fraction in SIGMA_FRACTIONS)
FORCE_UNIT = 1.0 / 4096.0
STEP_SIZE = 0.5
WAVE_STEP = float(np.pi / GRID)
CELLS = float(GRID**3)
DEAD_MARK = 4096.0
SCALAR_LANE = 96
f32 = jnp.float32
bf16 = jnp.bfloat16
EVERY = ("gvec", "band", "dom")
GROUP = ("band", "dom")


def cosine_table():
    points = np.arange(GRID).astype(np.float32)
    angles = np.float32(np.pi) * (points[:, None] + np.float32(0.5)) * points[None, :]
    angles = (angles / np.float32(GRID)).astype(np.float32)
    scales = np.where(
        points == 0, np.sqrt(np.float32(1.0 / GRID)), np.sqrt(np.float32(2.0 / GRID))
    ).astype(np.float32)
    return jnp.asarray(np.cos(angles).astype(np.float32) * scales[None, :], bf16)


def dot_nn(a, b):
    return lax.dot_general(a, b, (((1,), (0,)), ((), ())), preferred_element_type=f32)


def dot_nt(a, b):
    return lax.dot_general(a, b, (((1,), (1,)), ((), ())), preferred_element_type=f32)


def iota(shape, dim):
    return lax.broadcasted_iota(jnp.int32, shape, dim)


def occupancy(band):
    return 2.0 / (1.0 + jnp.exp((band.astype(f32) - 0.5 * BANDS) / (0.125 * BANDS)))


def near_one_hot(near_ref):
    slot = iota((128, 128), 0) % CAP
    wanted = jnp.zeros((128, 128), jnp.int32)
    for s in range(CAP):
        wanted = jnp.where(slot == s, near_ref[s], wanted)
    lanes = iota((128, 128), 1)
    parts = [
        jnp.where(wanted == lanes + 128 * t, 1.0, 0.0).astype(bf16) for t in range(ATOMS // 128)
    ]
    return jnp.concatenate(parts, axis=1)


def halves(value):
    high = value.astype(bf16).astype(f32)
    return high, value - high


def pick_kernel(
    near_hbm, count_hbm, pos_hbm, charge_hbm, out_ref,
    near_ref, count_ref, pos_ref, charge_ref, sems,
):
    moves = [
        pltpu.make_async_copy(near_hbm, near_ref, sems.at[0]),
        pltpu.make_async_copy(count_hbm, count_ref, sems.at[1]),
        pltpu.make_async_copy(pos_hbm, pos_ref, sems.at[2]),
        pltpu.make_async_copy(charge_hbm, charge_ref, sems.at[3]),
    ]
    for move in moves:
        move.start()
    for move in moves:
        move.wait()
    one_hot = near_one_hot(near_ref)
    wide = jnp.concatenate([pos_ref[...], charge_ref[...]], axis=0)
    high, low = halves(wide)
    both = jnp.concatenate([high, low], axis=0).astype(bf16)
    picked = dot_nt(both, one_hot)
    lane = iota((8, 128), 1)
    row = jnp.sum(jnp.where(lane // CAP == iota((8, 128), 0), picked, 0.0), axis=0, keepdims=True)
    lane_row = iota((1, 128), 1)
    dead = (lane_row < CAP) & (lane_row >= count_ref[0])
    row = jnp.where(dead, DEAD_MARK, row)
    out_ref[...] = jnp.broadcast_to(row, out_ref.shape)


def section_kernel(coeffs_ref, table_ref, out_ref, wide_ref):
    table = table_ref[...]
    along_z = dot_nt(coeffs_ref[...].reshape(1024, GRID), table).astype(bf16)
    for a in range(8):
        wide_ref[:, a, :] = dot_nn(table, along_z[a * GRID : (a + 1) * GRID])
    out_ref[...] = wide_ref[...].reshape(SHARES, 64, GRID).astype(bf16)


def stats_kernel(where_ref, coeffs_ref, out_ref):
    first = where_ref[0] * 8
    q_wave = iota((GRID, GRID), 0).astype(f32) * WAVE_STEP
    l_wave = iota((1, GRID), 1).astype(f32) * WAVE_STEP
    sums = [jnp.zeros((1, GRID), f32) for _ in range(7)]
    for a in range(8):
        a_wave = (first + a).astype(f32) * WAVE_STEP
        value = coeffs_ref[a].astype(f32)
        square = value * value
        scaled = square * q_wave
        flat = jnp.sum(square, axis=0, keepdims=True)
        once = jnp.sum(scaled, axis=0, keepdims=True)
        twice = jnp.sum(scaled * q_wave, axis=0, keepdims=True)
        terms = (
            flat,
            a_wave * a_wave * flat,
            twice,
            l_wave * l_wave * flat,
            a_wave * once,
            a_wave * l_wave * flat,
            l_wave * once,
        )
        sums = [total + term for total, term in zip(sums, terms)]
    lane = iota((1, GRID), 1)
    weight = occupancy(jnp.full((1, 1), where_ref[1], jnp.int32)) / CELLS
    row = jnp.where(lane == SCALAR_LANE, jnp.sum(sums[0]), 0.0)
    for i in range(1, 7):
        value = jnp.sum(sums[i], axis=1, keepdims=True) * weight
        row = jnp.where(lane == SCALAR_LANE + 2 + i, value, row)
    out_ref[...] = row


def gauss_values(offset):
    wide = jnp.exp(-EXPONENTS[3] * offset * offset)
    values = [wide]
    for _ in range(3):
        square = values[0] * values[0]
        values.insert(0, square * square)
    return values


def slot_place(blocks):
    lane = iota((OWNERS, 128), 1)
    live = jnp.where((blocks < 1000.0) & (lane < CAP), 1.0, 0.0).astype(bf16)
    return live


def place_by_row(live):
    ones = jnp.ones((128, 128), bf16)
    counts = dot_nn(live, ones)
    before = jnp.where(iota((OWNERS, OWNERS), 1) < iota((OWNERS, OWNERS), 0), 1.0, 0.0).astype(bf16)
    starts = dot_nn(before, counts.astype(bf16))
    return counts, starts


def place_by_lane(live):
    ones = jnp.ones((128, 128), bf16)
    counts = dot_nt(ones, live)
    before = jnp.where(iota((OWNERS, OWNERS), 0) < iota((OWNERS, OWNERS), 1), 1.0, 0.0).astype(bf16)
    starts = dot_nn(counts.astype(bf16), before)
    return counts, starts


def slot_masks(live):
    counts, starts = place_by_lane(live)
    place = iota((LIVE, OWNERS), 0).astype(f32)
    start_row = starts[:1]
    owner = (place >= start_row) & (place < start_row + counts[:1])
    owner = jnp.where(owner, 1.0, 0.0).astype(bf16)
    coarse = jnp.floor(starts * 0.125)
    fine = starts - 8.0 * coarse
    own_start = 8.0 * dot_nt(owner, coarse.astype(bf16)) + dot_nt(owner, fine.astype(bf16))
    slot = iota((LIVE, 128), 0).astype(f32) - own_start
    chosen = slot == (iota((LIVE, 128), 1) % CAP).astype(f32)
    return owner, chosen


def potential_kernel(where_ref, blocks_ref, potential_ref, slots_ref, gx_ref, depth_ref):
    blocks = blocks_ref[...]
    owner, chosen = slot_masks(slot_place(blocks))
    rows = jnp.where(chosen, dot_nn(owner, blocks.astype(bf16)), 0.0).astype(bf16)
    pick = jnp.where(iota((8, 128), 1) // CAP == iota((8, 128), 0), 1.0, 0.0).astype(bf16)
    slots = dot_nt(pick, rows)
    slots = slots[:4] + slots[4:]
    slots_ref[...] = jnp.concatenate([slots, slots], axis=0)
    points = iota((GRID, LIVE), 0).astype(f32)
    y_points = (where_ref[0] * 8 + iota((8, LIVE), 0)).astype(f32)
    gx_values = gauss_values(points - slots[0:1])
    gy_values = gauss_values(y_points - slots[1:2])
    gz_values = gauss_values(points - slots[2:3])
    for k in range(4):
        gx_ref[k] = gx_values[k].astype(bf16)
        depth_ref[k] = gz_values[k] * (slots[3:4] * KERNEL_WEIGHTS[k])
    for y in range(8):
        potential = jnp.zeros((GRID, GRID), f32)
        for k in range(4):
            plane = (depth_ref[k] * gy_values[k][y : y + 1]).astype(bf16)
            potential = potential + dot_nt(gx_ref[k], plane)
        potential_ref[y] = potential


def field_kernel(
    where_ref, got_ref, local_ref, table_ref, potential_ref, stats_ref,
    back_ref, density_ref, energy_ref, local_wide, back_wide,
):
    table = table_ref[...]
    got = got_ref[...].astype(f32)
    local_wide[...] = local_ref[...].astype(f32)
    weight = occupancy(jnp.full((1, 1), where_ref[1], jnp.int32))
    energy = jnp.zeros((1, GRID), f32)
    for y in range(8):
        potential = potential_ref[y]
        mine = got[:, y * 8 : (y + 1) * 8, :].reshape(GRID, GRID).astype(bf16)
        real = dot_nn(table, mine).astype(bf16).astype(f32)
        density = weight * real * real
        density_ref[y] = density
        energy = energy + jnp.sum(density * potential, axis=0, keepdims=True)
        field = local_wide[:, y, :] + potential.astype(bf16).astype(f32)
        applied = (field * real).astype(bf16)
        back = lax.dot_general(
            table, applied, (((0,), (0,)), ((), ())), preferred_element_type=f32
        )
        back_wide[:, y * 8 : (y + 1) * 8, :] = back.reshape(SHARES, 8, GRID)
    back_ref[...] = back_wide[...].astype(bf16)
    total = jnp.sum(energy, axis=1, keepdims=True) / CELLS
    lane = iota((1, GRID), 1)
    energy_ref[...] = stats_ref[...] + jnp.where(lane == SCALAR_LANE + 9, total, 0.0)


def force_kernel(
    where_ref, blocks_ref, density_ref, slots_ref, out_ref,
    turned_ref, x_ref, gz_ref, hz_ref, gy_ref, hy_ref, sum_ref,
):
    for y in range(8):
        turned_ref[y] = density_ref[y].T.astype(bf16)
    slots = slots_ref[...]
    points = iota((GRID, LIVE), 0).astype(f32)
    x_offset = points - slots[0:1]
    y_offset = (where_ref[0] * 8 + iota((8, LIVE), 0)).astype(f32) - slots[1:2]
    z_offset = points - slots[2:3]
    gx_values = gauss_values(x_offset)
    gy_values = gauss_values(y_offset)
    gz_values = gauss_values(z_offset)
    for k in range(4):
        slope = 2.0 * EXPONENTS[k]
        x_ref[k, 0] = gx_values[k].astype(bf16)
        x_ref[k, 1] = (slope * x_offset * gx_values[k]).astype(bf16)
        gy_ref[k] = gy_values[k]
        hy_ref[k] = slope * y_offset * gy_values[k]
        scale = KERNEL_WEIGHTS[k] * slots[3:4]
        gz_ref[k] = gz_values[k] * scale
        hz_ref[k] = slope * z_offset * gz_values[k] * scale

    @pl.loop(0, LIVE // 128)
    def _(chunk):
        lanes = pl.ds(pl.multiple_of(chunk * 128, 128), 128)
        force_x = jnp.zeros((1, 128), f32)
        force_y = jnp.zeros((1, 128), f32)
        force_z = jnp.zeros((1, 128), f32)
        for k in range(4):
            both = jnp.concatenate([x_ref[k, 0, :, lanes], x_ref[k, 1, :, lanes]], axis=1)
            value_y = gy_ref[k, :, lanes]
            slope_y = hy_ref[k, :, lanes]
            with_x = jnp.zeros((GRID, 128), f32)
            with_y = jnp.zeros((GRID, 128), f32)
            with_z = jnp.zeros((GRID, 128), f32)
            for y in range(8):
                part = dot_nn(turned_ref[y], both)
                with_x = with_x + part[:, 128:] * value_y[y : y + 1]
                with_y = with_y + part[:, :128] * slope_y[y : y + 1]
                with_z = with_z + part[:, :128] * value_y[y : y + 1]
            value_z = gz_ref[k, :, lanes]
            force_x = force_x + jnp.sum(with_x * value_z, axis=0, keepdims=True)
            force_y = force_y + jnp.sum(with_y * value_z, axis=0, keepdims=True)
            force_z = force_z + jnp.sum(with_z * hz_ref[k, :, lanes], axis=0, keepdims=True)
        sum_ref[0:1, lanes] = force_x
        sum_ref[1:2, lanes] = force_y
        sum_ref[2:3, lanes] = force_z

    forces = sum_ref[0:3, :] * -FORCE_UNIT
    high, low = halves(forces)
    stacked = jnp.concatenate([high, low, jnp.zeros((2, LIVE), f32)], axis=0)
    live = slot_place(blocks_ref[...])
    owner, chosen = slot_masks(live)
    spread = jnp.where(iota((8, 128), 1) // CAP == iota((8, 128), 0), 1.0, 0.0).astype(bf16)
    per_slot = lax.dot_general(
        stacked.astype(bf16), spread, (((0,), (0,)), ((), ())), preferred_element_type=f32
    )
    per_slot = jnp.where(chosen, per_slot, 0.0).astype(bf16)
    counts, starts = place_by_row(live)
    place = iota((OWNERS, 128), 1).astype(f32)
    total = jnp.zeros((OWNERS, 128), f32)
    for t in range(LIVE // 128):
        here = place + (128.0 * t)
        held = jnp.where((here >= starts) & (here < starts + counts), 1.0, 0.0).astype(bf16)
        total = total + dot_nn(held, per_slot[t * 128 : (t + 1) * 128])
    out_ref[...] = total


def wave_tables(where_ref):
    q_wave = iota((GRID, GRID), 0).astype(f32) * WAVE_STEP
    l_wave = iota((GRID, GRID), 1).astype(f32) * WAVE_STEP
    return q_wave * q_wave + l_wave * l_wave


def kinetic_of(where_ref, plane_waves, a):
    a_wave = (where_ref[0] * 8 + a).astype(f32) * WAVE_STEP
    return 0.5 * (a_wave * a_wave + plane_waves)


def image_kernel(
    where_ref, got_ref, coeffs_ref, table_ref, force_ref, energy_ref,
    image_ref, out_ref, wide_ref,
):
    table = table_ref[...]
    wide_ref[...] = got_ref[...].astype(f32).reshape(GRID, 8, GRID)
    plane_waves = wave_tables(where_ref)
    overlap = jnp.zeros((1, GRID), f32)
    norm = jnp.zeros((1, GRID), f32)
    for a in range(8):
        along_y = lax.dot_general(
            table, wide_ref[:, a, :].astype(bf16), (((0,), (0,)), ((), ())),
            preferred_element_type=f32,
        ).astype(bf16)
        coeff = coeffs_ref[a].astype(f32)
        image = kinetic_of(where_ref, plane_waves, a) * coeff + dot_nn(along_y, table)
        image_ref[a] = image
        overlap = overlap + jnp.sum(coeff * image, axis=0, keepdims=True)
        norm = norm + jnp.sum(coeff * coeff, axis=0, keepdims=True)
    overlap = jnp.sum(overlap, axis=1, keepdims=True)
    norm = jnp.sum(norm, axis=1, keepdims=True)
    mean = overlap / jnp.maximum(norm, 1e-30)
    spread = jnp.zeros((1, GRID), f32)
    for a in range(8):
        residual = image_ref[a] - mean * coeffs_ref[a].astype(f32)
        spread = spread + jnp.sum(residual * residual, axis=0, keepdims=True)
    spread = jnp.sum(spread, axis=1, keepdims=True)
    lane = iota((1, GRID), 1)
    row = jnp.where(lane == SCALAR_LANE + 1, overlap, energy_ref[...])
    row = jnp.where(lane == SCALAR_LANE + 2, spread, row)
    out_ref[...] = force_ref[...] + row


def final_kernel(
    where_ref, near_ref, count_ref, got_ref, image_ref, coeffs_ref,
    waves_ref, force_ref, energy_ref, ratio_ref, totals_ref,
):
    got = got_ref[...]
    by_band = jnp.sum(got.reshape(SHARES, BANDS, 128), axis=0)
    column = lambda i: slice(SCALAR_LANE + i, SCALAR_LANE + i + 1)
    norms = by_band[:, column(0)]
    energies = by_band[:, column(1)] / norms
    band = iota((BANDS, 1), 0)
    own = band == where_ref[1]
    energy = jnp.sum(jnp.where(own, energies, 0.0), axis=0, keepdims=True)
    norm = jnp.sum(jnp.where(own, norms, 0.0), axis=0, keepdims=True)
    part_norm = got[:, column(0)]
    part_energy = got[:, column(1)] / jnp.maximum(part_norm, 1e-30)
    shift = part_energy - energy
    spread = got[:, column(2)] + part_norm * shift * shift
    own_rows = iota((OWNERS, 1), 0) % BANDS == where_ref[1]
    squares = jnp.sum(jnp.where(own_rows, spread, 0.0), axis=0, keepdims=True)
    energy_ref[...] = energy
    ratio_ref[...] = squares / norm
    everything = jnp.sum(by_band, axis=0, keepdims=True)
    band_energy = jnp.sum(occupancy(band) * energies, axis=0, keepdims=True) / BANDS
    totals_ref[...] = jnp.concatenate(
        [everything[:, SCALAR_LANE + 3 : SCALAR_LANE + 10], band_energy], axis=1
    )
    plane_waves = wave_tables(where_ref)
    for a in range(8):
        coeff = coeffs_ref[a].astype(f32)
        residual = image_ref[a] - energy * coeff
        kinetic = kinetic_of(where_ref, plane_waves, a)
        waves_ref[a] = (coeff - STEP_SIZE * residual / (1.0 + kinetic)).astype(bf16)
    lane = iota((8, 128), 1)
    wanted = (lane // CAP) % 3 == iota((8, 128), 0)
    wanted = wanted & (lane < SCALAR_LANE) & (lane % CAP < count_ref[0])
    split = jnp.where(wanted, everything, 0.0)
    high, rest = halves(split)
    middle, low = halves(rest)
    pieces = jnp.concatenate([high, middle, low, jnp.zeros_like(low)], axis=0).astype(bf16)
    placed = dot_nn(pieces, near_one_hot(near_ref))
    forces = placed[0:8] + placed[8:16] + placed[16:24]
    force_ref[...] = forces[:3]


VMEM = pl.BlockSpec(memory_space=pltpu.VMEM)
SMEM = pl.BlockSpec(memory_space=pltpu.SMEM)


def call(kernel, inputs, outputs, scratch=(), cost=2000000000, specs=None):
    if specs is None:
        specs = [SMEM if x.dtype == jnp.int32 else VMEM for x in inputs]
    shapes = [jax.ShapeDtypeStruct(*out) for out in outputs]
    return pl.pallas_call(
        kernel,
        out_shape=shapes,
        in_specs=specs,
        out_specs=[VMEM] * len(shapes),
        scratch_shapes=[pltpu.VMEM(*one) if isinstance(one, tuple) else one for one in scratch],
        compiler_params=pltpu.CompilerParams(vmem_limit_bytes=40 * 1024 * 1024),
        cost_estimate=pl.CostEstimate(flops=cost, bytes_accessed=1000000, transcendentals=0),
    )(*inputs)


def exchange(block, axes):
    return lax.all_to_all(block, axes, split_axis=0, concat_axis=0, tiled=True)


def per_device(coeffs, v_local, atom_pos, atom_charge, near_list, live_count):
    table = cosine_table()
    coeffs = coeffs[0]
    where = jnp.stack([lax.axis_index("gvec"), lax.axis_index(GROUP)]).astype(jnp.int32)
    (own,) = call(
        pick_kernel,
        [near_list, live_count, atom_pos, atom_charge.reshape(1, ATOMS)],
        [((OWNERS, 128), f32)],
        [
            pltpu.SMEM((CAP,), jnp.int32),
            pltpu.SMEM((1,), jnp.int32),
            ((3, ATOMS), f32),
            ((1, ATOMS), f32),
            pltpu.SemaphoreType.DMA((4,)),
        ],
        specs=[pl.BlockSpec(memory_space=pltpu.HBM)] * 4,
    )
    blocks = exchange(own.reshape(OWNERS, 1, 128), EVERY).reshape(OWNERS, 128)
    (sections,) = call(
        section_kernel,
        [coeffs, table],
        [((SHARES, 64, GRID), bf16)],
        [((GRID, 8, GRID), f32)],
    )
    got = exchange(sections, "gvec")
    (stats,) = call(stats_kernel, [where, coeffs], [((1, 128), f32)])
    potential, slots = call(
        potential_kernel,
        [where, blocks],
        [((8, GRID, GRID), f32), ((8, LIVE), f32)],
        [((4, GRID, LIVE), bf16), ((4, GRID, LIVE), f32)],
    )
    back, density, energy = call(
        field_kernel,
        [where, got, v_local, table, potential, stats],
        [
            ((SHARES, 64, GRID), bf16),
            ((8, GRID, GRID), f32),
            ((1, 128), f32),
        ],
        [((GRID, 8, GRID), f32), ((SHARES, 64, GRID), f32)],
    )
    returned = exchange(back, "gvec")
    (forces,) = call(
        force_kernel,
        [where, blocks, density, slots],
        [((OWNERS, 128), f32)],
        [
            ((8, GRID, GRID), bf16),
            ((4, 2, GRID, LIVE), bf16),
            ((4, GRID, LIVE), f32),
            ((4, GRID, LIVE), f32),
            ((4, 8, LIVE), f32),
            ((4, 8, LIVE), f32),
            ((8, LIVE), f32),
        ],
    )
    image, message = call(
        image_kernel,
        [where, returned, coeffs, table, forces, energy],
        [((8, GRID, GRID), f32), ((OWNERS, 128), f32)],
        [((GRID, 8, GRID), f32)],
    )
    arrived = exchange(message.reshape(OWNERS, 1, 128), EVERY).reshape(OWNERS, 128)
    waves, atom_force, energies, ratio, totals = call(
        final_kernel,
        [where, near_list, live_count, arrived, image, coeffs],
        [
            ((8, GRID, GRID), bf16),
            ((3, ATOMS), f32),
            ((1, 1), f32),
            ((1, 1), f32),
            ((1, 8), f32),
        ],
    )
    return (waves[None], energies.reshape(1), ratio.reshape(1), atom_force, totals.reshape(8))


def solution(mesh):
    return jax.shard_map(
        per_device,
        mesh=mesh,
        in_specs=(
            P(("band", "dom"), "gvec", None, None),
            P(None, "gvec", None),
            P(None, ("band", "gvec", "dom")),
            P(("band", "gvec", "dom")),
            P(("band", "gvec", "dom")),
            P(("band", "gvec", "dom")),
        ),
        out_specs=(
            P(("band", "dom"), "gvec", None, None),
            P(("band", "dom")),
            P(("band", "dom")),
            P(None, ("band", "gvec", "dom")),
            P(),
        ),
        check_vma=False,
    )
```

```python
import jax
import jax.numpy as jnp
import numpy as np
from jax import lax
from jax.experimental import pallas as pl
from jax.experimental.pallas import tpu as pltpu
from jax.sharding import PartitionSpec as P

GRID = 128
CAP = 16
BANDS = 16
SHARES = 16
OWNERS = 256
LIVE = 1024
ATOMS = 1024
SIGMA_FRACTIONS = (1.0 / 32.0, 1.0 / 16.0, 1.0 / 8.0, 1.0 / 4.0)
KERNEL_WEIGHTS = (1.0, 0.5, 0.25, 0.125)
EXPONENTS = tuple(0.5 / (GRID * fraction) ** 2 for fraction in SIGMA_FRACTIONS)
FORCE_UNIT = 1.0 / 4096.0
STEP_SIZE = 0.5
WAVE_STEP = float(np.pi / GRID)
CELLS = float(GRID**3)
DEAD_MARK = 4096.0
SCALAR_LANE = 96
f32 = jnp.float32
bf16 = jnp.bfloat16
EVERY = ("gvec", "band", "dom")
GROUP = ("band", "dom")


def cosine_table():
    points = np.arange(GRID).astype(np.float32)
    angles = np.float32(np.pi) * (points[:, None] + np.float32(0.5)) * points[None, :]
    angles = (angles / np.float32(GRID)).astype(np.float32)
    scales = np.where(
        points == 0, np.sqrt(np.float32(1.0 / GRID)), np.sqrt(np.float32(2.0 / GRID))
    ).astype(np.float32)
    return jnp.asarray(np.cos(angles).astype(np.float32) * scales[None, :], bf16)


def dot_nn(a, b):
    return lax.dot_general(a, b, (((1,), (0,)), ((), ())), preferred_element_type=f32)


def dot_nt(a, b):
    return lax.dot_general(a, b, (((1,), (1,)), ((), ())), preferred_element_type=f32)


def iota(shape, dim):
    return lax.broadcasted_iota(jnp.int32, shape, dim)


def occupancy(band):
    return 2.0 / (1.0 + jnp.exp((band.astype(f32) - 0.5 * BANDS) / (0.125 * BANDS)))


def near_one_hot(near_ref):
    slot = iota((128, 128), 0) % CAP
    wanted = jnp.zeros((128, 128), jnp.int32)
    for s in range(CAP):
        wanted = jnp.where(slot == s, near_ref[s], wanted)
    lanes = iota((128, 128), 1)
    parts = [
        jnp.where(wanted == lanes + 128 * t, 1.0, 0.0).astype(bf16) for t in range(ATOMS // 128)
    ]
    return jnp.concatenate(parts, axis=1)


def halves(value):
    high = value.astype(bf16).astype(f32)
    return high, value - high


def pick_kernel(
    near_hbm, count_hbm, pos_hbm, charge_hbm, out_ref,
    near_ref, count_ref, pos_ref, charge_ref, sems,
):
    moves = [
        pltpu.make_async_copy(near_hbm, near_ref, sems.at[0]),
        pltpu.make_async_copy(count_hbm, count_ref, sems.at[1]),
        pltpu.make_async_copy(pos_hbm, pos_ref, sems.at[2]),
        pltpu.make_async_copy(charge_hbm, charge_ref, sems.at[3]),
    ]
    for move in moves:
        move.start()
    for move in moves:
        move.wait()
    one_hot = near_one_hot(near_ref)
    wide = jnp.concatenate([pos_ref[...], charge_ref[...]], axis=0)
    high, low = halves(wide)
    both = jnp.concatenate([high, low], axis=0).astype(bf16)
    picked = dot_nt(both, one_hot)
    lane = iota((8, 128), 1)
    row = jnp.sum(jnp.where(lane // CAP == iota((8, 128), 0), picked, 0.0), axis=0, keepdims=True)
    lane_row = iota((1, 128), 1)
    dead = (lane_row < CAP) & (lane_row >= count_ref[0])
    row = jnp.where(dead, DEAD_MARK, row)
    out_ref[...] = jnp.broadcast_to(row.astype(bf16)[None], out_ref.shape)


def section_kernel(coeffs_ref, table_ref, out_ref, wide_ref):
    table = table_ref[...]
    along_z = dot_nt(coeffs_ref[...].reshape(1024, GRID), table).astype(bf16)
    for a in range(8):
        wide_ref[:, a, :] = dot_nn(table, along_z[a * GRID : (a + 1) * GRID])
    out_ref[:, :64, :] = wide_ref[...].reshape(SHARES, 64, GRID).astype(bf16)
    out_ref[:, 64:, :] = jnp.zeros((SHARES, 16, GRID), bf16)


def stats_kernel(where_ref, coeffs_ref, out_ref):
    first = where_ref[0] * 8
    q_wave = iota((GRID, GRID), 0).astype(f32) * WAVE_STEP
    l_wave = iota((1, GRID), 1).astype(f32) * WAVE_STEP
    sums = [jnp.zeros((1, GRID), f32) for _ in range(7)]
    for a in range(8):
        a_wave = (first + a).astype(f32) * WAVE_STEP
        value = coeffs_ref[a].astype(f32)
        square = value * value
        scaled = square * q_wave
        flat = jnp.sum(square, axis=0, keepdims=True)
        once = jnp.sum(scaled, axis=0, keepdims=True)
        twice = jnp.sum(scaled * q_wave, axis=0, keepdims=True)
        terms = (
            flat,
            a_wave * a_wave * flat,
            twice,
            l_wave * l_wave * flat,
            a_wave * once,
            a_wave * l_wave * flat,
            l_wave * once,
        )
        sums = [total + term for total, term in zip(sums, terms)]
    lane = iota((1, GRID), 1)
    weight = occupancy(jnp.full((1, 1), where_ref[1], jnp.int32)) / CELLS
    row = jnp.where(lane == SCALAR_LANE, jnp.sum(sums[0]), 0.0)
    for i in range(1, 7):
        value = jnp.sum(sums[i], axis=1, keepdims=True) * weight
        row = jnp.where(lane == SCALAR_LANE + 2 + i, value, row)
    out_ref[...] = row


def gauss_values(offset):
    wide = jnp.exp(-EXPONENTS[3] * offset * offset)
    values = [wide]
    for _ in range(3):
        square = values[0] * values[0]
        values.insert(0, square * square)
    return values


def slot_place(blocks):
    lane = iota((OWNERS, 128), 1)
    live = jnp.where((blocks < 1000.0) & (lane < CAP), 1.0, 0.0).astype(bf16)
    return live


def place_by_row(live):
    ones = jnp.ones((128, 128), bf16)
    counts = dot_nn(live, ones)
    before = jnp.where(iota((OWNERS, OWNERS), 1) < iota((OWNERS, OWNERS), 0), 1.0, 0.0).astype(bf16)
    starts = dot_nn(before, counts.astype(bf16))
    return counts, starts


def place_by_lane(live):
    ones = jnp.ones((128, 128), bf16)
    counts = dot_nt(ones, live)
    before = jnp.where(iota((OWNERS, OWNERS), 0) < iota((OWNERS, OWNERS), 1), 1.0, 0.0).astype(bf16)
    starts = dot_nn(counts.astype(bf16), before)
    return counts, starts


def slot_masks(live):
    counts, starts = place_by_lane(live)
    place = iota((LIVE, OWNERS), 0).astype(f32)
    start_row = starts[:1]
    owner = (place >= start_row) & (place < start_row + counts[:1])
    owner = jnp.where(owner, 1.0, 0.0).astype(bf16)
    coarse = jnp.floor(starts * 0.125)
    fine = starts - 8.0 * coarse
    own_start = 8.0 * dot_nt(owner, coarse.astype(bf16)) + dot_nt(owner, fine.astype(bf16))
    slot = iota((LIVE, 128), 0).astype(f32) - own_start
    chosen = slot == (iota((LIVE, 128), 1) % CAP).astype(f32)
    return owner, chosen


def potential_kernel(
    where_ref, got_ref, potential_ref, slots_ref, blocks_ref, gx_ref, depth_ref
):
    blocks = got_ref[:, 64:, :].astype(f32).reshape(OWNERS, 128)
    blocks_ref[...] = blocks
    owner, chosen = slot_masks(slot_place(blocks))
    rows = jnp.where(chosen, dot_nn(owner, blocks.astype(bf16)), 0.0).astype(bf16)
    pick = jnp.where(iota((8, 128), 1) // CAP == iota((8, 128), 0), 1.0, 0.0).astype(bf16)
    slots = dot_nt(pick, rows)
    slots = slots[:4] + slots[4:]
    slots_ref[...] = jnp.concatenate([slots, slots], axis=0)
    points = iota((GRID, LIVE), 0).astype(f32)
    y_points = (where_ref[0] * 8 + iota((8, LIVE), 0)).astype(f32)
    gx_values = gauss_values(points - slots[0:1])
    gy_values = gauss_values(y_points - slots[1:2])
    gz_values = gauss_values(points - slots[2:3])
    for k in range(4):
        gx_ref[k] = gx_values[k].astype(bf16)
        depth_ref[k] = gz_values[k] * (slots[3:4] * KERNEL_WEIGHTS[k])
    for y in range(8):
        potential = jnp.zeros((GRID, GRID), f32)
        for k in range(4):
            plane = (depth_ref[k] * gy_values[k][y : y + 1]).astype(bf16)
            potential = potential + dot_nt(gx_ref[k], plane)
        potential_ref[y] = potential


def field_kernel(
    where_ref, got_ref, local_ref, table_ref, potential_ref, stats_ref,
    back_ref, density_ref, energy_ref, local_wide, back_wide,
):
    table = table_ref[...]
    got = got_ref[:, :64, :].astype(f32)
    local_wide[...] = local_ref[...].astype(f32)
    weight = occupancy(jnp.full((1, 1), where_ref[1], jnp.int32))
    energy = jnp.zeros((1, GRID), f32)
    for y in range(8):
        potential = potential_ref[y]
        mine = got[:, y * 8 : (y + 1) * 8, :].reshape(GRID, GRID).astype(bf16)
        real = dot_nn(table, mine).astype(bf16).astype(f32)
        density = weight * real * real
        density_ref[y] = density
        energy = energy + jnp.sum(density * potential, axis=0, keepdims=True)
        field = local_wide[:, y, :] + potential.astype(bf16).astype(f32)
        applied = (field * real).astype(bf16)
        back = lax.dot_general(
            table, applied, (((0,), (0,)), ((), ())), preferred_element_type=f32
        )
        back_wide[:, y * 8 : (y + 1) * 8, :] = back.reshape(SHARES, 8, GRID)
    back_ref[...] = back_wide[...].astype(bf16)
    total = jnp.sum(energy, axis=1, keepdims=True) / CELLS
    lane = iota((1, GRID), 1)
    energy_ref[...] = stats_ref[...] + jnp.where(lane == SCALAR_LANE + 9, total, 0.0)


def force_kernel(
    where_ref, blocks_ref, density_ref, slots_ref, out_ref,
    turned_ref, x_ref, gz_ref, hz_ref, gy_ref, hy_ref, sum_ref,
):
    for y in range(8):
        turned_ref[y] = density_ref[y].T.astype(bf16)
    slots = slots_ref[...]
    points = iota((GRID, LIVE), 0).astype(f32)
    x_offset = points - slots[0:1]
    y_offset = (where_ref[0] * 8 + iota((8, LIVE), 0)).astype(f32) - slots[1:2]
    z_offset = points - slots[2:3]
    gx_values = gauss_values(x_offset)
    gy_values = gauss_values(y_offset)
    gz_values = gauss_values(z_offset)
    for k in range(4):
        slope = 2.0 * EXPONENTS[k]
        x_ref[k, 0] = gx_values[k].astype(bf16)
        x_ref[k, 1] = (slope * x_offset * gx_values[k]).astype(bf16)
        gy_ref[k] = gy_values[k]
        hy_ref[k] = slope * y_offset * gy_values[k]
        scale = KERNEL_WEIGHTS[k] * slots[3:4]
        gz_ref[k] = gz_values[k] * scale
        hz_ref[k] = slope * z_offset * gz_values[k] * scale

    for chunk in range(LIVE // 128):
        lanes = pl.ds(chunk * 128, 128)
        force_x = jnp.zeros((1, 128), f32)
        force_y = jnp.zeros((1, 128), f32)
        force_z = jnp.zeros((1, 128), f32)
        for k in range(4):
            both = jnp.concatenate([x_ref[k, 0, :, lanes], x_ref[k, 1, :, lanes]], axis=1)
            value_y = gy_ref[k, :, lanes]
            slope_y = hy_ref[k, :, lanes]
            with_x = jnp.zeros((GRID, 128), f32)
            with_y = jnp.zeros((GRID, 128), f32)
            with_z = jnp.zeros((GRID, 128), f32)
            for y in range(8):
                part = dot_nn(turned_ref[y], both)
                with_x = with_x + part[:, 128:] * value_y[y : y + 1]
                with_y = with_y + part[:, :128] * slope_y[y : y + 1]
                with_z = with_z + part[:, :128] * value_y[y : y + 1]
            value_z = gz_ref[k, :, lanes]
            force_x = force_x + jnp.sum(with_x * value_z, axis=0, keepdims=True)
            force_y = force_y + jnp.sum(with_y * value_z, axis=0, keepdims=True)
            force_z = force_z + jnp.sum(with_z * hz_ref[k, :, lanes], axis=0, keepdims=True)
        sum_ref[0:1, lanes] = force_x
        sum_ref[1:2, lanes] = force_y
        sum_ref[2:3, lanes] = force_z

    forces = sum_ref[0:3, :] * -FORCE_UNIT
    high, low = halves(forces)
    stacked = jnp.concatenate([high, low, jnp.zeros((2, LIVE), f32)], axis=0)
    live = slot_place(blocks_ref[...])
    owner, chosen = slot_masks(live)
    spread = jnp.where(iota((8, 128), 1) // CAP == iota((8, 128), 0), 1.0, 0.0).astype(bf16)
    per_slot = lax.dot_general(
        stacked.astype(bf16), spread, (((0,), (0,)), ((), ())), preferred_element_type=f32
    )
    per_slot = jnp.where(chosen, per_slot, 0.0).astype(bf16)
    counts, starts = place_by_row(live)
    place = iota((OWNERS, 128), 1).astype(f32)
    total = jnp.zeros((OWNERS, 128), f32)
    for t in range(LIVE // 128):
        here = place + (128.0 * t)
        held = jnp.where((here >= starts) & (here < starts + counts), 1.0, 0.0).astype(bf16)
        total = total + dot_nn(held, per_slot[t * 128 : (t + 1) * 128])
    out_ref[...] = total


def wave_tables(where_ref):
    q_wave = iota((GRID, GRID), 0).astype(f32) * WAVE_STEP
    l_wave = iota((GRID, GRID), 1).astype(f32) * WAVE_STEP
    return q_wave * q_wave + l_wave * l_wave


def kinetic_of(where_ref, plane_waves, a):
    a_wave = (where_ref[0] * 8 + a).astype(f32) * WAVE_STEP
    return 0.5 * (a_wave * a_wave + plane_waves)


def image_kernel(
    where_ref, got_ref, coeffs_ref, table_ref, force_ref, energy_ref,
    image_ref, out_ref, wide_ref,
):
    table = table_ref[...]
    wide_ref[...] = got_ref[...].astype(f32).reshape(GRID, 8, GRID)
    plane_waves = wave_tables(where_ref)
    overlap = jnp.zeros((1, GRID), f32)
    norm = jnp.zeros((1, GRID), f32)
    for a in range(8):
        along_y = lax.dot_general(
            table, wide_ref[:, a, :].astype(bf16), (((0,), (0,)), ((), ())),
            preferred_element_type=f32,
        ).astype(bf16)
        coeff = coeffs_ref[a].astype(f32)
        image = kinetic_of(where_ref, plane_waves, a) * coeff + dot_nn(along_y, table)
        image_ref[a] = image
        overlap = overlap + jnp.sum(coeff * image, axis=0, keepdims=True)
        norm = norm + jnp.sum(coeff * coeff, axis=0, keepdims=True)
    overlap = jnp.sum(overlap, axis=1, keepdims=True)
    norm = jnp.sum(norm, axis=1, keepdims=True)
    mean = overlap / jnp.maximum(norm, 1e-30)
    spread = jnp.zeros((1, GRID), f32)
    for a in range(8):
        residual = image_ref[a] - mean * coeffs_ref[a].astype(f32)
        spread = spread + jnp.sum(residual * residual, axis=0, keepdims=True)
    spread = jnp.sum(spread, axis=1, keepdims=True)
    lane = iota((1, GRID), 1)
    row = jnp.where(lane == SCALAR_LANE + 1, overlap, energy_ref[...])
    row = jnp.where(lane == SCALAR_LANE + 2, spread, row)
    out_ref[...] = force_ref[...] + row


def final_kernel(
    where_ref, near_ref, count_ref, got_ref, image_ref, coeffs_ref,
    waves_ref, force_ref, energy_ref, ratio_ref, totals_ref,
):
    got = got_ref[...]
    by_band = jnp.sum(got.reshape(SHARES, BANDS, 128), axis=0)
    column = lambda i: slice(SCALAR_LANE + i, SCALAR_LANE + i + 1)
    norms = by_band[:, column(0)]
    energies = by_band[:, column(1)] / norms
    band = iota((BANDS, 1), 0)
    own = band == where_ref[1]
    energy = jnp.sum(jnp.where(own, energies, 0.0), axis=0, keepdims=True)
    norm = jnp.sum(jnp.where(own, norms, 0.0), axis=0, keepdims=True)
    part_norm = got[:, column(0)]
    part_energy = got[:, column(1)] / jnp.maximum(part_norm, 1e-30)
    shift = part_energy - energy
    spread = got[:, column(2)] + part_norm * shift * shift
    own_rows = iota((OWNERS, 1), 0) % BANDS == where_ref[1]
    squares = jnp.sum(jnp.where(own_rows, spread, 0.0), axis=0, keepdims=True)
    energy_ref[...] = energy
    ratio_ref[...] = squares / norm
    everything = jnp.sum(by_band, axis=0, keepdims=True)
    band_energy = jnp.sum(occupancy(band) * energies, axis=0, keepdims=True) / BANDS
    totals_ref[...] = jnp.concatenate(
        [everything[:, SCALAR_LANE + 3 : SCALAR_LANE + 10], band_energy], axis=1
    )
    plane_waves = wave_tables(where_ref)
    for a in range(8):
        coeff = coeffs_ref[a].astype(f32)
        residual = image_ref[a] - energy * coeff
        kinetic = kinetic_of(where_ref, plane_waves, a)
        waves_ref[a] = (coeff - STEP_SIZE * residual / (1.0 + kinetic)).astype(bf16)
    lane = iota((8, 128), 1)
    wanted = (lane // CAP) % 3 == iota((8, 128), 0)
    wanted = wanted & (lane < SCALAR_LANE) & (lane % CAP < count_ref[0])
    split = jnp.where(wanted, everything, 0.0)
    high, rest = halves(split)
    middle, low = halves(rest)
    pieces = jnp.concatenate([high, middle, low, jnp.zeros_like(low)], axis=0).astype(bf16)
    placed = dot_nn(pieces, near_one_hot(near_ref))
    forces = placed[0:8] + placed[8:16] + placed[16:24]
    force_ref[...] = forces[:3]


VMEM = pl.BlockSpec(memory_space=pltpu.VMEM)
SMEM = pl.BlockSpec(memory_space=pltpu.SMEM)


def call(kernel, inputs, outputs, scratch=(), cost=2000000000, specs=None, room=40):
    if specs is None:
        specs = [SMEM if x.dtype == jnp.int32 else VMEM for x in inputs]
    shapes = [jax.ShapeDtypeStruct(*out) for out in outputs]
    return pl.pallas_call(
        kernel,
        out_shape=shapes,
        in_specs=specs,
        out_specs=[VMEM] * len(shapes),
        scratch_shapes=[pltpu.VMEM(*one) if isinstance(one, tuple) else one for one in scratch],
        compiler_params=pltpu.CompilerParams(vmem_limit_bytes=room * 1024 * 1024),
        cost_estimate=pl.CostEstimate(flops=cost, bytes_accessed=1000000, transcendentals=0),
    )(*inputs)


def exchange(block, axes):
    return lax.all_to_all(block, axes, split_axis=0, concat_axis=0, tiled=True)


def per_device(coeffs, v_local, atom_pos, atom_charge, near_list, live_count):
    table = cosine_table()
    coeffs = coeffs[0]
    where = jnp.stack([lax.axis_index("gvec"), lax.axis_index(GROUP)]).astype(jnp.int32)
    (own,) = call(
        pick_kernel,
        [near_list, live_count, atom_pos, atom_charge.reshape(1, ATOMS)],
        [((SHARES, 1, 128), bf16)],
        [
            pltpu.SMEM((CAP,), jnp.int32),
            pltpu.SMEM((1,), jnp.int32),
            ((3, ATOMS), f32),
            ((1, ATOMS), f32),
            pltpu.SemaphoreType.DMA((4,)),
        ],
        specs=[pl.BlockSpec(memory_space=pl.ANY)] * 4,
        room=60,
    )
    group = exchange(own, GROUP)
    (sections,) = call(
        section_kernel,
        [coeffs, table],
        [((SHARES, 80, GRID), bf16)],
        [((GRID, 8, GRID), f32)],
    )
    rows = jnp.broadcast_to(group.reshape(1, SHARES, 128), (SHARES, SHARES, 128))
    got = exchange(lax.dynamic_update_slice(sections, rows, (0, 64, 0)), "gvec")
    (stats,) = call(stats_kernel, [where, coeffs], [((1, 128), f32)])
    potential, slots, blocks = call(
        potential_kernel,
        [where, got],
        [((8, GRID, GRID), f32), ((8, LIVE), f32), ((OWNERS, 128), f32)],
        [((4, GRID, LIVE), bf16), ((4, GRID, LIVE), f32)],
    )
    back, density, energy = call(
        field_kernel,
        [where, got, v_local, table, potential, stats],
        [
            ((SHARES, 64, GRID), bf16),
            ((8, GRID, GRID), f32),
            ((1, 128), f32),
        ],
        [((GRID, 8, GRID), f32), ((SHARES, 64, GRID), f32)],
    )
    returned = exchange(back, "gvec")
    (forces,) = call(
        force_kernel,
        [where, blocks, density, slots],
        [((OWNERS, 128), f32)],
        [
            ((8, GRID, GRID), bf16),
            ((4, 2, GRID, LIVE), bf16),
            ((4, GRID, LIVE), f32),
            ((4, GRID, LIVE), f32),
            ((4, 8, LIVE), f32),
            ((4, 8, LIVE), f32),
            ((8, LIVE), f32),
        ],
    )
    image, message = call(
        image_kernel,
        [where, returned, coeffs, table, forces, energy],
        [((8, GRID, GRID), f32), ((OWNERS, 128), f32)],
        [((GRID, 8, GRID), f32)],
    )
    arrived = exchange(message.reshape(OWNERS, 1, 128), EVERY).reshape(OWNERS, 128)
    waves, atom_force, energies, ratio, totals = call(
        final_kernel,
        [where, near_list, live_count, arrived, image, coeffs],
        [
            ((8, GRID, GRID), bf16),
            ((3, ATOMS), f32),
            ((1, 1), f32),
            ((1, 1), f32),
            ((1, 8), f32),
        ],
    )
    return (waves[None], energies.reshape(1), ratio.reshape(1), atom_force, totals.reshape(8))


def solution(mesh):
    return jax.shard_map(
        per_device,
        mesh=mesh,
        in_specs=(
            P(("band", "dom"), "gvec", None, None),
            P(None, "gvec", None),
            P(None, ("band", "gvec", "dom")),
            P(("band", "gvec", "dom")),
            P(("band", "gvec", "dom")),
            P(("band", "gvec", "dom")),
        ),
        out_specs=(
            P(("band", "dom"), "gvec", None, None),
            P(("band", "dom")),
            P(("band", "dom")),
            P(None, ("band", "gvec", "dom")),
            P(),
        ),
        check_vma=False,
    )
```

```python
import jax
import jax.numpy as jnp
import numpy as np
from jax import lax
from jax.experimental import pallas as pl
from jax.experimental.pallas import tpu as pltpu
from jax.sharding import PartitionSpec as P

GRID = 128
CAP = 16
BANDS = 16
SHARES = 16
OWNERS = 256
LIVE = 1024
ATOMS = 1024
SIGMA_FRACTIONS = (1.0 / 32.0, 1.0 / 16.0, 1.0 / 8.0, 1.0 / 4.0)
KERNEL_WEIGHTS = (1.0, 0.5, 0.25, 0.125)
EXPONENTS = tuple(0.5 / (GRID * fraction) ** 2 for fraction in SIGMA_FRACTIONS)
FORCE_UNIT = 1.0 / 4096.0
STEP_SIZE = 0.5
WAVE_STEP = float(np.pi / GRID)
CELLS = float(GRID**3)
DEAD_MARK = 4096.0
SCALAR_LANE = 96
f32 = jnp.float32
bf16 = jnp.bfloat16
EVERY = ("gvec", "band", "dom")
GROUP = ("band", "dom")


def cosine_table():
    points = np.arange(GRID).astype(np.float32)
    angles = np.float32(np.pi) * (points[:, None] + np.float32(0.5)) * points[None, :]
    angles = (angles / np.float32(GRID)).astype(np.float32)
    scales = np.where(
        points == 0, np.sqrt(np.float32(1.0 / GRID)), np.sqrt(np.float32(2.0 / GRID))
    ).astype(np.float32)
    return jnp.asarray(np.cos(angles).astype(np.float32) * scales[None, :], bf16)


def dot_nn(a, b):
    return lax.dot_general(a, b, (((1,), (0,)), ((), ())), preferred_element_type=f32)


def dot_nt(a, b):
    return lax.dot_general(a, b, (((1,), (1,)), ((), ())), preferred_element_type=f32)


def iota(shape, dim):
    return lax.broadcasted_iota(jnp.int32, shape, dim)


def occupancy(band):
    return 2.0 / (1.0 + jnp.exp((band.astype(f32) - 0.5 * BANDS) / (0.125 * BANDS)))


def near_one_hot(near_ref):
    slot = iota((128, 128), 0) % CAP
    wanted = jnp.zeros((128, 128), jnp.int32)
    for s in range(CAP):
        wanted = jnp.where(slot == s, near_ref[s], wanted)
    lanes = iota((128, 128), 1)
    parts = [
        jnp.where(wanted == lanes + 128 * t, 1.0, 0.0).astype(bf16) for t in range(ATOMS // 128)
    ]
    return jnp.concatenate(parts, axis=1)


def halves(value):
    high = value.astype(bf16).astype(f32)
    return high, value - high


def pick_kernel(
    near_hbm, count_hbm, pos_hbm, charge_hbm, out_ref,
    near_ref, count_ref, pos_ref, charge_ref, sems,
):
    moves = [
        pltpu.make_async_copy(near_hbm, near_ref, sems.at[0]),
        pltpu.make_async_copy(count_hbm, count_ref, sems.at[1]),
        pltpu.make_async_copy(pos_hbm, pos_ref, sems.at[2]),
        pltpu.make_async_copy(charge_hbm, charge_ref, sems.at[3]),
    ]
    for move in moves:
        move.start()
    for move in moves:
        move.wait()
    one_hot = near_one_hot(near_ref)
    wide = jnp.concatenate([pos_ref[...], charge_ref[...]], axis=0)
    high, low = halves(wide)
    both = jnp.concatenate([high, low], axis=0).astype(bf16)
    picked = dot_nt(both, one_hot)
    lane = iota((8, 128), 1)
    row = jnp.sum(jnp.where(lane // CAP == iota((8, 128), 0), picked, 0.0), axis=0, keepdims=True)
    lane_row = iota((1, 128), 1)
    dead = (lane_row < CAP) & (lane_row >= count_ref[0])
    row = jnp.where(dead, DEAD_MARK, row)
    out_ref[...] = jnp.broadcast_to(row.astype(bf16)[None], out_ref.shape)


def section_kernel(coeffs_ref, table_ref, out_ref, wide_ref):
    table = table_ref[...]
    along_z = dot_nt(coeffs_ref[...].reshape(1024, GRID), table).astype(bf16)
    for a in range(8):
        wide_ref[:, a, :] = dot_nn(table, along_z[a * GRID : (a + 1) * GRID])
    out_ref[:, :64, :] = wide_ref[...].reshape(SHARES, 64, GRID).astype(bf16)
    out_ref[:, 64:, :] = jnp.zeros((SHARES, 16, GRID), bf16)


def stats_kernel(
    where_ref, near_ref, count_ref, coeffs_ref, out_ref, hot_ref, halved_ref, drawn_ref
):
    first = where_ref[0] * 8
    q_wave = iota((GRID, GRID), 0).astype(f32) * WAVE_STEP
    l_wave = iota((1, GRID), 1).astype(f32) * WAVE_STEP
    sums = [jnp.zeros((1, GRID), f32) for _ in range(7)]
    for a in range(8):
        a_wave = (first + a).astype(f32) * WAVE_STEP
        value = coeffs_ref[a].astype(f32)
        square = value * value
        scaled = square * q_wave
        flat = jnp.sum(square, axis=0, keepdims=True)
        once = jnp.sum(scaled, axis=0, keepdims=True)
        twice = jnp.sum(scaled * q_wave, axis=0, keepdims=True)
        terms = (
            flat,
            a_wave * a_wave * flat,
            twice,
            l_wave * l_wave * flat,
            a_wave * once,
            a_wave * l_wave * flat,
            l_wave * once,
        )
        sums = [total + term for total, term in zip(sums, terms)]
    lane = iota((1, GRID), 1)
    weight = occupancy(jnp.full((1, 1), where_ref[1], jnp.int32)) / CELLS
    row = jnp.where(lane == SCALAR_LANE, jnp.sum(sums[0]), 0.0)
    for i in range(1, 7):
        value = jnp.sum(sums[i], axis=1, keepdims=True) * weight
        row = jnp.where(lane == SCALAR_LANE + 2 + i, value, row)
    out_ref[...] = row
    plane_waves = wave_tables()
    for a in range(8):
        halved = STEP_SIZE / (1.0 + kinetic_of(where_ref, plane_waves, a))
        halved_ref[a] = halved
        drawn_ref[a] = halved * coeffs_ref[a].astype(f32)
    alive = iota((128, ATOMS), 0) % CAP < count_ref[0]
    hot_ref[...] = jnp.where(alive, near_one_hot(near_ref), jnp.zeros((), bf16))


def gauss_values(offset):
    wide = jnp.exp(-EXPONENTS[3] * offset * offset)
    values = [wide]
    for _ in range(3):
        square = values[0] * values[0]
        values.insert(0, square * square)
    return values


def slot_place(blocks):
    lane = iota((OWNERS, 128), 1)
    live = jnp.where((blocks < 1000.0) & (lane < CAP), 1.0, 0.0).astype(bf16)
    return live


def slot_masks(live):
    counts = dot_nn(live, jnp.ones((128, 128), bf16))
    before = jnp.where(iota((OWNERS, OWNERS), 1) < iota((OWNERS, OWNERS), 0), 1.0, 0.0).astype(bf16)
    starts = dot_nn(before, counts.astype(bf16))
    ends = starts + counts
    lane = iota((OWNERS, 128), 1).astype(f32)
    tiles = []
    for t in range(LIVE // 128):
        here = lane + (128.0 * t)
        tiles.append(jnp.where((here >= starts) & (here < ends), 1.0, 0.0).astype(bf16))
    return jnp.concatenate(tiles, axis=1), starts


def choose(held, starts, rows):
    coarse = jnp.floor(starts * 0.125)
    fine = starts - 8.0 * coarse
    left = jnp.concatenate(rows + [coarse.T[:16], fine.T[:16]], axis=0).astype(bf16)
    moved = dot_nn(left, held)
    size = moved.shape[0] - 32
    own_start = 8.0 * moved[size : size + 1] + moved[size + 16 : size + 17]
    slot = iota((1, LIVE), 1).astype(f32) - own_start
    chosen = (iota((128, LIVE), 0) % CAP).astype(f32) == slot
    return chosen, moved


def potential_kernel(
    where_ref, got_ref, potential_ref, slots_ref, blocks_ref, gx_ref, depth_ref
):
    blocks = got_ref[:, 64:, :].astype(f32).reshape(OWNERS, 128)
    blocks_ref[...] = blocks
    held, starts = slot_masks(slot_place(blocks))
    chosen, moved = choose(held, starts, [blocks.T])
    pick = jnp.where(iota((8, 128), 1) // CAP == iota((8, 128), 0), 1.0, 0.0).astype(bf16)
    slots = dot_nn(pick, jnp.where(chosen, moved[:128], 0.0).astype(bf16))
    slots = slots[:4] + slots[4:]
    slots_ref[...] = jnp.concatenate([slots, slots], axis=0)
    points = iota((GRID, LIVE), 0).astype(f32)
    y_points = (where_ref[0] * 8 + iota((8, LIVE), 0)).astype(f32)
    gx_values = gauss_values(points - slots[0:1])
    gy_values = gauss_values(y_points - slots[1:2])
    gz_values = gauss_values(points - slots[2:3])
    for k in range(4):
        gx_ref[k] = gx_values[k].astype(bf16)
        depth_ref[k] = gz_values[k] * (slots[3:4] * KERNEL_WEIGHTS[k])
    for y in range(8):
        potential = jnp.zeros((GRID, GRID), f32)
        for k in range(4):
            plane = (depth_ref[k] * gy_values[k][y : y + 1]).astype(bf16)
            potential = potential + dot_nt(gx_ref[k], plane)
        potential_ref[y] = potential


def field_kernel(
    where_ref, got_ref, local_ref, table_ref, potential_ref, stats_ref,
    back_ref, density_ref, energy_ref, local_wide, back_wide,
):
    table = table_ref[...]
    got = got_ref[:, :64, :].astype(f32)
    local_wide[...] = local_ref[...].astype(f32)
    weight = occupancy(jnp.full((1, 1), where_ref[1], jnp.int32))
    energy = jnp.zeros((1, GRID), f32)
    for y in range(8):
        potential = potential_ref[y]
        mine = got[:, y * 8 : (y + 1) * 8, :].reshape(GRID, GRID).astype(bf16)
        real = dot_nn(table, mine).astype(bf16).astype(f32)
        density = weight * real * real
        density_ref[y] = density
        energy = energy + jnp.sum(density * potential, axis=0, keepdims=True)
        field = local_wide[:, y, :] + potential.astype(bf16).astype(f32)
        applied = (field * real).astype(bf16)
        back = lax.dot_general(
            table, applied, (((0,), (0,)), ((), ())), preferred_element_type=f32
        )
        back_wide[:, y * 8 : (y + 1) * 8, :] = back.reshape(SHARES, 8, GRID)
    back_ref[...] = back_wide[...].astype(bf16)
    total = jnp.sum(energy, axis=1, keepdims=True) / CELLS
    lane = iota((1, GRID), 1)
    energy_ref[...] = stats_ref[...] + jnp.where(lane == SCALAR_LANE + 9, total, 0.0)


def force_kernel(
    where_ref, blocks_ref, density_ref, slots_ref, out_ref,
    turned_ref, x_ref, gz_ref, hz_ref, gy_ref, hy_ref, sum_ref,
):
    for y in range(8):
        turned_ref[y] = density_ref[y].T.astype(bf16)
    slots = slots_ref[...]
    points = iota((GRID, LIVE), 0).astype(f32)
    x_offset = points - slots[0:1]
    y_offset = (where_ref[0] * 8 + iota((8, LIVE), 0)).astype(f32) - slots[1:2]
    z_offset = points - slots[2:3]
    gx_values = gauss_values(x_offset)
    gy_values = gauss_values(y_offset)
    gz_values = gauss_values(z_offset)
    for k in range(4):
        slope = 2.0 * EXPONENTS[k]
        x_ref[k, 0] = gx_values[k].astype(bf16)
        x_ref[k, 1] = (slope * x_offset * gx_values[k]).astype(bf16)
        gy_ref[k] = gy_values[k]
        hy_ref[k] = slope * y_offset * gy_values[k]
        scale = KERNEL_WEIGHTS[k] * slots[3:4]
        gz_ref[k] = gz_values[k] * scale
        hz_ref[k] = slope * z_offset * gz_values[k] * scale

    for chunk in range(LIVE // 128):
        lanes = pl.ds(chunk * 128, 128)
        force_x = jnp.zeros((1, 128), f32)
        force_y = jnp.zeros((1, 128), f32)
        force_z = jnp.zeros((1, 128), f32)
        for k in range(4):
            both = jnp.concatenate([x_ref[k, 0, :, lanes], x_ref[k, 1, :, lanes]], axis=1)
            value_y = gy_ref[k, :, lanes]
            slope_y = hy_ref[k, :, lanes]
            with_x = jnp.zeros((GRID, 128), f32)
            with_y = jnp.zeros((GRID, 128), f32)
            with_z = jnp.zeros((GRID, 128), f32)
            for y in range(8):
                part = dot_nn(turned_ref[y], both)
                with_x = with_x + part[:, 128:] * value_y[y : y + 1]
                with_y = with_y + part[:, :128] * slope_y[y : y + 1]
                with_z = with_z + part[:, :128] * value_y[y : y + 1]
            value_z = gz_ref[k, :, lanes]
            force_x = force_x + jnp.sum(with_x * value_z, axis=0, keepdims=True)
            force_y = force_y + jnp.sum(with_y * value_z, axis=0, keepdims=True)
            force_z = force_z + jnp.sum(with_z * hz_ref[k, :, lanes], axis=0, keepdims=True)
        sum_ref[0:1, lanes] = force_x
        sum_ref[1:2, lanes] = force_y
        sum_ref[2:3, lanes] = force_z

    forces = sum_ref[0:3, :] * -FORCE_UNIT
    high, low = halves(forces)
    stacked = jnp.concatenate(
        [jnp.broadcast_to(part[c : c + 1], (CAP, LIVE)) for part in (high, low) for c in range(3)]
        + [jnp.zeros((128 - 6 * CAP, LIVE), f32)],
        axis=0,
    )
    held, starts = slot_masks(slot_place(blocks_ref[...]))
    chosen, _ = choose(held, starts, [])
    per_slot = jnp.where(chosen, stacked, 0.0).astype(bf16)
    out_ref[...] = dot_nt(per_slot, held).T


def wave_tables():
    q_wave = iota((GRID, GRID), 0).astype(f32) * WAVE_STEP
    l_wave = iota((GRID, GRID), 1).astype(f32) * WAVE_STEP
    return q_wave * q_wave + l_wave * l_wave


def kinetic_of(where_ref, plane_waves, a):
    a_wave = (where_ref[0] * 8 + a).astype(f32) * WAVE_STEP
    return 0.5 * (a_wave * a_wave + plane_waves)


def image_kernel(
    where_ref, got_ref, coeffs_ref, table_ref, force_ref, energy_ref, halved_ref,
    ahead_ref, out_ref, wide_ref, image_ref,
):
    table = table_ref[...]
    wide_ref[...] = got_ref[...].astype(f32).reshape(GRID, 8, GRID)
    plane_waves = wave_tables()
    overlap = jnp.zeros((1, GRID), f32)
    norm = jnp.zeros((1, GRID), f32)
    for a in range(8):
        along_y = lax.dot_general(
            table, wide_ref[:, a, :].astype(bf16), (((0,), (0,)), ((), ())),
            preferred_element_type=f32,
        ).astype(bf16)
        coeff = coeffs_ref[a].astype(f32)
        image = kinetic_of(where_ref, plane_waves, a) * coeff + dot_nn(along_y, table)
        image_ref[a] = image
        ahead_ref[a] = coeff - halved_ref[a] * image
        overlap = overlap + jnp.sum(coeff * image, axis=0, keepdims=True)
        norm = norm + jnp.sum(coeff * coeff, axis=0, keepdims=True)
    overlap = jnp.sum(overlap, axis=1, keepdims=True)
    norm = jnp.sum(norm, axis=1, keepdims=True)
    mean = overlap / jnp.maximum(norm, 1e-30)
    spread = jnp.zeros((1, GRID), f32)
    for a in range(8):
        residual = image_ref[a] - mean * coeffs_ref[a].astype(f32)
        spread = spread + jnp.sum(residual * residual, axis=0, keepdims=True)
    spread = jnp.sum(spread, axis=1, keepdims=True)
    lane = iota((1, GRID), 1)
    row = jnp.where(lane == SCALAR_LANE + 1, overlap, energy_ref[...])
    row = jnp.where(lane == SCALAR_LANE + 2, spread, row)
    out_ref[...] = force_ref[...] + row


def final_kernel(
    where_ref, got_ref, ahead_ref, drawn_ref, hot_ref,
    waves_ref, force_ref, energy_ref, ratio_ref, totals_ref,
):
    got = got_ref[...]
    by_band = jnp.sum(got.reshape(SHARES, BANDS, 128), axis=0)
    column = lambda i: slice(SCALAR_LANE + i, SCALAR_LANE + i + 1)
    norms = by_band[:, column(0)]
    energies = by_band[:, column(1)] / norms
    band = iota((BANDS, 1), 0)
    own = band == where_ref[1]
    energy = jnp.sum(jnp.where(own, energies, 0.0), axis=0, keepdims=True)
    norm = jnp.sum(jnp.where(own, norms, 0.0), axis=0, keepdims=True)
    part_norm = got[:, column(0)]
    part_energy = got[:, column(1)] / jnp.maximum(part_norm, 1e-30)
    shift = part_energy - energy
    spread = got[:, column(2)] + part_norm * shift * shift
    own_rows = iota((OWNERS, 1), 0) % BANDS == where_ref[1]
    squares = jnp.sum(jnp.where(own_rows, spread, 0.0), axis=0, keepdims=True)
    energy_ref[...] = energy
    ratio_ref[...] = squares / norm
    everything = jnp.sum(by_band, axis=0, keepdims=True)
    band_energy = jnp.sum(occupancy(band) * energies, axis=0, keepdims=True) / BANDS
    totals_ref[...] = jnp.concatenate(
        [everything[:, SCALAR_LANE + 3 : SCALAR_LANE + 10], band_energy], axis=1
    )
    for a in range(8):
        waves_ref[a] = (ahead_ref[a] + energy * drawn_ref[a]).astype(bf16)
    lane = iota((8, 128), 1)
    wanted = ((lane // CAP) % 3 == iota((8, 128), 0)) & (lane < SCALAR_LANE)
    split = jnp.where(wanted, everything, 0.0)
    high, rest = halves(split)
    middle, low = halves(rest)
    pieces = jnp.concatenate([high, middle, low, jnp.zeros_like(low)], axis=0).astype(bf16)
    placed = dot_nn(pieces, hot_ref[...])
    forces = placed[0:8] + placed[8:16] + placed[16:24]
    force_ref[...] = forces[:3]


VMEM = pl.BlockSpec(memory_space=pltpu.VMEM)
SMEM = pl.BlockSpec(memory_space=pltpu.SMEM)


def call(kernel, inputs, outputs, scratch=(), cost=2000000000, specs=None, room=40):
    if specs is None:
        specs = [SMEM if x.dtype == jnp.int32 else VMEM for x in inputs]
    shapes = [jax.ShapeDtypeStruct(*out) for out in outputs]
    return pl.pallas_call(
        kernel,
        out_shape=shapes,
        in_specs=specs,
        out_specs=[VMEM] * len(shapes),
        scratch_shapes=[pltpu.VMEM(*one) if isinstance(one, tuple) else one for one in scratch],
        compiler_params=pltpu.CompilerParams(vmem_limit_bytes=room * 1024 * 1024),
        cost_estimate=pl.CostEstimate(flops=cost, bytes_accessed=1000000, transcendentals=0),
    )(*inputs)


def exchange(block, axes):
    return lax.all_to_all(block, axes, split_axis=0, concat_axis=0, tiled=True)


def per_device(coeffs, v_local, atom_pos, atom_charge, near_list, live_count):
    table = cosine_table()
    coeffs = coeffs[0]
    where = jnp.stack([lax.axis_index("gvec"), lax.axis_index(GROUP)]).astype(jnp.int32)
    (own,) = call(
        pick_kernel,
        [near_list, live_count, atom_pos, atom_charge.reshape(1, ATOMS)],
        [((SHARES, 1, 128), bf16)],
        [
            pltpu.SMEM((CAP,), jnp.int32),
            pltpu.SMEM((1,), jnp.int32),
            ((3, ATOMS), f32),
            ((1, ATOMS), f32),
            pltpu.SemaphoreType.DMA((4,)),
        ],
        specs=[pl.BlockSpec(memory_space=pl.ANY)] * 4,
        room=60,
    )
    group = exchange(own, GROUP)
    (sections,) = call(
        section_kernel,
        [coeffs, table],
        [((SHARES, 80, GRID), bf16)],
        [((GRID, 8, GRID), f32)],
    )
    rows = jnp.broadcast_to(group.reshape(1, SHARES, 128), (SHARES, SHARES, 128))
    got = exchange(lax.dynamic_update_slice(sections, rows, (0, 64, 0)), "gvec")
    stats, hot, halved, drawn = call(
        stats_kernel,
        [where, near_list, live_count, coeffs],
        [
            ((1, 128), f32),
            ((128, ATOMS), bf16),
            ((8, GRID, GRID), f32),
            ((8, GRID, GRID), f32),
        ],
    )
    potential, slots, blocks = call(
        potential_kernel,
        [where, got],
        [((8, GRID, GRID), f32), ((8, LIVE), f32), ((OWNERS, 128), f32)],
        [((4, GRID, LIVE), bf16), ((4, GRID, LIVE), f32)],
    )
    back, density, energy = call(
        field_kernel,
        [where, got, v_local, table, potential, stats],
        [
            ((SHARES, 64, GRID), bf16),
            ((8, GRID, GRID), f32),
            ((1, 128), f32),
        ],
        [((GRID, 8, GRID), f32), ((SHARES, 64, GRID), f32)],
    )
    returned = exchange(back, "gvec")
    (forces,) = call(
        force_kernel,
        [where, blocks, density, slots],
        [((OWNERS, 128), f32)],
        [
            ((8, GRID, GRID), bf16),
            ((4, 2, GRID, LIVE), bf16),
            ((4, GRID, LIVE), f32),
            ((4, GRID, LIVE), f32),
            ((4, 8, LIVE), f32),
            ((4, 8, LIVE), f32),
            ((8, LIVE), f32),
        ],
    )
    ahead, message = call(
        image_kernel,
        [where, returned, coeffs, table, forces, energy, halved],
        [((8, GRID, GRID), f32), ((OWNERS, 128), f32)],
        [((GRID, 8, GRID), f32), ((8, GRID, GRID), f32)],
    )
    arrived = exchange(message.reshape(OWNERS, 1, 128), EVERY).reshape(OWNERS, 128)
    waves, atom_force, energies, ratio, totals = call(
        final_kernel,
        [where, arrived, ahead, drawn, hot],
        [
            ((8, GRID, GRID), bf16),
            ((3, ATOMS), f32),
            ((1, 1), f32),
            ((1, 1), f32),
            ((1, 8), f32),
        ],
    )
    return (waves[None], energies.reshape(1), ratio.reshape(1), atom_force, totals.reshape(8))


def solution(mesh):
    return jax.shard_map(
        per_device,
        mesh=mesh,
        in_specs=(
            P(("band", "dom"), "gvec", None, None),
            P(None, "gvec", None),
            P(None, ("band", "gvec", "dom")),
            P(("band", "gvec", "dom")),
            P(("band", "gvec", "dom")),
            P(("band", "gvec", "dom")),
        ),
        out_specs=(
            P(("band", "dom"), "gvec", None, None),
            P(("band", "dom")),
            P(("band", "dom")),
            P(None, ("band", "gvec", "dom")),
            P(),
        ),
        check_vma=False,
    )
```

```python
import jax
import jax.numpy as jnp
import numpy as np
from jax import lax
from jax.experimental import pallas as pl
from jax.experimental.pallas import tpu as pltpu
from jax.sharding import PartitionSpec as P

GRID = 128
CAP = 16
BANDS = 16
SHARES = 16
OWNERS = 256
LIVE = 1024
ATOMS = 1024
SIGMA_FRACTIONS = (1.0 / 32.0, 1.0 / 16.0, 1.0 / 8.0, 1.0 / 4.0)
KERNEL_WEIGHTS = (1.0, 0.5, 0.25, 0.125)
EXPONENTS = tuple(0.5 / (GRID * fraction) ** 2 for fraction in SIGMA_FRACTIONS)
FORCE_UNIT = 1.0 / 4096.0
STEP_SIZE = 0.5
WAVE_STEP = float(np.pi / GRID)
CELLS = float(GRID**3)
DEAD_MARK = 4096.0
SCALAR_LANE = 96
f32 = jnp.float32
bf16 = jnp.bfloat16
EVERY = ("gvec", "band", "dom")
GROUP = ("band", "dom")


def cosine_table():
    points = np.arange(GRID).astype(np.float32)
    angles = np.float32(np.pi) * (points[:, None] + np.float32(0.5)) * points[None, :]
    angles = (angles / np.float32(GRID)).astype(np.float32)
    scales = np.where(
        points == 0, np.sqrt(np.float32(1.0 / GRID)), np.sqrt(np.float32(2.0 / GRID))
    ).astype(np.float32)
    return jnp.asarray(np.cos(angles).astype(np.float32) * scales[None, :], bf16)


def dot_nn(a, b):
    return lax.dot_general(a, b, (((1,), (0,)), ((), ())), preferred_element_type=f32)


def dot_nt(a, b):
    return lax.dot_general(a, b, (((1,), (1,)), ((), ())), preferred_element_type=f32)


def iota(shape, dim):
    return lax.broadcasted_iota(jnp.int32, shape, dim)


def occupancy(band):
    return 2.0 / (1.0 + jnp.exp((band.astype(f32) - 0.5 * BANDS) / (0.125 * BANDS)))


def near_one_hot(near_ref):
    slot = iota((128, 128), 0) % CAP
    wanted = jnp.zeros((128, 128), jnp.int32)
    for s in range(CAP):
        wanted = jnp.where(slot == s, near_ref[s], wanted)
    lanes = iota((128, 128), 1)
    parts = [
        jnp.where(wanted == lanes + 128 * t, 1.0, 0.0).astype(bf16) for t in range(ATOMS // 128)
    ]
    return jnp.concatenate(parts, axis=1)


def halves(value):
    high = value.astype(bf16).astype(f32)
    return high, value - high


def pick_kernel(
    near_hbm, count_hbm, pos_hbm, charge_hbm, out_ref,
    near_ref, count_ref, pos_ref, charge_ref, sems,
):
    moves = [
        pltpu.make_async_copy(near_hbm, near_ref, sems.at[0]),
        pltpu.make_async_copy(count_hbm, count_ref, sems.at[1]),
        pltpu.make_async_copy(pos_hbm, pos_ref, sems.at[2]),
        pltpu.make_async_copy(charge_hbm, charge_ref, sems.at[3]),
    ]
    for move in moves:
        move.start()
    for move in moves:
        move.wait()
    one_hot = near_one_hot(near_ref)
    wide = jnp.concatenate([pos_ref[...], charge_ref[...]], axis=0)
    high, low = halves(wide)
    both = jnp.concatenate([high, low], axis=0).astype(bf16)
    picked = dot_nt(both, one_hot)
    lane = iota((8, 128), 1)
    row = jnp.sum(jnp.where(lane // CAP == iota((8, 128), 0), picked, 0.0), axis=0, keepdims=True)
    lane_row = iota((1, 128), 1)
    dead = (lane_row < CAP) & (lane_row >= count_ref[0])
    row = jnp.where(dead, DEAD_MARK, row)
    out_ref[...] = jnp.broadcast_to(row.astype(bf16)[None], out_ref.shape)


def section_kernel(coeffs_ref, table_ref, out_ref, wide_ref):
    table = table_ref[...]
    along_z = dot_nt(coeffs_ref[...].reshape(1024, GRID), table).astype(bf16)
    for a in range(8):
        wide_ref[:, a, :] = dot_nn(table, along_z[a * GRID : (a + 1) * GRID])
    out_ref[:, :64, :] = wide_ref[...].reshape(SHARES, 64, GRID).astype(bf16)
    out_ref[:, 64:, :] = jnp.zeros((SHARES, 16, GRID), bf16)


def stats_kernel(
    near_ref, count_ref, coeffs_ref, out_ref, hot_ref, halved_ref, drawn_ref
):
    first = lax.axis_index("gvec") * 8
    q_wave = iota((GRID, GRID), 0).astype(f32) * WAVE_STEP
    l_wave = iota((1, GRID), 1).astype(f32) * WAVE_STEP
    sums = [jnp.zeros((1, GRID), f32) for _ in range(7)]
    for a in range(8):
        a_wave = (first + a).astype(f32) * WAVE_STEP
        value = coeffs_ref[a].astype(f32)
        square = value * value
        scaled = square * q_wave
        flat = jnp.sum(square, axis=0, keepdims=True)
        once = jnp.sum(scaled, axis=0, keepdims=True)
        twice = jnp.sum(scaled * q_wave, axis=0, keepdims=True)
        terms = (
            flat,
            a_wave * a_wave * flat,
            twice,
            l_wave * l_wave * flat,
            a_wave * once,
            a_wave * l_wave * flat,
            l_wave * once,
        )
        sums = [total + term for total, term in zip(sums, terms)]
    lane = iota((1, GRID), 1)
    weight = occupancy(jnp.full((1, 1), lax.axis_index(GROUP), jnp.int32)) / CELLS
    row = jnp.where(lane == SCALAR_LANE, jnp.sum(sums[0]), 0.0)
    for i in range(1, 7):
        value = jnp.sum(sums[i], axis=1, keepdims=True) * weight
        row = jnp.where(lane == SCALAR_LANE + 2 + i, value, row)
    out_ref[...] = row
    plane_waves = wave_tables()
    for a in range(8):
        halved = STEP_SIZE / (1.0 + kinetic_of(plane_waves, a))
        halved_ref[a] = halved
        drawn_ref[a] = halved * coeffs_ref[a].astype(f32)
    alive = iota((128, ATOMS), 0) % CAP < count_ref[0]
    hot_ref[...] = jnp.where(alive, near_one_hot(near_ref), jnp.zeros((), bf16))


def gauss_values(offset):
    wide = jnp.exp(-EXPONENTS[3] * offset * offset)
    values = [wide]
    for _ in range(3):
        square = values[0] * values[0]
        values.insert(0, square * square)
    return values


def slot_place(blocks):
    lane = iota((OWNERS, 128), 1)
    live = jnp.where((blocks < 1000.0) & (lane < CAP), 1.0, 0.0).astype(bf16)
    return live


def slot_masks(live):
    counts = dot_nn(live, jnp.ones((128, 128), bf16))
    before = jnp.where(iota((OWNERS, OWNERS), 1) < iota((OWNERS, OWNERS), 0), 1.0, 0.0).astype(bf16)
    starts = dot_nn(before, counts.astype(bf16))
    ends = starts + counts
    lane = iota((OWNERS, 128), 1).astype(f32)
    tiles = []
    for t in range(LIVE // 128):
        here = lane + (128.0 * t)
        tiles.append(jnp.where((here >= starts) & (here < ends), 1.0, 0.0).astype(bf16))
    return jnp.concatenate(tiles, axis=1), starts


def choose(held, starts, rows):
    coarse = jnp.floor(starts * 0.125)
    fine = starts - 8.0 * coarse
    left = jnp.concatenate(rows + [coarse.T[:16], fine.T[:16]], axis=0).astype(bf16)
    moved = dot_nn(left, held)
    size = moved.shape[0] - 32
    own_start = 8.0 * moved[size : size + 1] + moved[size + 16 : size + 17]
    slot = iota((1, LIVE), 1).astype(f32) - own_start
    chosen = (iota((128, LIVE), 0) % CAP).astype(f32) == slot
    return chosen, moved


def potential_kernel(
    got_ref, potential_ref, slots_ref, blocks_ref, gx_ref, depth_ref
):
    blocks = got_ref[:, 64:, :].astype(f32).reshape(OWNERS, 128)
    blocks_ref[...] = blocks
    held, starts = slot_masks(slot_place(blocks))
    chosen, moved = choose(held, starts, [blocks.T])
    pick = jnp.where(iota((8, 128), 1) // CAP == iota((8, 128), 0), 1.0, 0.0).astype(bf16)
    slots = dot_nn(pick, jnp.where(chosen, moved[:128], 0.0).astype(bf16))
    slots = slots[:4] + slots[4:]
    slots_ref[...] = jnp.concatenate([slots, slots], axis=0)
    points = iota((GRID, LIVE), 0).astype(f32)
    y_points = (lax.axis_index("gvec") * 8 + iota((8, LIVE), 0)).astype(f32)
    gx_values = gauss_values(points - slots[0:1])
    gy_values = gauss_values(y_points - slots[1:2])
    gz_values = gauss_values(points - slots[2:3])
    for k in range(4):
        gx_ref[k] = gx_values[k].astype(bf16)
        depth_ref[k] = gz_values[k] * (slots[3:4] * KERNEL_WEIGHTS[k])
    for y in range(8):
        potential = jnp.zeros((GRID, GRID), f32)
        for k in range(4):
            plane = (depth_ref[k] * gy_values[k][y : y + 1]).astype(bf16)
            potential = potential + dot_nt(gx_ref[k], plane)
        potential_ref[y] = potential


def field_kernel(
    got_ref, local_ref, table_ref, potential_ref, stats_ref,
    back_ref, density_ref, energy_ref, local_wide, back_wide,
):
    table = table_ref[...]
    got = got_ref[:, :64, :].astype(f32)
    local_wide[...] = local_ref[...].astype(f32)
    weight = occupancy(jnp.full((1, 1), lax.axis_index(GROUP), jnp.int32))
    energy = jnp.zeros((1, GRID), f32)
    for y in range(8):
        potential = potential_ref[y]
        mine = got[:, y * 8 : (y + 1) * 8, :].reshape(GRID, GRID).astype(bf16)
        real = dot_nn(table, mine).astype(bf16).astype(f32)
        density = weight * real * real
        density_ref[y] = density
        energy = energy + jnp.sum(density * potential, axis=0, keepdims=True)
        field = local_wide[:, y, :] + potential.astype(bf16).astype(f32)
        applied = (field * real).astype(bf16)
        back = lax.dot_general(
            table, applied, (((0,), (0,)), ((), ())), preferred_element_type=f32
        )
        back_wide[:, y * 8 : (y + 1) * 8, :] = back.reshape(SHARES, 8, GRID)
    back_ref[...] = back_wide[...].astype(bf16)
    total = jnp.sum(energy, axis=1, keepdims=True) / CELLS
    lane = iota((1, GRID), 1)
    energy_ref[...] = stats_ref[...] + jnp.where(lane == SCALAR_LANE + 9, total, 0.0)


def force_kernel(
    blocks_ref, density_ref, slots_ref, out_ref,
    turned_ref, x_ref, gz_ref, hz_ref, gy_ref, hy_ref, sum_ref,
):
    for y in range(8):
        turned_ref[y] = density_ref[y].T.astype(bf16)
    slots = slots_ref[...]
    points = iota((GRID, LIVE), 0).astype(f32)
    x_offset = points - slots[0:1]
    y_offset = (lax.axis_index("gvec") * 8 + iota((8, LIVE), 0)).astype(f32) - slots[1:2]
    z_offset = points - slots[2:3]
    gx_values = gauss_values(x_offset)
    gy_values = gauss_values(y_offset)
    gz_values = gauss_values(z_offset)
    for k in range(4):
        slope = 2.0 * EXPONENTS[k]
        x_ref[k, 0] = gx_values[k].astype(bf16)
        x_ref[k, 1] = (slope * x_offset * gx_values[k]).astype(bf16)
        gy_ref[k] = gy_values[k]
        hy_ref[k] = slope * y_offset * gy_values[k]
        scale = KERNEL_WEIGHTS[k] * slots[3:4]
        gz_ref[k] = gz_values[k] * scale
        hz_ref[k] = slope * z_offset * gz_values[k] * scale

    for chunk in range(LIVE // 128):
        lanes = pl.ds(chunk * 128, 128)
        force_x = jnp.zeros((1, 128), f32)
        force_y = jnp.zeros((1, 128), f32)
        force_z = jnp.zeros((1, 128), f32)
        for k in range(4):
            both = jnp.concatenate([x_ref[k, 0, :, lanes], x_ref[k, 1, :, lanes]], axis=1)
            value_y = gy_ref[k, :, lanes]
            slope_y = hy_ref[k, :, lanes]
            with_x = jnp.zeros((GRID, 128), f32)
            with_y = jnp.zeros((GRID, 128), f32)
            with_z = jnp.zeros((GRID, 128), f32)
            for y in range(8):
                part = dot_nn(turned_ref[y], both)
                with_x = with_x + part[:, 128:] * value_y[y : y + 1]
                with_y = with_y + part[:, :128] * slope_y[y : y + 1]
                with_z = with_z + part[:, :128] * value_y[y : y + 1]
            value_z = gz_ref[k, :, lanes]
            force_x = force_x + jnp.sum(with_x * value_z, axis=0, keepdims=True)
            force_y = force_y + jnp.sum(with_y * value_z, axis=0, keepdims=True)
            force_z = force_z + jnp.sum(with_z * hz_ref[k, :, lanes], axis=0, keepdims=True)
        sum_ref[0:1, lanes] = force_x
        sum_ref[1:2, lanes] = force_y
        sum_ref[2:3, lanes] = force_z

    forces = sum_ref[0:3, :] * -FORCE_UNIT
    high, low = halves(forces)
    stacked = jnp.concatenate(
        [jnp.broadcast_to(part[c : c + 1], (CAP, LIVE)) for part in (high, low) for c in range(3)]
        + [jnp.zeros((128 - 6 * CAP, LIVE), f32)],
        axis=0,
    )
    held, starts = slot_masks(slot_place(blocks_ref[...]))
    chosen, _ = choose(held, starts, [])
    per_slot = jnp.where(chosen, stacked, 0.0).astype(bf16)
    out_ref[...] = dot_nt(per_slot, held).T


def wave_tables():
    q_wave = iota((GRID, GRID), 0).astype(f32) * WAVE_STEP
    l_wave = iota((GRID, GRID), 1).astype(f32) * WAVE_STEP
    return q_wave * q_wave + l_wave * l_wave


def kinetic_of(plane_waves, a):
    a_wave = (lax.axis_index("gvec") * 8 + a).astype(f32) * WAVE_STEP
    return 0.5 * (a_wave * a_wave + plane_waves)


def image_kernel(
    got_ref, coeffs_ref, table_ref, force_ref, energy_ref, halved_ref,
    ahead_ref, out_ref, wide_ref, image_ref,
):
    table = table_ref[...]
    wide_ref[...] = got_ref[...].astype(f32).reshape(GRID, 8, GRID)
    plane_waves = wave_tables()
    overlap = jnp.zeros((1, GRID), f32)
    norm = jnp.zeros((1, GRID), f32)
    for a in range(8):
        along_y = lax.dot_general(
            table, wide_ref[:, a, :].astype(bf16), (((0,), (0,)), ((), ())),
            preferred_element_type=f32,
        ).astype(bf16)
        coeff = coeffs_ref[a].astype(f32)
        image = kinetic_of(plane_waves, a) * coeff + dot_nn(along_y, table)
        image_ref[a] = image
        ahead_ref[a] = coeff - halved_ref[a] * image
        overlap = overlap + jnp.sum(coeff * image, axis=0, keepdims=True)
        norm = norm + jnp.sum(coeff * coeff, axis=0, keepdims=True)
    overlap = jnp.sum(overlap, axis=1, keepdims=True)
    norm = jnp.sum(norm, axis=1, keepdims=True)
    mean = overlap / jnp.maximum(norm, 1e-30)
    spread = jnp.zeros((1, GRID), f32)
    for a in range(8):
        residual = image_ref[a] - mean * coeffs_ref[a].astype(f32)
        spread = spread + jnp.sum(residual * residual, axis=0, keepdims=True)
    spread = jnp.sum(spread, axis=1, keepdims=True)
    lane = iota((1, GRID), 1)
    row = jnp.where(lane == SCALAR_LANE + 1, overlap, energy_ref[...])
    row = jnp.where(lane == SCALAR_LANE + 2, spread, row)
    out_ref[...] = force_ref[...] + row


def final_kernel(
    got_ref, ahead_ref, drawn_ref, hot_ref,
    waves_ref, force_ref, energy_ref, ratio_ref, totals_ref,
):
    got = got_ref[...]
    by_band = jnp.sum(got.reshape(SHARES, BANDS, 128), axis=0)
    column = lambda i: slice(SCALAR_LANE + i, SCALAR_LANE + i + 1)
    norms = by_band[:, column(0)]
    energies = by_band[:, column(1)] / norms
    band = iota((BANDS, 1), 0)
    own = band == lax.axis_index(GROUP)
    energy = jnp.sum(jnp.where(own, energies, 0.0), axis=0, keepdims=True)
    norm = jnp.sum(jnp.where(own, norms, 0.0), axis=0, keepdims=True)
    part_norm = got[:, column(0)]
    part_energy = got[:, column(1)] / jnp.maximum(part_norm, 1e-30)
    shift = part_energy - energy
    spread = got[:, column(2)] + part_norm * shift * shift
    own_rows = iota((OWNERS, 1), 0) % BANDS == lax.axis_index(GROUP)
    squares = jnp.sum(jnp.where(own_rows, spread, 0.0), axis=0, keepdims=True)
    energy_ref[...] = energy
    ratio_ref[...] = squares / norm
    everything = jnp.sum(by_band, axis=0, keepdims=True)
    band_energy = jnp.sum(occupancy(band) * energies, axis=0, keepdims=True) / BANDS
    totals_ref[...] = jnp.concatenate(
        [everything[:, SCALAR_LANE + 3 : SCALAR_LANE + 10], band_energy], axis=1
    )
    for a in range(8):
        waves_ref[a] = (ahead_ref[a] + energy * drawn_ref[a]).astype(bf16)
    lane = iota((8, 128), 1)
    wanted = ((lane // CAP) % 3 == iota((8, 128), 0)) & (lane < SCALAR_LANE)
    split = jnp.where(wanted, everything, 0.0)
    high, rest = halves(split)
    middle, low = halves(rest)
    pieces = jnp.concatenate([high, middle, low, jnp.zeros_like(low)], axis=0).astype(bf16)
    placed = dot_nn(pieces, hot_ref[...])
    forces = placed[0:8] + placed[8:16] + placed[16:24]
    force_ref[...] = forces[:3]


VMEM = pl.BlockSpec(memory_space=pltpu.VMEM)
SMEM = pl.BlockSpec(memory_space=pltpu.SMEM)


def call(kernel, inputs, outputs, scratch=(), cost=2000000000, specs=None, room=40):
    if specs is None:
        specs = [SMEM if x.dtype == jnp.int32 else VMEM for x in inputs]
    shapes = [jax.ShapeDtypeStruct(*out) for out in outputs]
    return pl.pallas_call(
        kernel,
        out_shape=shapes,
        in_specs=specs,
        out_specs=[VMEM] * len(shapes),
        scratch_shapes=[pltpu.VMEM(*one) if isinstance(one, tuple) else one for one in scratch],
        compiler_params=pltpu.CompilerParams(vmem_limit_bytes=room * 1024 * 1024),
        cost_estimate=pl.CostEstimate(flops=cost, bytes_accessed=1000000, transcendentals=0),
    )(*inputs)


def exchange(block, axes):
    return lax.all_to_all(block, axes, split_axis=0, concat_axis=0, tiled=True)


def per_device(coeffs, v_local, atom_pos, atom_charge, near_list, live_count):
    table = cosine_table()
    coeffs = coeffs[0]
    (own,) = call(
        pick_kernel,
        [near_list, live_count, atom_pos, atom_charge.reshape(1, ATOMS)],
        [((SHARES, 1, 128), bf16)],
        [
            pltpu.SMEM((CAP,), jnp.int32),
            pltpu.SMEM((1,), jnp.int32),
            ((3, ATOMS), f32),
            ((1, ATOMS), f32),
            pltpu.SemaphoreType.DMA((4,)),
        ],
        specs=[pl.BlockSpec(memory_space=pl.ANY)] * 4,
        room=60,
    )
    group = exchange(own, GROUP)
    (sections,) = call(
        section_kernel,
        [coeffs, table],
        [((SHARES, 80, GRID), bf16)],
        [((GRID, 8, GRID), f32)],
    )
    rows = jnp.broadcast_to(group.reshape(1, SHARES, 128), (SHARES, SHARES, 128))
    got = exchange(lax.dynamic_update_slice(sections, rows, (0, 64, 0)), "gvec")
    stats, hot, halved, drawn = call(
        stats_kernel,
        [near_list, live_count, coeffs],
        [
            ((1, 128), f32),
            ((128, ATOMS), bf16),
            ((8, GRID, GRID), f32),
            ((8, GRID, GRID), f32),
        ],
    )
    potential, slots, blocks = call(
        potential_kernel,
        [got],
        [((8, GRID, GRID), f32), ((8, LIVE), f32), ((OWNERS, 128), f32)],
        [((4, GRID, LIVE), bf16), ((4, GRID, LIVE), f32)],
    )
    back, density, energy = call(
        field_kernel,
        [got, v_local, table, potential, stats],
        [
            ((SHARES, 64, GRID), bf16),
            ((8, GRID, GRID), f32),
            ((1, 128), f32),
        ],
        [((GRID, 8, GRID), f32), ((SHARES, 64, GRID), f32)],
    )
    returned = exchange(back, "gvec")
    (forces,) = call(
        force_kernel,
        [blocks, density, slots],
        [((OWNERS, 128), f32)],
        [
            ((8, GRID, GRID), bf16),
            ((4, 2, GRID, LIVE), bf16),
            ((4, GRID, LIVE), f32),
            ((4, GRID, LIVE), f32),
            ((4, 8, LIVE), f32),
            ((4, 8, LIVE), f32),
            ((8, LIVE), f32),
        ],
    )
    ahead, message = call(
        image_kernel,
        [returned, coeffs, table, forces, energy, halved],
        [((8, GRID, GRID), f32), ((OWNERS, 128), f32)],
        [((GRID, 8, GRID), f32), ((8, GRID, GRID), f32)],
    )
    arrived = exchange(message.reshape(OWNERS, 1, 128), EVERY).reshape(OWNERS, 128)
    waves, atom_force, energies, ratio, totals = call(
        final_kernel,
        [arrived, ahead, drawn, hot],
        [
            ((8, GRID, GRID), bf16),
            ((3, ATOMS), f32),
            ((1, 1), f32),
            ((1, 1), f32),
            ((1, 8), f32),
        ],
    )
    return (waves[None], energies.reshape(1), ratio.reshape(1), atom_force, totals.reshape(8))


def solution(mesh):
    return jax.shard_map(
        per_device,
        mesh=mesh,
        in_specs=(
            P(("band", "dom"), "gvec", None, None),
            P(None, "gvec", None),
            P(None, ("band", "gvec", "dom")),
            P(("band", "gvec", "dom")),
            P(("band", "gvec", "dom")),
            P(("band", "gvec", "dom")),
        ),
        out_specs=(
            P(("band", "dom"), "gvec", None, None),
            P(("band", "dom")),
            P(("band", "dom")),
            P(None, ("band", "gvec", "dom")),
            P(),
        ),
        check_vma=False,
    )
```

```python
import jax
import jax.numpy as jnp
import numpy as np
from jax import lax
from jax.experimental import pallas as pl
from jax.experimental.pallas import tpu as pltpu
from jax.sharding import PartitionSpec as P

GRID = 128
CAP = 16
BANDS = 16
SHARES = 16
OWNERS = 256
LIVE = 1024
ATOMS = 1024
SIGMA_FRACTIONS = (1.0 / 32.0, 1.0 / 16.0, 1.0 / 8.0, 1.0 / 4.0)
KERNEL_WEIGHTS = (1.0, 0.5, 0.25, 0.125)
EXPONENTS = tuple(0.5 / (GRID * fraction) ** 2 for fraction in SIGMA_FRACTIONS)
FORCE_UNIT = 1.0 / 4096.0
STEP_SIZE = 0.5
WAVE_STEP = float(np.pi / GRID)
CELLS = float(GRID**3)
DEAD_MARK = 4096.0
SCALAR_LANE = 96
f32 = jnp.float32
bf16 = jnp.bfloat16
EVERY = ("gvec", "band", "dom")
GROUP = ("band", "dom")


def cosine_table():
    points = np.arange(GRID).astype(np.float32)
    angles = np.float32(np.pi) * (points[:, None] + np.float32(0.5)) * points[None, :]
    angles = (angles / np.float32(GRID)).astype(np.float32)
    scales = np.where(
        points == 0, np.sqrt(np.float32(1.0 / GRID)), np.sqrt(np.float32(2.0 / GRID))
    ).astype(np.float32)
    return np.cos(angles).astype(np.float32) * scales[None, :]


def dot_nn(a, b):
    return lax.dot_general(a, b, (((1,), (0,)), ((), ())), preferred_element_type=f32)


def dot_nt(a, b):
    return lax.dot_general(a, b, (((1,), (1,)), ((), ())), preferred_element_type=f32)


def iota(shape, dim):
    return lax.broadcasted_iota(jnp.int32, shape, dim)


def occupancy(band):
    return 2.0 / (1.0 + jnp.exp((band.astype(f32) - 0.5 * BANDS) / (0.125 * BANDS)))


def near_one_hot(near_ref):
    slot = iota((128, 128), 0) % CAP
    wanted = jnp.zeros((128, 128), jnp.int32)
    for s in range(CAP):
        wanted = jnp.where(slot == s, near_ref[s], wanted)
    lanes = iota((128, 128), 1)
    parts = [
        jnp.where(wanted == lanes + 128 * t, 1.0, 0.0).astype(bf16) for t in range(ATOMS // 128)
    ]
    return jnp.concatenate(parts, axis=1)


def halves(value):
    high = value.astype(bf16).astype(f32)
    return high, value - high


def pick_kernel(
    near_hbm, count_hbm, pos_hbm, charge_hbm, out_ref,
    near_ref, count_ref, pos_ref, charge_ref, sems,
):
    moves = [
        pltpu.make_async_copy(near_hbm, near_ref, sems.at[0]),
        pltpu.make_async_copy(count_hbm, count_ref, sems.at[1]),
        pltpu.make_async_copy(pos_hbm, pos_ref, sems.at[2]),
        pltpu.make_async_copy(charge_hbm, charge_ref, sems.at[3]),
    ]
    for move in moves:
        move.start()
    moves[0].wait()
    slot = iota((1, 128), 1) % CAP
    wanted = jnp.zeros((1, 128), jnp.int32)
    for s in range(CAP):
        wanted = jnp.where(slot == s, near_ref[s], wanted)
    parts = [
        jnp.where(iota((128, 128), 0) + 128 * t == wanted, 1.0, 0.0).astype(bf16)
        for t in range(ATOMS // 128)
    ]
    one_hot = jnp.concatenate(parts, axis=0)
    for move in moves[1:]:
        move.wait()
    wide = jnp.concatenate([pos_ref[...], charge_ref[...]], axis=0)
    high, low = halves(wide)
    both = jnp.concatenate([high, low], axis=0).astype(bf16)
    picked = dot_nn(both, one_hot)
    lane = iota((8, 128), 1)
    row = jnp.sum(jnp.where(lane // CAP == iota((8, 128), 0), picked, 0.0), axis=0, keepdims=True)
    lane_row = iota((1, 128), 1)
    dead = (lane_row < CAP) & (lane_row >= count_ref[0])
    row = jnp.where(dead, DEAD_MARK, row)
    out_ref[...] = jnp.broadcast_to(row.astype(bf16)[None], out_ref.shape)


def section_kernel(coeffs_ref, table_ref, out_ref, wide_ref):
    table = table_ref[...]
    along_z = dot_nt(coeffs_ref[...].reshape(1024, GRID), table).astype(bf16)
    for a in range(8):
        wide_ref[:, a, :] = dot_nn(table, along_z[a * GRID : (a + 1) * GRID])
    out_ref[:, :64, :] = wide_ref[...].reshape(SHARES, 64, GRID).astype(bf16)
    out_ref[:, 64:, :] = jnp.zeros((SHARES, 16, GRID), bf16)


def stats_kernel(
    near_ref, count_ref, coeffs_ref, local_ref,
    out_ref, hot_ref, halved_ref, drawn_ref, turned_ref, wide_ref,
):
    first = lax.axis_index("gvec") * 8
    q_wave = iota((GRID, GRID), 0).astype(f32) * WAVE_STEP
    l_wave = iota((1, GRID), 1).astype(f32) * WAVE_STEP
    sums = [jnp.zeros((1, GRID), f32) for _ in range(7)]
    for a in range(8):
        a_wave = (first + a).astype(f32) * WAVE_STEP
        value = coeffs_ref[a].astype(f32)
        square = value * value
        scaled = square * q_wave
        flat = jnp.sum(square, axis=0, keepdims=True)
        once = jnp.sum(scaled, axis=0, keepdims=True)
        twice = jnp.sum(scaled * q_wave, axis=0, keepdims=True)
        terms = (
            flat,
            a_wave * a_wave * flat,
            twice,
            l_wave * l_wave * flat,
            a_wave * once,
            a_wave * l_wave * flat,
            l_wave * once,
        )
        sums = [total + term for total, term in zip(sums, terms)]
    lane = iota((1, GRID), 1)
    weight = occupancy(jnp.full((1, 1), lax.axis_index(GROUP), jnp.int32)) / CELLS
    row = jnp.where(lane == SCALAR_LANE, jnp.sum(sums[0]), 0.0)
    for i in range(1, 7):
        value = jnp.sum(sums[i], axis=1, keepdims=True) * weight
        row = jnp.where(lane == SCALAR_LANE + 2 + i, value, row)
    out_ref[...] = row
    plane_waves = wave_tables()
    for a in range(8):
        halved = STEP_SIZE / (1.0 + kinetic_of(plane_waves, a))
        halved_ref[a] = halved
        drawn_ref[a] = halved * coeffs_ref[a].astype(f32)
    wide_ref[...] = local_ref[...].astype(f32)
    for y in range(8):
        turned_ref[y] = wide_ref[:, y, :]
    alive = iota((128, ATOMS), 0) % CAP < count_ref[0]
    hot_ref[...] = jnp.where(alive, near_one_hot(near_ref), jnp.zeros((), bf16))


def gauss_values(offset):
    wide = jnp.exp(-EXPONENTS[3] * offset * offset)
    values = [wide]
    for _ in range(3):
        square = values[0] * values[0]
        values.insert(0, square * square)
    return values


def slot_place(blocks):
    lane = iota((OWNERS, 128), 1)
    live = jnp.where((blocks < 1000.0) & (lane < CAP), 1.0, 0.0).astype(bf16)
    return live


def slot_masks(live):
    counts = dot_nn(live, jnp.ones((128, 128), bf16))
    before = jnp.where(iota((OWNERS, OWNERS), 1) < iota((OWNERS, OWNERS), 0), 1.0, 0.0).astype(bf16)
    starts = dot_nn(before, counts.astype(bf16))
    ends = starts + counts
    lane = iota((OWNERS, 128), 1).astype(f32)
    tiles = []
    for t in range(LIVE // 128):
        here = lane + (128.0 * t)
        tiles.append(jnp.where((here >= starts) & (here < ends), 1.0, 0.0).astype(bf16))
    return jnp.concatenate(tiles, axis=1), starts


def choose(held, starts, rows):
    coarse = jnp.floor(starts * 0.125)
    fine = starts - 8.0 * coarse
    left = jnp.concatenate(rows + [coarse.T[:16], fine.T[:16]], axis=0).astype(bf16)
    moved = dot_nn(left, held)
    size = moved.shape[0] - 32
    own_start = 8.0 * moved[size : size + 1] + moved[size + 16 : size + 17]
    slot = iota((1, LIVE), 1).astype(f32) - own_start
    chosen = (iota((128, LIVE), 0) % CAP).astype(f32) == slot
    return chosen, moved


def potential_kernel(
    got_ref, potential_ref, slots_ref, blocks_ref, gx_ref, depth_ref
):
    blocks = got_ref[:, 64:, :].astype(f32).reshape(OWNERS, 128)
    blocks_ref[...] = blocks
    held, starts = slot_masks(slot_place(blocks))
    chosen, moved = choose(held, starts, [blocks.T])
    pick = jnp.where(iota((8, 128), 1) // CAP == iota((8, 128), 0), 1.0, 0.0).astype(bf16)
    slots = dot_nn(pick, jnp.where(chosen, moved[:128], 0.0).astype(bf16))
    slots = slots[:4] + slots[4:]
    slots_ref[...] = jnp.concatenate([slots, slots], axis=0)
    points = iota((GRID, LIVE), 0).astype(f32)
    y_points = (lax.axis_index("gvec") * 8 + iota((8, LIVE), 0)).astype(f32)
    gx_values = gauss_values(points - slots[0:1])
    gy_values = gauss_values(y_points - slots[1:2])
    gz_values = gauss_values(points - slots[2:3])
    for k in range(4):
        gx_ref[k] = gx_values[k].astype(bf16)
        depth_ref[k] = gz_values[k] * (slots[3:4] * KERNEL_WEIGHTS[k])
    for y in range(8):
        potential = jnp.zeros((GRID, GRID), f32)
        for k in range(4):
            plane = (depth_ref[k] * gy_values[k][y : y + 1]).astype(bf16)
            potential = potential + dot_nt(gx_ref[k], plane)
        potential_ref[y] = potential


def field_kernel(
    got_ref, local_ref, table_ref, turned_ref, potential_ref, stats_ref,
    back_ref, density_ref, energy_ref, back_wide,
):
    table = table_ref[...]
    got = got_ref[:, :64, :].astype(f32)
    turned = turned_ref[...]
    weight = occupancy(jnp.full((1, 1), lax.axis_index(GROUP), jnp.int32))
    energy = jnp.zeros((1, GRID), f32)
    for y in range(8):
        potential = potential_ref[y]
        mine = got[:, y * 8 : (y + 1) * 8, :].reshape(GRID, GRID).astype(bf16)
        real = dot_nn(table, mine).astype(bf16).astype(f32)
        density = weight * real * real
        density_ref[y] = density
        energy = energy + jnp.sum(density * potential, axis=0, keepdims=True)
        field = local_ref[y] + potential.astype(bf16).astype(f32)
        applied = (field * real).astype(bf16)
        back = dot_nn(turned, applied)
        back_wide[:, y * 8 : (y + 1) * 8, :] = back.reshape(SHARES, 8, GRID)
    back_ref[...] = back_wide[...].astype(bf16)
    total = jnp.sum(energy, axis=1, keepdims=True) / CELLS
    lane = iota((1, GRID), 1)
    energy_ref[...] = stats_ref[...] + jnp.where(lane == SCALAR_LANE + 9, total, 0.0)


def force_kernel(
    blocks_ref, density_ref, slots_ref, out_ref,
    turned_ref, x_ref, gz_ref, hz_ref, gy_ref, hy_ref, sum_ref,
):
    for y in range(8):
        turned_ref[y] = density_ref[y].T.astype(bf16)
    slots = slots_ref[...]
    points = iota((GRID, LIVE), 0).astype(f32)
    x_offset = points - slots[0:1]
    y_offset = (lax.axis_index("gvec") * 8 + iota((8, LIVE), 0)).astype(f32) - slots[1:2]
    z_offset = points - slots[2:3]
    gx_values = gauss_values(x_offset)
    gy_values = gauss_values(y_offset)
    gz_values = gauss_values(z_offset)
    for k in range(4):
        slope = 2.0 * EXPONENTS[k]
        x_ref[k, 0] = gx_values[k].astype(bf16)
        x_ref[k, 1] = (slope * x_offset * gx_values[k]).astype(bf16)
        gy_ref[k] = gy_values[k]
        hy_ref[k] = slope * y_offset * gy_values[k]
        scale = KERNEL_WEIGHTS[k] * slots[3:4]
        gz_ref[k] = gz_values[k] * scale
        hz_ref[k] = slope * z_offset * gz_values[k] * scale

    for chunk in range(LIVE // 128):
        lanes = pl.ds(chunk * 128, 128)
        force_x = jnp.zeros((1, 128), f32)
        force_y = jnp.zeros((1, 128), f32)
        force_z = jnp.zeros((1, 128), f32)
        for k in range(4):
            both = jnp.concatenate([x_ref[k, 0, :, lanes], x_ref[k, 1, :, lanes]], axis=1)
            value_y = gy_ref[k, :, lanes]
            slope_y = hy_ref[k, :, lanes]
            with_x = jnp.zeros((GRID, 128), f32)
            with_y = jnp.zeros((GRID, 128), f32)
            with_z = jnp.zeros((GRID, 128), f32)
            for y in range(8):
                part = dot_nn(turned_ref[y], both)
                with_x = with_x + part[:, 128:] * value_y[y : y + 1]
                with_y = with_y + part[:, :128] * slope_y[y : y + 1]
                with_z = with_z + part[:, :128] * value_y[y : y + 1]
            value_z = gz_ref[k, :, lanes]
            force_x = force_x + jnp.sum(with_x * value_z, axis=0, keepdims=True)
            force_y = force_y + jnp.sum(with_y * value_z, axis=0, keepdims=True)
            force_z = force_z + jnp.sum(with_z * hz_ref[k, :, lanes], axis=0, keepdims=True)
        sum_ref[0:1, lanes] = force_x
        sum_ref[1:2, lanes] = force_y
        sum_ref[2:3, lanes] = force_z

    forces = sum_ref[0:3, :] * -FORCE_UNIT
    high, low = halves(forces)
    stacked = jnp.concatenate(
        [jnp.broadcast_to(part[c : c + 1], (CAP, LIVE)) for part in (high, low) for c in range(3)]
        + [jnp.zeros((128 - 6 * CAP, LIVE), f32)],
        axis=0,
    )
    held, starts = slot_masks(slot_place(blocks_ref[...]))
    chosen, _ = choose(held, starts, [])
    per_slot = jnp.where(chosen, stacked, 0.0).astype(bf16)
    out_ref[...] = dot_nt(per_slot, held).T


def wave_tables():
    q_wave = iota((GRID, GRID), 0).astype(f32) * WAVE_STEP
    l_wave = iota((GRID, GRID), 1).astype(f32) * WAVE_STEP
    return q_wave * q_wave + l_wave * l_wave


def kinetic_of(plane_waves, a):
    a_wave = (lax.axis_index("gvec") * 8 + a).astype(f32) * WAVE_STEP
    return 0.5 * (a_wave * a_wave + plane_waves)


def image_kernel(
    got_ref, coeffs_ref, table_ref, turned_ref, force_ref, energy_ref, halved_ref,
    ahead_ref, out_ref, wide_ref, image_ref,
):
    table = table_ref[...]
    turned = turned_ref[...]
    wide_ref[...] = got_ref[...].astype(f32).reshape(GRID, 8, GRID)
    plane_waves = wave_tables()
    overlap = jnp.zeros((1, GRID), f32)
    norm = jnp.zeros((1, GRID), f32)
    for a in range(8):
        along_y = dot_nn(turned, wide_ref[:, a, :].astype(bf16)).astype(bf16)
        coeff = coeffs_ref[a].astype(f32)
        image = kinetic_of(plane_waves, a) * coeff + dot_nn(along_y, table)
        image_ref[a] = image
        ahead_ref[a] = coeff - halved_ref[a] * image
        overlap = overlap + jnp.sum(coeff * image, axis=0, keepdims=True)
        norm = norm + jnp.sum(coeff * coeff, axis=0, keepdims=True)
    overlap = jnp.sum(overlap, axis=1, keepdims=True)
    norm = jnp.sum(norm, axis=1, keepdims=True)
    mean = overlap / jnp.maximum(norm, 1e-30)
    spread = jnp.zeros((1, GRID), f32)
    for a in range(8):
        residual = image_ref[a] - mean * coeffs_ref[a].astype(f32)
        spread = spread + jnp.sum(residual * residual, axis=0, keepdims=True)
    spread = jnp.sum(spread, axis=1, keepdims=True)
    lane = iota((1, GRID), 1)
    row = jnp.where(lane == SCALAR_LANE + 1, overlap, energy_ref[...])
    row = jnp.where(lane == SCALAR_LANE + 2, spread, row)
    out_ref[...] = force_ref[...] + row


def final_kernel(
    got_ref, ahead_ref, drawn_ref, hot_ref,
    waves_ref, force_ref, energy_ref, ratio_ref, totals_ref,
):
    got = got_ref[...]
    by_band = jnp.sum(got.reshape(SHARES, BANDS, 128), axis=0)
    column = lambda i: slice(SCALAR_LANE + i, SCALAR_LANE + i + 1)
    norms = by_band[:, column(0)]
    energies = by_band[:, column(1)] / norms
    band = iota((BANDS, 1), 0)
    own = band == lax.axis_index(GROUP)
    energy = jnp.sum(jnp.where(own, energies, 0.0), axis=0, keepdims=True)
    norm = jnp.sum(jnp.where(own, norms, 0.0), axis=0, keepdims=True)
    part_norm = got[:, column(0)]
    part_energy = got[:, column(1)] / jnp.maximum(part_norm, 1e-30)
    shift = part_energy - energy
    spread = got[:, column(2)] + part_norm * shift * shift
    own_rows = iota((OWNERS, 1), 0) % BANDS == lax.axis_index(GROUP)
    squares = jnp.sum(jnp.where(own_rows, spread, 0.0), axis=0, keepdims=True)
    energy_ref[...] = energy
    ratio_ref[...] = squares / norm
    everything = jnp.sum(by_band, axis=0, keepdims=True)
    band_energy = jnp.sum(occupancy(band) * energies, axis=0, keepdims=True) / BANDS
    totals_ref[...] = jnp.concatenate(
        [everything[:, SCALAR_LANE + 3 : SCALAR_LANE + 10], band_energy], axis=1
    )
    for a in range(8):
        waves_ref[a] = (ahead_ref[a] + energy * drawn_ref[a]).astype(bf16)
    lane = iota((8, 128), 1)
    wanted = ((lane // CAP) % 3 == iota((8, 128), 0)) & (lane < SCALAR_LANE)
    split = jnp.where(wanted, everything, 0.0)
    high, rest = halves(split)
    middle, low = halves(rest)
    pieces = jnp.concatenate([high, middle, low, jnp.zeros_like(low)], axis=0).astype(bf16)
    placed = dot_nn(pieces, hot_ref[...])
    forces = placed[0:8] + placed[8:16] + placed[16:24]
    force_ref[...] = forces[:3]


VMEM = pl.BlockSpec(memory_space=pltpu.VMEM)
SMEM = pl.BlockSpec(memory_space=pltpu.SMEM)


def call(kernel, inputs, outputs, scratch=(), cost=2000000000, specs=None, room=40):
    if specs is None:
        specs = [SMEM if x.dtype == jnp.int32 else VMEM for x in inputs]
    shapes = [jax.ShapeDtypeStruct(*out) for out in outputs]
    return pl.pallas_call(
        kernel,
        out_shape=shapes,
        in_specs=specs,
        out_specs=[VMEM] * len(shapes),
        scratch_shapes=[pltpu.VMEM(*one) if isinstance(one, tuple) else one for one in scratch],
        compiler_params=pltpu.CompilerParams(vmem_limit_bytes=room * 1024 * 1024),
        cost_estimate=pl.CostEstimate(flops=cost, bytes_accessed=1000000, transcendentals=0),
    )(*inputs)


def exchange(block, axes):
    return lax.all_to_all(block, axes, split_axis=0, concat_axis=0, tiled=True)


def per_device(coeffs, v_local, atom_pos, atom_charge, near_list, live_count):
    cosines = cosine_table()
    table, turned = jnp.asarray(cosines, bf16), jnp.asarray(cosines.T, bf16)
    coeffs = coeffs[0]
    (own,) = call(
        pick_kernel,
        [near_list, live_count, atom_pos, atom_charge.reshape(1, ATOMS)],
        [((SHARES, 1, 128), bf16)],
        [
            pltpu.SMEM((CAP,), jnp.int32),
            pltpu.SMEM((1,), jnp.int32),
            ((3, ATOMS), f32),
            ((1, ATOMS), f32),
            pltpu.SemaphoreType.DMA((4,)),
        ],
        specs=[pl.BlockSpec(memory_space=pl.ANY)] * 4,
        room=60,
    )
    group = exchange(own, GROUP)
    (sections,) = call(
        section_kernel,
        [coeffs, table],
        [((SHARES, 80, GRID), bf16)],
        [((GRID, 8, GRID), f32)],
    )
    rows = jnp.broadcast_to(group.reshape(1, SHARES, 128), (SHARES, SHARES, 128))
    got = exchange(lax.dynamic_update_slice(sections, rows, (0, 64, 0)), "gvec")
    stats, hot, halved, drawn, local = call(
        stats_kernel,
        [near_list, live_count, coeffs, v_local],
        [
            ((1, 128), f32),
            ((128, ATOMS), bf16),
            ((8, GRID, GRID), f32),
            ((8, GRID, GRID), f32),
            ((8, GRID, GRID), f32),
        ],
        [((GRID, 8, GRID), f32)],
    )
    potential, slots, blocks = call(
        potential_kernel,
        [got],
        [((8, GRID, GRID), f32), ((8, LIVE), f32), ((OWNERS, 128), f32)],
        [((4, GRID, LIVE), bf16), ((4, GRID, LIVE), f32)],
    )
    back, density, energy = call(
        field_kernel,
        [got, local, table, turned, potential, stats],
        [
            ((SHARES, 64, GRID), bf16),
            ((8, GRID, GRID), f32),
            ((1, 128), f32),
        ],
        [((SHARES, 64, GRID), f32)],
    )
    returned = exchange(back, "gvec")
    (forces,) = call(
        force_kernel,
        [blocks, density, slots],
        [((OWNERS, 128), f32)],
        [
            ((8, GRID, GRID), bf16),
            ((4, 2, GRID, LIVE), bf16),
            ((4, GRID, LIVE), f32),
            ((4, GRID, LIVE), f32),
            ((4, 8, LIVE), f32),
            ((4, 8, LIVE), f32),
            ((8, LIVE), f32),
        ],
    )
    ahead, message = call(
        image_kernel,
        [returned, coeffs, table, turned, forces, energy, halved],
        [((8, GRID, GRID), f32), ((OWNERS, 128), f32)],
        [((GRID, 8, GRID), f32), ((8, GRID, GRID), f32)],
    )
    arrived = exchange(message.reshape(OWNERS, 1, 128), EVERY).reshape(OWNERS, 128)
    waves, atom_force, energies, ratio, totals = call(
        final_kernel,
        [arrived, ahead, drawn, hot],
        [
            ((8, GRID, GRID), bf16),
            ((3, ATOMS), f32),
            ((1, 1), f32),
            ((1, 1), f32),
            ((1, 8), f32),
        ],
    )
    return (waves[None], energies.reshape(1), ratio.reshape(1), atom_force, totals.reshape(8))


def solution(mesh):
    return jax.shard_map(
        per_device,
        mesh=mesh,
        in_specs=(
            P(("band", "dom"), "gvec", None, None),
            P(None, "gvec", None),
            P(None, ("band", "gvec", "dom")),
            P(("band", "gvec", "dom")),
            P(("band", "gvec", "dom")),
            P(("band", "gvec", "dom")),
        ),
        out_specs=(
            P(("band", "dom"), "gvec", None, None),
            P(("band", "dom")),
            P(("band", "dom")),
            P(None, ("band", "gvec", "dom")),
            P(),
        ),
        check_vma=False,
    )
```

```python
import jax
import jax.numpy as jnp
import numpy as np
from jax import lax
from jax.experimental import pallas as pl
from jax.experimental.pallas import tpu as pltpu
from jax.sharding import PartitionSpec as P

GRID = 128
CAP = 16
BANDS = 16
SHARES = 16
OWNERS = 256
LIVE = 1024
ATOMS = 1024
SIGMA_FRACTIONS = (1.0 / 32.0, 1.0 / 16.0, 1.0 / 8.0, 1.0 / 4.0)
KERNEL_WEIGHTS = (1.0, 0.5, 0.25, 0.125)
EXPONENTS = tuple(0.5 / (GRID * fraction) ** 2 for fraction in SIGMA_FRACTIONS)
FORCE_UNIT = 1.0 / 4096.0
STEP_SIZE = 0.5
WAVE_STEP = float(np.pi / GRID)
CELLS = float(GRID**3)
DEAD_MARK = 4096.0
SCALAR_LANE = 96
f32 = jnp.float32
bf16 = jnp.bfloat16
EVERY = ("gvec", "band", "dom")
GROUP = ("band", "dom")


def cosine_table():
    points = np.arange(GRID).astype(np.float32)
    angles = np.float32(np.pi) * (points[:, None] + np.float32(0.5)) * points[None, :]
    angles = (angles / np.float32(GRID)).astype(np.float32)
    scales = np.where(
        points == 0, np.sqrt(np.float32(1.0 / GRID)), np.sqrt(np.float32(2.0 / GRID))
    ).astype(np.float32)
    return np.cos(angles).astype(np.float32) * scales[None, :]


def dot_nn(a, b):
    return lax.dot_general(a, b, (((1,), (0,)), ((), ())), preferred_element_type=f32)


def dot_nt(a, b):
    return lax.dot_general(a, b, (((1,), (1,)), ((), ())), preferred_element_type=f32)


def iota(shape, dim):
    return lax.broadcasted_iota(jnp.int32, shape, dim)


def occupancy(band):
    return 2.0 / (1.0 + jnp.exp((band.astype(f32) - 0.5 * BANDS) / (0.125 * BANDS)))


def near_one_hot(near_ref):
    slot = iota((128, 128), 0) % CAP
    wanted = jnp.zeros((128, 128), jnp.int32)
    for s in range(CAP):
        wanted = jnp.where(slot == s, near_ref[s], wanted)
    lanes = iota((128, 128), 1)
    parts = [
        jnp.where(wanted == lanes + 128 * t, 1.0, 0.0).astype(bf16) for t in range(ATOMS // 128)
    ]
    return jnp.concatenate(parts, axis=1)


def halves(value):
    high = value.astype(bf16).astype(f32)
    return high, value - high


def pick_kernel(
    near_hbm, count_hbm, pos_hbm, charge_hbm, out_ref,
    near_ref, count_ref, pos_ref, charge_ref, sems,
):
    moves = [
        pltpu.make_async_copy(near_hbm, near_ref, sems.at[0]),
        pltpu.make_async_copy(count_hbm, count_ref, sems.at[1]),
        pltpu.make_async_copy(pos_hbm, pos_ref, sems.at[2]),
        pltpu.make_async_copy(charge_hbm, charge_ref, sems.at[3]),
    ]
    for move in moves:
        move.start()
    moves[0].wait()
    slot = iota((1, 128), 1) % CAP
    wanted = jnp.zeros((1, 128), jnp.int32)
    for s in range(CAP):
        wanted = jnp.where(slot == s, near_ref[s], wanted)
    parts = [
        jnp.where(iota((128, 128), 0) + 128 * t == wanted, 1.0, 0.0).astype(bf16)
        for t in range(ATOMS // 128)
    ]
    one_hot = jnp.concatenate(parts, axis=0)
    for move in moves[1:]:
        move.wait()
    wide = jnp.concatenate([pos_ref[...], charge_ref[...]], axis=0)
    high, low = halves(wide)
    both = jnp.concatenate([high, low], axis=0).astype(bf16)
    picked = dot_nn(both, one_hot)
    lane = iota((8, 128), 1)
    row = jnp.sum(jnp.where(lane // CAP == iota((8, 128), 0), picked, 0.0), axis=0, keepdims=True)
    lane_row = iota((1, 128), 1)
    dead = (lane_row < CAP) & (lane_row >= count_ref[0])
    row = jnp.where(dead, DEAD_MARK, row)
    out_ref[...] = jnp.broadcast_to(row.astype(bf16)[None], out_ref.shape)


def section_kernel(coeffs_ref, table_ref, out_ref, wide_ref):
    table = table_ref[...]
    along_z = dot_nt(coeffs_ref[...].reshape(1024, GRID), table).astype(bf16)
    for a in range(8):
        wide_ref[:, a, :] = dot_nn(table, along_z[a * GRID : (a + 1) * GRID])
    out_ref[:, :64, :] = wide_ref[...].reshape(SHARES, 64, GRID).astype(bf16)
    out_ref[:, 64:, :] = jnp.zeros((SHARES, 16, GRID), bf16)


def stats_kernel(
    near_ref, count_ref, coeffs_ref, local_ref,
    out_ref, hot_ref, halved_ref, drawn_ref, turned_ref, wide_ref,
):
    first = lax.axis_index("gvec") * 8
    q_wave = iota((GRID, GRID), 0).astype(f32) * WAVE_STEP
    l_wave = iota((1, GRID), 1).astype(f32) * WAVE_STEP
    sums = [jnp.zeros((1, GRID), f32) for _ in range(7)]
    for a in range(8):
        a_wave = (first + a).astype(f32) * WAVE_STEP
        value = coeffs_ref[a].astype(f32)
        square = value * value
        scaled = square * q_wave
        flat = jnp.sum(square, axis=0, keepdims=True)
        once = jnp.sum(scaled, axis=0, keepdims=True)
        twice = jnp.sum(scaled * q_wave, axis=0, keepdims=True)
        terms = (
            flat,
            a_wave * a_wave * flat,
            twice,
            l_wave * l_wave * flat,
            a_wave * once,
            a_wave * l_wave * flat,
            l_wave * once,
        )
        sums = [total + term for total, term in zip(sums, terms)]
    lane = iota((1, GRID), 1)
    weight = occupancy(jnp.full((1, 1), lax.axis_index(GROUP), jnp.int32)) / CELLS
    row = jnp.where(lane == SCALAR_LANE, jnp.sum(sums[0]), 0.0)
    for i in range(1, 7):
        value = jnp.sum(sums[i], axis=1, keepdims=True) * weight
        row = jnp.where(lane == SCALAR_LANE + 2 + i, value, row)
    out_ref[...] = row
    plane_waves = wave_tables()
    for a in range(8):
        halved = STEP_SIZE / (1.0 + kinetic_of(plane_waves, a))
        halved_ref[a] = halved
        drawn_ref[a] = halved * coeffs_ref[a].astype(f32)
    wide_ref[...] = local_ref[...].astype(f32)
    for y in range(8):
        turned_ref[y] = wide_ref[:, y, :]
    alive = iota((128, ATOMS), 0) % CAP < count_ref[0]
    hot_ref[...] = jnp.where(alive, near_one_hot(near_ref), jnp.zeros((), bf16))


def gauss_values(offset):
    wide = jnp.exp(-EXPONENTS[3] * offset * offset)
    values = [wide]
    for _ in range(3):
        square = values[0] * values[0]
        values.insert(0, square * square)
    return values


def slot_place(blocks):
    lane = iota((OWNERS, 128), 1)
    live = jnp.where((blocks < 1000.0) & (lane < CAP), 1.0, 0.0).astype(bf16)
    return live


def slot_masks(live):
    counts = dot_nn(live, jnp.ones((128, 128), bf16))
    before = jnp.where(iota((OWNERS, OWNERS), 1) < iota((OWNERS, OWNERS), 0), 1.0, 0.0).astype(bf16)
    starts = dot_nn(before, counts.astype(bf16))
    ends = starts + counts
    lane = iota((OWNERS, 128), 1).astype(f32)
    tiles = []
    for t in range(LIVE // 128):
        here = lane + (128.0 * t)
        tiles.append(jnp.where((here >= starts) & (here < ends), 1.0, 0.0).astype(bf16))
    return jnp.concatenate(tiles, axis=1), starts


def choose(held, starts, rows):
    coarse = jnp.floor(starts * 0.125)
    fine = starts - 8.0 * coarse
    left = jnp.concatenate(rows + [coarse.T[:16], fine.T[:16]], axis=0).astype(bf16)
    moved = dot_nn(left, held)
    size = moved.shape[0] - 32
    own_start = 8.0 * moved[size : size + 1] + moved[size + 16 : size + 17]
    slot = iota((1, LIVE), 1).astype(f32) - own_start
    chosen = (iota((128, LIVE), 0) % CAP).astype(f32) == slot
    return chosen, moved


def potential_kernel(
    got_ref, potential_ref, slots_ref, blocks_ref, gx_ref, depth_ref
):
    blocks = got_ref[:, 64:, :].astype(f32).reshape(OWNERS, 128)
    blocks_ref[...] = blocks
    held, starts = slot_masks(slot_place(blocks))
    chosen, moved = choose(held, starts, [blocks.T])
    pick = jnp.where(iota((8, 128), 1) // CAP == iota((8, 128), 0), 1.0, 0.0).astype(bf16)
    slots = dot_nn(pick, jnp.where(chosen, moved[:128], 0.0).astype(bf16))
    slots = slots[:4] + slots[4:]
    slots_ref[...] = jnp.concatenate([slots, slots], axis=0)
    points = iota((GRID, LIVE), 0).astype(f32)
    y_points = (lax.axis_index("gvec") * 8 + iota((8, LIVE), 0)).astype(f32)
    gx_values = gauss_values(points - slots[0:1])
    gy_values = gauss_values(y_points - slots[1:2])
    gz_values = gauss_values(points - slots[2:3])
    for k in range(4):
        gx_ref[k] = gx_values[k]
        depth_ref[k] = (gz_values[k] * (slots[3:4] * KERNEL_WEIGHTS[k])).astype(bf16)
    for k in range(4):
        plane = jnp.concatenate(
            [(gx_ref[k] * gy_values[k][y : y + 1]).astype(bf16) for y in range(8)], axis=0
        )
        part = dot_nt(plane, depth_ref[k]).reshape(8, GRID, GRID)
        potential_ref[...] = part if k == 0 else potential_ref[...] + part


def field_kernel(
    got_ref, local_ref, table_ref, turned_ref, potential_ref, stats_ref,
    back_ref, density_ref, energy_ref, back_wide,
):
    table = table_ref[...]
    got = got_ref[:, :64, :].astype(f32)
    turned = turned_ref[...]
    weight = occupancy(jnp.full((1, 1), lax.axis_index(GROUP), jnp.int32))
    energy = jnp.zeros((1, GRID), f32)
    for y in range(8):
        potential = potential_ref[y]
        mine = got[:, y * 8 : (y + 1) * 8, :].reshape(GRID, GRID).astype(bf16)
        real = dot_nn(table, mine).astype(bf16).astype(f32)
        density = weight * real * real
        density_ref[y] = density
        energy = energy + jnp.sum(density * potential, axis=0, keepdims=True)
        field = local_ref[y] + potential.astype(bf16).astype(f32)
        applied = (field * real).astype(bf16)
        back = dot_nn(turned, applied)
        back_wide[:, y * 8 : (y + 1) * 8, :] = back.reshape(SHARES, 8, GRID)
    back_ref[...] = back_wide[...].astype(bf16)
    total = jnp.sum(energy, axis=1, keepdims=True) / CELLS
    lane = iota((1, GRID), 1)
    energy_ref[...] = stats_ref[...] + jnp.where(lane == SCALAR_LANE + 9, total, 0.0)


def force_kernel(
    blocks_ref, density_ref, slots_ref, out_ref,
    turned_ref, x_ref, gz_ref, hz_ref, gy_ref, hy_ref, sum_ref,
):
    for y in range(8):
        turned_ref[y] = density_ref[y].T.astype(bf16)
    slots = slots_ref[...]
    points = iota((GRID, LIVE), 0).astype(f32)
    x_offset = points - slots[0:1]
    y_offset = (lax.axis_index("gvec") * 8 + iota((8, LIVE), 0)).astype(f32) - slots[1:2]
    z_offset = points - slots[2:3]
    gx_values = gauss_values(x_offset)
    gy_values = gauss_values(y_offset)
    gz_values = gauss_values(z_offset)
    for k in range(4):
        slope = 2.0 * EXPONENTS[k]
        x_ref[k, 0] = gx_values[k].astype(bf16)
        x_ref[k, 1] = (slope * x_offset * gx_values[k]).astype(bf16)
        gy_ref[k] = gy_values[k]
        hy_ref[k] = slope * y_offset * gy_values[k]
        scale = KERNEL_WEIGHTS[k] * slots[3:4]
        gz_ref[k] = gz_values[k] * scale
        hz_ref[k] = slope * z_offset * gz_values[k] * scale

    for chunk in range(LIVE // 128):
        lanes = pl.ds(chunk * 128, 128)
        force_x = jnp.zeros((1, 128), f32)
        force_y = jnp.zeros((1, 128), f32)
        force_z = jnp.zeros((1, 128), f32)
        for k in range(4):
            both = jnp.concatenate([x_ref[k, 0, :, lanes], x_ref[k, 1, :, lanes]], axis=1)
            value_y = gy_ref[k, :, lanes]
            slope_y = hy_ref[k, :, lanes]
            with_x = jnp.zeros((GRID, 128), f32)
            with_y = jnp.zeros((GRID, 128), f32)
            with_z = jnp.zeros((GRID, 128), f32)
            for y in range(8):
                part = dot_nn(turned_ref[y], both)
                with_x = with_x + part[:, 128:] * value_y[y : y + 1]
                with_y = with_y + part[:, :128] * slope_y[y : y + 1]
                with_z = with_z + part[:, :128] * value_y[y : y + 1]
            value_z = gz_ref[k, :, lanes]
            force_x = force_x + jnp.sum(with_x * value_z, axis=0, keepdims=True)
            force_y = force_y + jnp.sum(with_y * value_z, axis=0, keepdims=True)
            force_z = force_z + jnp.sum(with_z * hz_ref[k, :, lanes], axis=0, keepdims=True)
        sum_ref[0:1, lanes] = force_x
        sum_ref[1:2, lanes] = force_y
        sum_ref[2:3, lanes] = force_z

    forces = sum_ref[0:3, :] * -FORCE_UNIT
    high, low = halves(forces)
    stacked = jnp.concatenate(
        [jnp.broadcast_to(part[c : c + 1], (CAP, LIVE)) for part in (high, low) for c in range(3)]
        + [jnp.zeros((128 - 6 * CAP, LIVE), f32)],
        axis=0,
    )
    held, starts = slot_masks(slot_place(blocks_ref[...]))
    chosen, _ = choose(held, starts, [])
    per_slot = jnp.where(chosen, stacked, 0.0).astype(bf16)
    out_ref[...] = dot_nt(per_slot, held).T


def wave_tables():
    q_wave = iota((GRID, GRID), 0).astype(f32) * WAVE_STEP
    l_wave = iota((GRID, GRID), 1).astype(f32) * WAVE_STEP
    return q_wave * q_wave + l_wave * l_wave


def kinetic_of(plane_waves, a):
    a_wave = (lax.axis_index("gvec") * 8 + a).astype(f32) * WAVE_STEP
    return 0.5 * (a_wave * a_wave + plane_waves)


def image_kernel(
    got_ref, coeffs_ref, table_ref, turned_ref, force_ref, energy_ref, halved_ref,
    ahead_ref, out_ref, wide_ref, image_ref,
):
    table = table_ref[...]
    turned = turned_ref[...]
    wide_ref[...] = got_ref[...].astype(f32).reshape(GRID, 8, GRID)
    plane_waves = wave_tables()
    overlap = jnp.zeros((1, GRID), f32)
    norm = jnp.zeros((1, GRID), f32)
    for a in range(8):
        along_y = dot_nn(turned, wide_ref[:, a, :].astype(bf16)).astype(bf16)
        coeff = coeffs_ref[a].astype(f32)
        image = kinetic_of(plane_waves, a) * coeff + dot_nn(along_y, table)
        image_ref[a] = image
        ahead_ref[a] = coeff - halved_ref[a] * image
        overlap = overlap + jnp.sum(coeff * image, axis=0, keepdims=True)
        norm = norm + jnp.sum(coeff * coeff, axis=0, keepdims=True)
    overlap = jnp.sum(overlap, axis=1, keepdims=True)
    norm = jnp.sum(norm, axis=1, keepdims=True)
    mean = overlap / jnp.maximum(norm, 1e-30)
    spread = jnp.zeros((1, GRID), f32)
    for a in range(8):
        residual = image_ref[a] - mean * coeffs_ref[a].astype(f32)
        spread = spread + jnp.sum(residual * residual, axis=0, keepdims=True)
    spread = jnp.sum(spread, axis=1, keepdims=True)
    lane = iota((1, GRID), 1)
    row = jnp.where(lane == SCALAR_LANE + 1, overlap, energy_ref[...])
    row = jnp.where(lane == SCALAR_LANE + 2, spread, row)
    out_ref[...] = force_ref[...] + row


def final_kernel(
    got_ref, ahead_ref, drawn_ref, hot_ref,
    waves_ref, force_ref, energy_ref, ratio_ref, totals_ref,
):
    got = got_ref[...]
    by_band = jnp.sum(got.reshape(SHARES, BANDS, 128), axis=0)
    column = lambda i: slice(SCALAR_LANE + i, SCALAR_LANE + i + 1)
    norms = by_band[:, column(0)]
    energies = by_band[:, column(1)] / norms
    band = iota((BANDS, 1), 0)
    own = band == lax.axis_index(GROUP)
    energy = jnp.sum(jnp.where(own, energies, 0.0), axis=0, keepdims=True)
    norm = jnp.sum(jnp.where(own, norms, 0.0), axis=0, keepdims=True)
    part_norm = got[:, column(0)]
    part_energy = got[:, column(1)] / jnp.maximum(part_norm, 1e-30)
    shift = part_energy - energy
    spread = got[:, column(2)] + part_norm * shift * shift
    own_rows = iota((OWNERS, 1), 0) % BANDS == lax.axis_index(GROUP)
    squares = jnp.sum(jnp.where(own_rows, spread, 0.0), axis=0, keepdims=True)
    energy_ref[...] = energy
    ratio_ref[...] = squares / norm
    everything = jnp.sum(by_band, axis=0, keepdims=True)
    band_energy = jnp.sum(occupancy(band) * energies, axis=0, keepdims=True) / BANDS
    totals_ref[...] = jnp.concatenate(
        [everything[:, SCALAR_LANE + 3 : SCALAR_LANE + 10], band_energy], axis=1
    )
    for a in range(8):
        waves_ref[a] = (ahead_ref[a] + energy * drawn_ref[a]).astype(bf16)
    lane = iota((8, 128), 1)
    wanted = ((lane // CAP) % 3 == iota((8, 128), 0)) & (lane < SCALAR_LANE)
    split = jnp.where(wanted, everything, 0.0)
    high, rest = halves(split)
    middle, low = halves(rest)
    pieces = jnp.concatenate([high, middle, low, jnp.zeros_like(low)], axis=0).astype(bf16)
    placed = dot_nn(pieces, hot_ref[...])
    forces = placed[0:8] + placed[8:16] + placed[16:24]
    force_ref[...] = forces[:3]


VMEM = pl.BlockSpec(memory_space=pltpu.VMEM)
SMEM = pl.BlockSpec(memory_space=pltpu.SMEM)


def call(kernel, inputs, outputs, scratch=(), cost=2000000000, specs=None, room=40):
    if specs is None:
        specs = [SMEM if x.dtype == jnp.int32 else VMEM for x in inputs]
    shapes = [jax.ShapeDtypeStruct(*out) for out in outputs]
    return pl.pallas_call(
        kernel,
        out_shape=shapes,
        in_specs=specs,
        out_specs=[VMEM] * len(shapes),
        scratch_shapes=[pltpu.VMEM(*one) if isinstance(one, tuple) else one for one in scratch],
        compiler_params=pltpu.CompilerParams(vmem_limit_bytes=room * 1024 * 1024),
        cost_estimate=pl.CostEstimate(flops=cost, bytes_accessed=1000000, transcendentals=0),
    )(*inputs)


def exchange(block, axes):
    return lax.all_to_all(block, axes, split_axis=0, concat_axis=0, tiled=True)


def per_device(coeffs, v_local, atom_pos, atom_charge, near_list, live_count):
    cosines = cosine_table()
    table, turned = jnp.asarray(cosines, bf16), jnp.asarray(cosines.T, bf16)
    coeffs = coeffs[0]
    (own,) = call(
        pick_kernel,
        [near_list, live_count, atom_pos, atom_charge.reshape(1, ATOMS)],
        [((SHARES, 1, 128), bf16)],
        [
            pltpu.SMEM((CAP,), jnp.int32),
            pltpu.SMEM((1,), jnp.int32),
            ((3, ATOMS), f32),
            ((1, ATOMS), f32),
            pltpu.SemaphoreType.DMA((4,)),
        ],
        specs=[pl.BlockSpec(memory_space=pl.ANY)] * 4,
        room=60,
    )
    group = exchange(own, GROUP)
    (sections,) = call(
        section_kernel,
        [coeffs, table],
        [((SHARES, 80, GRID), bf16)],
        [((GRID, 8, GRID), f32)],
    )
    rows = jnp.broadcast_to(group.reshape(1, SHARES, 128), (SHARES, SHARES, 128))
    got = exchange(lax.dynamic_update_slice(sections, rows, (0, 64, 0)), "gvec")
    stats, hot, halved, drawn, local = call(
        stats_kernel,
        [near_list, live_count, coeffs, v_local],
        [
            ((1, 128), f32),
            ((128, ATOMS), bf16),
            ((8, GRID, GRID), f32),
            ((8, GRID, GRID), f32),
            ((8, GRID, GRID), f32),
        ],
        [((GRID, 8, GRID), f32)],
    )
    potential, slots, blocks = call(
        potential_kernel,
        [got],
        [((8, GRID, GRID), f32), ((8, LIVE), f32), ((OWNERS, 128), f32)],
        [((4, GRID, LIVE), f32), ((4, GRID, LIVE), bf16)],
    )
    back, density, energy = call(
        field_kernel,
        [got, local, table, turned, potential, stats],
        [
            ((SHARES, 64, GRID), bf16),
            ((8, GRID, GRID), f32),
            ((1, 128), f32),
        ],
        [((SHARES, 64, GRID), f32)],
    )
    returned = exchange(back, "gvec")
    (forces,) = call(
        force_kernel,
        [blocks, density, slots],
        [((OWNERS, 128), f32)],
        [
            ((8, GRID, GRID), bf16),
            ((4, 2, GRID, LIVE), bf16),
            ((4, GRID, LIVE), f32),
            ((4, GRID, LIVE), f32),
            ((4, 8, LIVE), f32),
            ((4, 8, LIVE), f32),
            ((8, LIVE), f32),
        ],
    )
    ahead, message = call(
        image_kernel,
        [returned, coeffs, table, turned, forces, energy, halved],
        [((8, GRID, GRID), f32), ((OWNERS, 128), f32)],
        [((GRID, 8, GRID), f32), ((8, GRID, GRID), f32)],
    )
    arrived = exchange(message.reshape(OWNERS, 1, 128), EVERY).reshape(OWNERS, 128)
    waves, atom_force, energies, ratio, totals = call(
        final_kernel,
        [arrived, ahead, drawn, hot],
        [
            ((8, GRID, GRID), bf16),
            ((3, ATOMS), f32),
            ((1, 1), f32),
            ((1, 1), f32),
            ((1, 8), f32),
        ],
    )
    return (waves[None], energies.reshape(1), ratio.reshape(1), atom_force, totals.reshape(8))


def solution(mesh):
    return jax.shard_map(
        per_device,
        mesh=mesh,
        in_specs=(
            P(("band", "dom"), "gvec", None, None),
            P(None, "gvec", None),
            P(None, ("band", "gvec", "dom")),
            P(("band", "gvec", "dom")),
            P(("band", "gvec", "dom")),
            P(("band", "gvec", "dom")),
        ),
        out_specs=(
            P(("band", "dom"), "gvec", None, None),
            P(("band", "dom")),
            P(("band", "dom")),
            P(None, ("band", "gvec", "dom")),
            P(),
        ),
        check_vma=False,
    )
```

```python
import jax
import jax.numpy as jnp
import numpy as np
from jax import lax
from jax.experimental import pallas as pl
from jax.experimental.pallas import tpu as pltpu
from jax.sharding import PartitionSpec as P

GRID = 128
CAP = 16
BANDS = 16
SHARES = 16
OWNERS = 256
LIVE = 1024
ATOMS = 1024
SIGMA_FRACTIONS = (1.0 / 32.0, 1.0 / 16.0, 1.0 / 8.0, 1.0 / 4.0)
KERNEL_WEIGHTS = (1.0, 0.5, 0.25, 0.125)
EXPONENTS = tuple(0.5 / (GRID * fraction) ** 2 for fraction in SIGMA_FRACTIONS)
FORCE_UNIT = 1.0 / 4096.0
STEP_SIZE = 0.5
WAVE_STEP = float(np.pi / GRID)
CELLS = float(GRID**3)
DEAD_MARK = 4096.0
SCALAR_LANE = 96
f32 = jnp.float32
bf16 = jnp.bfloat16
EVERY = ("gvec", "band", "dom")
GROUP = ("band", "dom")


def cosine_table():
    points = np.arange(GRID).astype(np.float32)
    angles = np.float32(np.pi) * (points[:, None] + np.float32(0.5)) * points[None, :]
    angles = (angles / np.float32(GRID)).astype(np.float32)
    scales = np.where(
        points == 0, np.sqrt(np.float32(1.0 / GRID)), np.sqrt(np.float32(2.0 / GRID))
    ).astype(np.float32)
    return np.cos(angles).astype(np.float32) * scales[None, :]


def dot_nn(a, b):
    return lax.dot_general(a, b, (((1,), (0,)), ((), ())), preferred_element_type=f32)


def dot_nt(a, b):
    return lax.dot_general(a, b, (((1,), (1,)), ((), ())), preferred_element_type=f32)


def iota(shape, dim):
    return lax.broadcasted_iota(jnp.int32, shape, dim)


def occupancy(band):
    return 2.0 / (1.0 + jnp.exp((band.astype(f32) - 0.5 * BANDS) / (0.125 * BANDS)))


def near_one_hot(near_ref):
    slot = iota((128, 128), 0) % CAP
    wanted = jnp.zeros((128, 128), jnp.int32)
    for s in range(CAP):
        wanted = jnp.where(slot == s, near_ref[s], wanted)
    lanes = iota((128, 128), 1)
    parts = [
        jnp.where(wanted == lanes + 128 * t, 1.0, 0.0).astype(bf16) for t in range(ATOMS // 128)
    ]
    return jnp.concatenate(parts, axis=1)


def halves(value):
    high = value.astype(bf16).astype(f32)
    return high, value - high


def pick_kernel(
    near_hbm, count_hbm, pos_hbm, charge_hbm, out_ref,
    near_ref, count_ref, pos_ref, charge_ref, sems,
):
    moves = [
        pltpu.make_async_copy(near_hbm, near_ref, sems.at[0]),
        pltpu.make_async_copy(count_hbm, count_ref, sems.at[1]),
        pltpu.make_async_copy(pos_hbm, pos_ref, sems.at[2]),
        pltpu.make_async_copy(charge_hbm, charge_ref, sems.at[3]),
    ]
    for move in moves:
        move.start()
    moves[0].wait()
    slot = iota((1, 128), 1) % CAP
    wanted = jnp.zeros((1, 128), jnp.int32)
    for s in range(CAP):
        wanted = jnp.where(slot == s, near_ref[s], wanted)
    parts = [
        jnp.where(iota((128, 128), 0) + 128 * t == wanted, 1.0, 0.0).astype(bf16)
        for t in range(ATOMS // 128)
    ]
    one_hot = jnp.concatenate(parts, axis=0)
    for move in moves[1:]:
        move.wait()
    wide = jnp.concatenate([pos_ref[...], charge_ref[...]], axis=0)
    high, low = halves(wide)
    both = jnp.concatenate([high, low], axis=0).astype(bf16)
    picked = dot_nn(both, one_hot)
    lane = iota((8, 128), 1)
    row = jnp.sum(jnp.where(lane // CAP == iota((8, 128), 0), picked, 0.0), axis=0, keepdims=True)
    lane_row = iota((1, 128), 1)
    dead = (lane_row < CAP) & (lane_row >= count_ref[0])
    row = jnp.where(dead, DEAD_MARK, row)
    out_ref[...] = jnp.broadcast_to(row.astype(bf16)[None], out_ref.shape)


def section_kernel(coeffs_ref, table_ref, out_ref, wide_ref):
    table = table_ref[...]
    along_z = dot_nt(coeffs_ref[...].reshape(1024, GRID), table).astype(bf16)
    for a in range(8):
        wide_ref[:, a, :] = dot_nn(table, along_z[a * GRID : (a + 1) * GRID])
    out_ref[:, :64, :] = wide_ref[...].reshape(SHARES, 64, GRID).astype(bf16)
    out_ref[:, 64:, :] = jnp.zeros((SHARES, 16, GRID), bf16)


def stats_kernel(
    near_ref, count_ref, coeffs_ref, local_ref,
    out_ref, hot_ref, halved_ref, drawn_ref, turned_ref, wide_ref,
):
    first = lax.axis_index("gvec") * 8
    q_wave = iota((GRID, GRID), 0).astype(f32) * WAVE_STEP
    l_wave = iota((1, GRID), 1).astype(f32) * WAVE_STEP
    sums = [jnp.zeros((1, GRID), f32) for _ in range(7)]
    for a in range(8):
        a_wave = (first + a).astype(f32) * WAVE_STEP
        value = coeffs_ref[a].astype(f32)
        square = value * value
        scaled = square * q_wave
        flat = jnp.sum(square, axis=0, keepdims=True)
        once = jnp.sum(scaled, axis=0, keepdims=True)
        twice = jnp.sum(scaled * q_wave, axis=0, keepdims=True)
        terms = (
            flat,
            a_wave * a_wave * flat,
            twice,
            l_wave * l_wave * flat,
            a_wave * once,
            a_wave * l_wave * flat,
            l_wave * once,
        )
        sums = [total + term for total, term in zip(sums, terms)]
    lane = iota((1, GRID), 1)
    weight = occupancy(jnp.full((1, 1), lax.axis_index(GROUP), jnp.int32)) / CELLS
    row = jnp.where(lane == SCALAR_LANE, jnp.sum(sums[0]), 0.0)
    for i in range(1, 7):
        value = jnp.sum(sums[i], axis=1, keepdims=True) * weight
        row = jnp.where(lane == SCALAR_LANE + 2 + i, value, row)
    out_ref[...] = row
    plane_waves = wave_tables()
    for a in range(8):
        halved = STEP_SIZE / (1.0 + kinetic_of(plane_waves, a))
        halved_ref[a] = halved
        drawn_ref[a] = halved * coeffs_ref[a].astype(f32)
    wide_ref[...] = local_ref[...].astype(f32)
    for y in range(8):
        turned_ref[y] = wide_ref[:, y, :]
    alive = iota((128, ATOMS), 0) % CAP < count_ref[0]
    hot_ref[...] = jnp.where(alive, near_one_hot(near_ref), jnp.zeros((), bf16))


def gauss_values(offset):
    wide = jnp.exp(-EXPONENTS[3] * offset * offset)
    values = [wide]
    for _ in range(3):
        square = values[0] * values[0]
        values.insert(0, square * square)
    return values


def slot_place(blocks):
    lane = iota((OWNERS, 128), 1)
    live = jnp.where((blocks < 1000.0) & (lane < CAP), 1.0, 0.0).astype(bf16)
    return live


def slot_masks(live):
    counts = dot_nn(live, jnp.ones((128, 128), bf16))
    before = jnp.where(iota((OWNERS, OWNERS), 1) < iota((OWNERS, OWNERS), 0), 1.0, 0.0).astype(bf16)
    starts = dot_nn(before, counts.astype(bf16))
    ends = starts + counts
    lane = iota((OWNERS, 128), 1).astype(f32)
    tiles = []
    for t in range(LIVE // 128):
        here = lane + (128.0 * t)
        tiles.append(jnp.where((here >= starts) & (here < ends), 1.0, 0.0).astype(bf16))
    return jnp.concatenate(tiles, axis=1), starts


def choose(held, starts, rows):
    coarse = jnp.floor(starts * 0.125)
    fine = starts - 8.0 * coarse
    left = jnp.concatenate(rows + [coarse.T[:16], fine.T[:16]], axis=0).astype(bf16)
    moved = dot_nn(left, held)
    size = moved.shape[0] - 32
    own_start = 8.0 * moved[size : size + 1] + moved[size + 16 : size + 17]
    slot = iota((1, LIVE), 1).astype(f32) - own_start
    chosen = (iota((128, LIVE), 0) % CAP).astype(f32) == slot
    return chosen, moved


def potential_kernel(
    got_ref, potential_ref, slots_ref, blocks_ref, gx_ref, depth_ref
):
    blocks = got_ref[:, 64:, :].astype(f32).reshape(OWNERS, 128)
    blocks_ref[...] = blocks
    held, starts = slot_masks(slot_place(blocks))
    chosen, moved = choose(held, starts, [blocks.T])
    pick = jnp.where(iota((8, 128), 1) // CAP == iota((8, 128), 0), 1.0, 0.0).astype(bf16)
    slots = dot_nn(pick, jnp.where(chosen, moved[:128], 0.0).astype(bf16))
    slots = slots[:4] + slots[4:]
    slots_ref[...] = jnp.concatenate([slots, slots], axis=0)
    points = iota((GRID, LIVE), 0).astype(f32)
    y_points = (lax.axis_index("gvec") * 8 + iota((8, LIVE), 0)).astype(f32)
    gx_values = gauss_values(points - slots[0:1])
    gy_values = gauss_values(y_points - slots[1:2])
    gz_values = gauss_values(points - slots[2:3])
    for k in range(4):
        gx_ref[k] = gx_values[k]
        depth_ref[k] = (gz_values[k] * (slots[3:4] * KERNEL_WEIGHTS[k])).astype(bf16)
    for k in range(4):
        plane = jnp.concatenate(
            [(gx_ref[k] * gy_values[k][y : y + 1]).astype(bf16) for y in range(8)], axis=0
        )
        part = dot_nt(plane, depth_ref[k]).reshape(8, GRID, GRID)
        potential_ref[...] = part if k == 0 else potential_ref[...] + part


def field_kernel(
    got_ref, local_ref, table_ref, turned_ref, potential_ref, stats_ref,
    back_ref, density_ref, energy_ref, back_wide,
):
    table = table_ref[...]
    got = got_ref[:, :64, :].astype(f32)
    turned = turned_ref[...]
    weight = occupancy(jnp.full((1, 1), lax.axis_index(GROUP), jnp.int32))
    energy = jnp.zeros((1, GRID), f32)
    for y in range(8):
        potential = potential_ref[y]
        mine = got[:, y * 8 : (y + 1) * 8, :].reshape(GRID, GRID).astype(bf16)
        real = dot_nn(table, mine).astype(bf16).astype(f32)
        density = weight * real * real
        density_ref[y] = density
        energy = energy + jnp.sum(density * potential, axis=0, keepdims=True)
        field = local_ref[y] + potential.astype(bf16).astype(f32)
        applied = (field * real).astype(bf16)
        back = dot_nn(turned, applied)
        back_wide[:, y * 8 : (y + 1) * 8, :] = back.reshape(SHARES, 8, GRID)
    back_ref[...] = back_wide[...].astype(bf16)
    total = jnp.sum(energy, axis=1, keepdims=True) / CELLS
    lane = iota((1, GRID), 1)
    energy_ref[...] = stats_ref[...] + jnp.where(lane == SCALAR_LANE + 9, total, 0.0)


def slab_kernel(
    got_ref, local_ref, table_ref, turned_ref, stats_ref,
    back_ref, density_ref, energy_ref, slots_ref, blocks_ref,
    gx_ref, depth_ref, potential_ref, back_wide,
):
    potential_kernel(got_ref, potential_ref, slots_ref, blocks_ref, gx_ref, depth_ref)
    field_kernel(
        got_ref, local_ref, table_ref, turned_ref, potential_ref, stats_ref,
        back_ref, density_ref, energy_ref, back_wide,
    )


def force_kernel(
    blocks_ref, density_ref, slots_ref, out_ref,
    turned_ref, x_ref, gz_ref, hz_ref, gy_ref, hy_ref, sum_ref,
):
    for y in range(8):
        turned_ref[y] = density_ref[y].T.astype(bf16)
    slots = slots_ref[...]
    points = iota((GRID, LIVE), 0).astype(f32)
    x_offset = points - slots[0:1]
    y_offset = (lax.axis_index("gvec") * 8 + iota((8, LIVE), 0)).astype(f32) - slots[1:2]
    z_offset = points - slots[2:3]
    gx_values = gauss_values(x_offset)
    gy_values = gauss_values(y_offset)
    gz_values = gauss_values(z_offset)
    for k in range(4):
        slope = 2.0 * EXPONENTS[k]
        x_ref[k, 0] = gx_values[k].astype(bf16)
        x_ref[k, 1] = (slope * x_offset * gx_values[k]).astype(bf16)
        gy_ref[k] = gy_values[k]
        hy_ref[k] = slope * y_offset * gy_values[k]
        scale = KERNEL_WEIGHTS[k] * slots[3:4]
        gz_ref[k] = gz_values[k] * scale
        hz_ref[k] = slope * z_offset * gz_values[k] * scale

    for chunk in range(LIVE // 128):
        lanes = pl.ds(chunk * 128, 128)
        force_x = jnp.zeros((1, 128), f32)
        force_y = jnp.zeros((1, 128), f32)
        force_z = jnp.zeros((1, 128), f32)
        for k in range(4):
            both = jnp.concatenate([x_ref[k, 0, :, lanes], x_ref[k, 1, :, lanes]], axis=1)
            value_y = gy_ref[k, :, lanes]
            slope_y = hy_ref[k, :, lanes]
            with_x = jnp.zeros((GRID, 128), f32)
            with_y = jnp.zeros((GRID, 128), f32)
            with_z = jnp.zeros((GRID, 128), f32)
            for y in range(8):
                part = dot_nn(turned_ref[y], both)
                with_x = with_x + part[:, 128:] * value_y[y : y + 1]
                with_y = with_y + part[:, :128] * slope_y[y : y + 1]
                with_z = with_z + part[:, :128] * value_y[y : y + 1]
            value_z = gz_ref[k, :, lanes]
            force_x = force_x + jnp.sum(with_x * value_z, axis=0, keepdims=True)
            force_y = force_y + jnp.sum(with_y * value_z, axis=0, keepdims=True)
            force_z = force_z + jnp.sum(with_z * hz_ref[k, :, lanes], axis=0, keepdims=True)
        sum_ref[0:1, lanes] = force_x
        sum_ref[1:2, lanes] = force_y
        sum_ref[2:3, lanes] = force_z

    forces = sum_ref[0:3, :] * -FORCE_UNIT
    high, low = halves(forces)
    stacked = jnp.concatenate(
        [jnp.broadcast_to(part[c : c + 1], (CAP, LIVE)) for part in (high, low) for c in range(3)]
        + [jnp.zeros((128 - 6 * CAP, LIVE), f32)],
        axis=0,
    )
    held, starts = slot_masks(slot_place(blocks_ref[...]))
    chosen, _ = choose(held, starts, [])
    per_slot = jnp.where(chosen, stacked, 0.0).astype(bf16)
    out_ref[...] = dot_nt(per_slot, held).T


def wave_tables():
    q_wave = iota((GRID, GRID), 0).astype(f32) * WAVE_STEP
    l_wave = iota((GRID, GRID), 1).astype(f32) * WAVE_STEP
    return q_wave * q_wave + l_wave * l_wave


def kinetic_of(plane_waves, a):
    a_wave = (lax.axis_index("gvec") * 8 + a).astype(f32) * WAVE_STEP
    return 0.5 * (a_wave * a_wave + plane_waves)


def image_kernel(
    got_ref, coeffs_ref, table_ref, turned_ref, force_ref, energy_ref, halved_ref,
    ahead_ref, out_ref, wide_ref, image_ref,
):
    table = table_ref[...]
    turned = turned_ref[...]
    wide_ref[...] = got_ref[...].astype(f32).reshape(GRID, 8, GRID)
    plane_waves = wave_tables()
    overlap = jnp.zeros((1, GRID), f32)
    norm = jnp.zeros((1, GRID), f32)
    for a in range(8):
        along_y = dot_nn(turned, wide_ref[:, a, :].astype(bf16)).astype(bf16)
        coeff = coeffs_ref[a].astype(f32)
        image = kinetic_of(plane_waves, a) * coeff + dot_nn(along_y, table)
        image_ref[a] = image
        ahead_ref[a] = coeff - halved_ref[a] * image
        overlap = overlap + jnp.sum(coeff * image, axis=0, keepdims=True)
        norm = norm + jnp.sum(coeff * coeff, axis=0, keepdims=True)
    overlap = jnp.sum(overlap, axis=1, keepdims=True)
    norm = jnp.sum(norm, axis=1, keepdims=True)
    mean = overlap / jnp.maximum(norm, 1e-30)
    spread = jnp.zeros((1, GRID), f32)
    for a in range(8):
        residual = image_ref[a] - mean * coeffs_ref[a].astype(f32)
        spread = spread + jnp.sum(residual * residual, axis=0, keepdims=True)
    spread = jnp.sum(spread, axis=1, keepdims=True)
    lane = iota((1, GRID), 1)
    row = jnp.where(lane == SCALAR_LANE + 1, overlap, energy_ref[...])
    row = jnp.where(lane == SCALAR_LANE + 2, spread, row)
    out_ref[...] = force_ref[...] + row


def final_kernel(
    got_ref, ahead_ref, drawn_ref, hot_ref,
    waves_ref, force_ref, energy_ref, ratio_ref, totals_ref,
):
    got = got_ref[...]
    by_band = jnp.sum(got.reshape(SHARES, BANDS, 128), axis=0)
    column = lambda i: slice(SCALAR_LANE + i, SCALAR_LANE + i + 1)
    norms = by_band[:, column(0)]
    energies = by_band[:, column(1)] / norms
    band = iota((BANDS, 1), 0)
    own = band == lax.axis_index(GROUP)
    energy = jnp.sum(jnp.where(own, energies, 0.0), axis=0, keepdims=True)
    norm = jnp.sum(jnp.where(own, norms, 0.0), axis=0, keepdims=True)
    part_norm = got[:, column(0)]
    part_energy = got[:, column(1)] / jnp.maximum(part_norm, 1e-30)
    shift = part_energy - energy
    spread = got[:, column(2)] + part_norm * shift * shift
    own_rows = iota((OWNERS, 1), 0) % BANDS == lax.axis_index(GROUP)
    squares = jnp.sum(jnp.where(own_rows, spread, 0.0), axis=0, keepdims=True)
    energy_ref[...] = energy
    ratio_ref[...] = squares / norm
    everything = jnp.sum(by_band, axis=0, keepdims=True)
    band_energy = jnp.sum(occupancy(band) * energies, axis=0, keepdims=True) / BANDS
    totals_ref[...] = jnp.concatenate(
        [everything[:, SCALAR_LANE + 3 : SCALAR_LANE + 10], band_energy], axis=1
    )
    for a in range(8):
        waves_ref[a] = (ahead_ref[a] + energy * drawn_ref[a]).astype(bf16)
    lane = iota((8, 128), 1)
    wanted = ((lane // CAP) % 3 == iota((8, 128), 0)) & (lane < SCALAR_LANE)
    split = jnp.where(wanted, everything, 0.0)
    high, rest = halves(split)
    middle, low = halves(rest)
    pieces = jnp.concatenate([high, middle, low, jnp.zeros_like(low)], axis=0).astype(bf16)
    placed = dot_nn(pieces, hot_ref[...])
    forces = placed[0:8] + placed[8:16] + placed[16:24]
    force_ref[...] = forces[:3]


VMEM = pl.BlockSpec(memory_space=pltpu.VMEM)
SMEM = pl.BlockSpec(memory_space=pltpu.SMEM)


def call(kernel, inputs, outputs, scratch=(), cost=2000000000, specs=None, room=40):
    if specs is None:
        specs = [SMEM if x.dtype == jnp.int32 else VMEM for x in inputs]
    shapes = [jax.ShapeDtypeStruct(*out) for out in outputs]
    return pl.pallas_call(
        kernel,
        out_shape=shapes,
        in_specs=specs,
        out_specs=[VMEM] * len(shapes),
        scratch_shapes=[pltpu.VMEM(*one) if isinstance(one, tuple) else one for one in scratch],
        compiler_params=pltpu.CompilerParams(vmem_limit_bytes=room * 1024 * 1024),
        cost_estimate=pl.CostEstimate(flops=cost, bytes_accessed=1000000, transcendentals=0),
    )(*inputs)


def exchange(block, axes):
    return lax.all_to_all(block, axes, split_axis=0, concat_axis=0, tiled=True)


def per_device(coeffs, v_local, atom_pos, atom_charge, near_list, live_count):
    cosines = cosine_table()
    table, turned = jnp.asarray(cosines, bf16), jnp.asarray(cosines.T, bf16)
    coeffs = coeffs[0]
    (own,) = call(
        pick_kernel,
        [near_list, live_count, atom_pos, atom_charge.reshape(1, ATOMS)],
        [((SHARES, 1, 128), bf16)],
        [
            pltpu.SMEM((CAP,), jnp.int32),
            pltpu.SMEM((1,), jnp.int32),
            ((3, ATOMS), f32),
            ((1, ATOMS), f32),
            pltpu.SemaphoreType.DMA((4,)),
        ],
        specs=[pl.BlockSpec(memory_space=pl.ANY)] * 4,
        room=60,
    )
    group = exchange(own, GROUP)
    (sections,) = call(
        section_kernel,
        [coeffs, table],
        [((SHARES, 80, GRID), bf16)],
        [((GRID, 8, GRID), f32)],
    )
    rows = jnp.broadcast_to(group.reshape(1, SHARES, 128), (SHARES, SHARES, 128))
    got = exchange(lax.dynamic_update_slice(sections, rows, (0, 64, 0)), "gvec")
    stats, hot, halved, drawn, local = call(
        stats_kernel,
        [near_list, live_count, coeffs, v_local],
        [
            ((1, 128), f32),
            ((128, ATOMS), bf16),
            ((8, GRID, GRID), f32),
            ((8, GRID, GRID), f32),
            ((8, GRID, GRID), f32),
        ],
        [((GRID, 8, GRID), f32)],
    )
    back, density, energy, slots, blocks = call(
        slab_kernel,
        [got, local, table, turned, stats],
        [
            ((SHARES, 64, GRID), bf16),
            ((8, GRID, GRID), f32),
            ((1, 128), f32),
            ((8, LIVE), f32),
            ((OWNERS, 128), f32),
        ],
        [
            ((4, GRID, LIVE), f32),
            ((4, GRID, LIVE), bf16),
            ((8, GRID, GRID), f32),
            ((SHARES, 64, GRID), f32),
        ],
    )
    returned = exchange(back, "gvec")
    (forces,) = call(
        force_kernel,
        [blocks, density, slots],
        [((OWNERS, 128), f32)],
        [
            ((8, GRID, GRID), bf16),
            ((4, 2, GRID, LIVE), bf16),
            ((4, GRID, LIVE), f32),
            ((4, GRID, LIVE), f32),
            ((4, 8, LIVE), f32),
            ((4, 8, LIVE), f32),
            ((8, LIVE), f32),
        ],
    )
    ahead, message = call(
        image_kernel,
        [returned, coeffs, table, turned, forces, energy, halved],
        [((8, GRID, GRID), f32), ((OWNERS, 128), f32)],
        [((GRID, 8, GRID), f32), ((8, GRID, GRID), f32)],
    )
    arrived = exchange(message.reshape(OWNERS, 1, 128), EVERY).reshape(OWNERS, 128)
    waves, atom_force, energies, ratio, totals = call(
        final_kernel,
        [arrived, ahead, drawn, hot],
        [
            ((8, GRID, GRID), bf16),
            ((3, ATOMS), f32),
            ((1, 1), f32),
            ((1, 1), f32),
            ((1, 8), f32),
        ],
    )
    return (waves[None], energies.reshape(1), ratio.reshape(1), atom_force, totals.reshape(8))


def solution(mesh):
    return jax.shard_map(
        per_device,
        mesh=mesh,
        in_specs=(
            P(("band", "dom"), "gvec", None, None),
            P(None, "gvec", None),
            P(None, ("band", "gvec", "dom")),
            P(("band", "gvec", "dom")),
            P(("band", "gvec", "dom")),
            P(("band", "gvec", "dom")),
        ),
        out_specs=(
            P(("band", "dom"), "gvec", None, None),
            P(("band", "dom")),
            P(("band", "dom")),
            P(None, ("band", "gvec", "dom")),
            P(),
        ),
        check_vma=False,
    )
```

```python
import jax
import jax.numpy as jnp
import numpy as np
from jax import lax
from jax.experimental import pallas as pl
from jax.experimental.pallas import tpu as pltpu
from jax.sharding import PartitionSpec as P

GRID = 128
CAP = 16
BANDS = 16
SHARES = 16
OWNERS = 256
LIVE = 1024
ATOMS = 1024
SIGMA_FRACTIONS = (1.0 / 32.0, 1.0 / 16.0, 1.0 / 8.0, 1.0 / 4.0)
KERNEL_WEIGHTS = (1.0, 0.5, 0.25, 0.125)
EXPONENTS = tuple(0.5 / (GRID * fraction) ** 2 for fraction in SIGMA_FRACTIONS)
FORCE_UNIT = 1.0 / 4096.0
STEP_SIZE = 0.5
WAVE_STEP = float(np.pi / GRID)
CELLS = float(GRID**3)
DEAD_MARK = 4096.0
SCALAR_LANE = 96
f32 = jnp.float32
bf16 = jnp.bfloat16
EVERY = ("gvec", "band", "dom")
GROUP = ("band", "dom")


def cosine_table():
    points = np.arange(GRID).astype(np.float32)
    angles = np.float32(np.pi) * (points[:, None] + np.float32(0.5)) * points[None, :]
    angles = (angles / np.float32(GRID)).astype(np.float32)
    scales = np.where(
        points == 0, np.sqrt(np.float32(1.0 / GRID)), np.sqrt(np.float32(2.0 / GRID))
    ).astype(np.float32)
    return np.cos(angles).astype(np.float32) * scales[None, :]


def dot_nn(a, b):
    return lax.dot_general(a, b, (((1,), (0,)), ((), ())), preferred_element_type=f32)


def dot_nt(a, b):
    return lax.dot_general(a, b, (((1,), (1,)), ((), ())), preferred_element_type=f32)


def iota(shape, dim):
    return lax.broadcasted_iota(jnp.int32, shape, dim)


def occupancy(band):
    return 2.0 / (1.0 + jnp.exp((band.astype(f32) - 0.5 * BANDS) / (0.125 * BANDS)))


def near_one_hot(near_ref):
    slot = iota((128, 128), 0) % CAP
    wanted = jnp.zeros((128, 128), jnp.int32)
    for s in range(CAP):
        wanted = jnp.where(slot == s, near_ref[s], wanted)
    lanes = iota((128, 128), 1)
    parts = [
        jnp.where(wanted == lanes + 128 * t, 1.0, 0.0).astype(bf16) for t in range(ATOMS // 128)
    ]
    return jnp.concatenate(parts, axis=1)


def halves(value):
    high = value.astype(bf16).astype(f32)
    return high, value - high


def pick_kernel(
    near_hbm, count_ref, pos_hbm, charge_hbm, out_ref, near_ref, pos_ref, charge_ref, sems
):
    moves = [
        pltpu.make_async_copy(near_hbm, near_ref, sems.at[0]),
        pltpu.make_async_copy(pos_hbm, pos_ref, sems.at[1]),
        pltpu.make_async_copy(charge_hbm, charge_ref, sems.at[2]),
    ]
    for move in moves:
        move.start()
    for move in moves:
        move.wait()
    one_hot = jnp.where(iota((ATOMS, CAP), 0) == near_ref[...], 1.0, 0.0).astype(bf16)
    high, low = halves(jnp.concatenate([pos_ref[...], charge_ref[...]], axis=0))
    both = jnp.concatenate([high, low], axis=0).astype(bf16)
    picked = dot_nn(both, one_hot).astype(bf16)
    lane = iota((8, 128), 1)
    spread = jnp.where(iota((CAP, 128), 1) % CAP == iota((CAP, 128), 0), 1.0, 0.0).astype(bf16)
    wide = dot_nn(picked, spread)
    row = jnp.sum(jnp.where(lane // CAP == iota((8, 128), 0), wide, 0.0), axis=0, keepdims=True)
    lane_row = iota((1, 128), 1)
    dead = (lane_row < CAP) & (lane_row >= count_ref[0])
    row = jnp.where(dead, DEAD_MARK, row)
    out_ref[...] = jnp.broadcast_to(row.astype(bf16)[None], out_ref.shape)


def section_kernel(coeffs_ref, table_ref, out_ref, wide_ref):
    table = table_ref[...]
    along_z = dot_nt(coeffs_ref[...].reshape(1024, GRID), table).astype(bf16)
    for a in range(8):
        wide_ref[:, a, :] = dot_nn(table, along_z[a * GRID : (a + 1) * GRID])
    out_ref[:, :64, :] = wide_ref[...].reshape(SHARES, 64, GRID).astype(bf16)
    out_ref[:, 64:, :] = jnp.zeros((SHARES, 16, GRID), bf16)


def stats_kernel(
    near_ref, count_ref, coeffs_ref, local_ref,
    out_ref, hot_ref, halved_ref, drawn_ref, turned_ref, wide_ref,
):
    first = lax.axis_index("gvec") * 8
    q_wave = iota((GRID, GRID), 0).astype(f32) * WAVE_STEP
    l_wave = iota((1, GRID), 1).astype(f32) * WAVE_STEP
    sums = [jnp.zeros((1, GRID), f32) for _ in range(7)]
    for a in range(8):
        a_wave = (first + a).astype(f32) * WAVE_STEP
        value = coeffs_ref[a].astype(f32)
        square = value * value
        scaled = square * q_wave
        flat = jnp.sum(square, axis=0, keepdims=True)
        once = jnp.sum(scaled, axis=0, keepdims=True)
        twice = jnp.sum(scaled * q_wave, axis=0, keepdims=True)
        terms = (
            flat,
            a_wave * a_wave * flat,
            twice,
            l_wave * l_wave * flat,
            a_wave * once,
            a_wave * l_wave * flat,
            l_wave * once,
        )
        sums = [total + term for total, term in zip(sums, terms)]
    lane = iota((1, GRID), 1)
    weight = occupancy(jnp.full((1, 1), lax.axis_index(GROUP), jnp.int32)) / CELLS
    row = jnp.where(lane == SCALAR_LANE, jnp.sum(sums[0]), 0.0)
    for i in range(1, 7):
        value = jnp.sum(sums[i], axis=1, keepdims=True) * weight
        row = jnp.where(lane == SCALAR_LANE + 2 + i, value, row)
    out_ref[...] = row
    plane_waves = wave_tables()
    for a in range(8):
        halved = STEP_SIZE / (1.0 + kinetic_of(plane_waves, a))
        halved_ref[a] = halved
        drawn_ref[a] = halved * coeffs_ref[a].astype(f32)
    wide_ref[...] = local_ref[...].astype(f32)
    for y in range(8):
        turned_ref[y] = wide_ref[:, y, :]
    alive = iota((128, ATOMS), 0) % CAP < count_ref[0]
    hot_ref[...] = jnp.where(alive, near_one_hot(near_ref), jnp.zeros((), bf16))


def gauss_values(offset):
    wide = jnp.exp(-EXPONENTS[3] * offset * offset)
    values = [wide]
    for _ in range(3):
        square = values[0] * values[0]
        values.insert(0, square * square)
    return values


def slot_place(blocks):
    lane = iota((OWNERS, 128), 1)
    live = jnp.where((blocks < 1000.0) & (lane < CAP), 1.0, 0.0).astype(bf16)
    return live


def slot_masks(live):
    counts = dot_nn(live, jnp.ones((128, 128), bf16))
    before = jnp.where(iota((OWNERS, OWNERS), 1) < iota((OWNERS, OWNERS), 0), 1.0, 0.0).astype(bf16)
    starts = dot_nn(before, counts.astype(bf16))
    ends = starts + counts
    lane = iota((OWNERS, 128), 1).astype(f32)
    tiles = []
    for t in range(LIVE // 128):
        here = lane + (128.0 * t)
        tiles.append(jnp.where((here >= starts) & (here < ends), 1.0, 0.0).astype(bf16))
    return jnp.concatenate(tiles, axis=1), starts


def choose(held, starts, rows):
    coarse = jnp.floor(starts * 0.125)
    fine = starts - 8.0 * coarse
    left = jnp.concatenate(rows + [coarse.T[:16], fine.T[:16]], axis=0).astype(bf16)
    moved = dot_nn(left, held)
    size = moved.shape[0] - 32
    own_start = 8.0 * moved[size : size + 1] + moved[size + 16 : size + 17]
    slot = iota((1, LIVE), 1).astype(f32) - own_start
    chosen = (iota((128, LIVE), 0) % CAP).astype(f32) == slot
    return chosen, moved


def potential_kernel(
    got_ref, potential_ref, slots_ref, blocks_ref, gx_ref, depth_ref
):
    blocks = got_ref[:, 64:, :].astype(f32).reshape(OWNERS, 128)
    blocks_ref[...] = blocks
    held, starts = slot_masks(slot_place(blocks))
    chosen, moved = choose(held, starts, [blocks.T])
    pick = jnp.where(iota((8, 128), 1) // CAP == iota((8, 128), 0), 1.0, 0.0).astype(bf16)
    slots = dot_nn(pick, jnp.where(chosen, moved[:128], 0.0).astype(bf16))
    slots = slots[:4] + slots[4:]
    slots_ref[...] = jnp.concatenate([slots, slots], axis=0)
    points = iota((GRID, LIVE), 0).astype(f32)
    y_points = (lax.axis_index("gvec") * 8 + iota((8, LIVE), 0)).astype(f32)
    gx_values = gauss_values(points - slots[0:1])
    gy_values = gauss_values(y_points - slots[1:2])
    gz_values = gauss_values(points - slots[2:3])
    for k in range(4):
        gx_ref[k] = gx_values[k]
        depth_ref[k] = (gz_values[k] * (slots[3:4] * KERNEL_WEIGHTS[k])).astype(bf16)
    for k in range(4):
        plane = jnp.concatenate(
            [(gx_ref[k] * gy_values[k][y : y + 1]).astype(bf16) for y in range(8)], axis=0
        )
        part = dot_nt(plane, depth_ref[k]).reshape(8, GRID, GRID)
        potential_ref[...] = part if k == 0 else potential_ref[...] + part


def field_kernel(
    got_ref, local_ref, table_ref, turned_ref, potential_ref, stats_ref,
    back_ref, density_ref, energy_ref, back_wide,
):
    table = table_ref[...]
    got = got_ref[:, :64, :].astype(f32)
    turned = turned_ref[...]
    weight = occupancy(jnp.full((1, 1), lax.axis_index(GROUP), jnp.int32))
    energy = jnp.zeros((1, GRID), f32)
    for y in range(8):
        potential = potential_ref[y]
        mine = got[:, y * 8 : (y + 1) * 8, :].reshape(GRID, GRID).astype(bf16)
        real = dot_nn(table, mine).astype(bf16).astype(f32)
        density = weight * real * real
        density_ref[y] = density
        energy = energy + jnp.sum(density * potential, axis=0, keepdims=True)
        field = local_ref[y] + potential.astype(bf16).astype(f32)
        applied = (field * real).astype(bf16)
        back = dot_nn(turned, applied)
        back_wide[:, y * 8 : (y + 1) * 8, :] = back.reshape(SHARES, 8, GRID)
    back_ref[...] = back_wide[...].astype(bf16)
    total = jnp.sum(energy, axis=1, keepdims=True) / CELLS
    lane = iota((1, GRID), 1)
    energy_ref[...] = stats_ref[...] + jnp.where(lane == SCALAR_LANE + 9, total, 0.0)


def force_kernel(
    blocks_ref, density_ref, slots_ref, out_ref,
    turned_ref, x_ref, gz_ref, hz_ref, gy_ref, hy_ref, sum_ref,
):
    for y in range(8):
        turned_ref[y] = density_ref[y].T.astype(bf16)
    slots = slots_ref[...]
    points = iota((GRID, LIVE), 0).astype(f32)
    x_offset = points - slots[0:1]
    y_offset = (lax.axis_index("gvec") * 8 + iota((8, LIVE), 0)).astype(f32) - slots[1:2]
    z_offset = points - slots[2:3]
    gx_values = gauss_values(x_offset)
    gy_values = gauss_values(y_offset)
    gz_values = gauss_values(z_offset)
    for k in range(4):
        slope = 2.0 * EXPONENTS[k]
        x_ref[k, 0] = gx_values[k].astype(bf16)
        x_ref[k, 1] = (slope * x_offset * gx_values[k]).astype(bf16)
        gy_ref[k] = gy_values[k]
        hy_ref[k] = slope * y_offset * gy_values[k]
        scale = KERNEL_WEIGHTS[k] * slots[3:4]
        gz_ref[k] = gz_values[k] * scale
        hz_ref[k] = slope * z_offset * gz_values[k] * scale

    for chunk in range(LIVE // 128):
        lanes = pl.ds(chunk * 128, 128)
        force_x = jnp.zeros((1, 128), f32)
        force_y = jnp.zeros((1, 128), f32)
        force_z = jnp.zeros((1, 128), f32)
        for k in range(4):
            both = jnp.concatenate([x_ref[k, 0, :, lanes], x_ref[k, 1, :, lanes]], axis=1)
            value_y = gy_ref[k, :, lanes]
            slope_y = hy_ref[k, :, lanes]
            with_x = jnp.zeros((GRID, 128), f32)
            with_y = jnp.zeros((GRID, 128), f32)
            with_z = jnp.zeros((GRID, 128), f32)
            for y in range(8):
                part = dot_nn(turned_ref[y], both)
                with_x = with_x + part[:, 128:] * value_y[y : y + 1]
                with_y = with_y + part[:, :128] * slope_y[y : y + 1]
                with_z = with_z + part[:, :128] * value_y[y : y + 1]
            value_z = gz_ref[k, :, lanes]
            force_x = force_x + jnp.sum(with_x * value_z, axis=0, keepdims=True)
            force_y = force_y + jnp.sum(with_y * value_z, axis=0, keepdims=True)
            force_z = force_z + jnp.sum(with_z * hz_ref[k, :, lanes], axis=0, keepdims=True)
        sum_ref[0:1, lanes] = force_x
        sum_ref[1:2, lanes] = force_y
        sum_ref[2:3, lanes] = force_z

    forces = sum_ref[0:3, :] * -FORCE_UNIT
    high, low = halves(forces)
    stacked = jnp.concatenate(
        [jnp.broadcast_to(part[c : c + 1], (CAP, LIVE)) for part in (high, low) for c in range(3)]
        + [jnp.zeros((128 - 6 * CAP, LIVE), f32)],
        axis=0,
    )
    held, starts = slot_masks(slot_place(blocks_ref[...]))
    chosen, _ = choose(held, starts, [])
    per_slot = jnp.where(chosen, stacked, 0.0).astype(bf16)
    out_ref[...] = dot_nt(per_slot, held).T


def wave_tables():
    q_wave = iota((GRID, GRID), 0).astype(f32) * WAVE_STEP
    l_wave = iota((GRID, GRID), 1).astype(f32) * WAVE_STEP
    return q_wave * q_wave + l_wave * l_wave


def kinetic_of(plane_waves, a):
    a_wave = (lax.axis_index("gvec") * 8 + a).astype(f32) * WAVE_STEP
    return 0.5 * (a_wave * a_wave + plane_waves)


def image_kernel(
    got_ref, coeffs_ref, table_ref, turned_ref, force_ref, energy_ref, halved_ref,
    ahead_ref, out_ref, wide_ref, image_ref,
):
    table = table_ref[...]
    turned = turned_ref[...]
    wide_ref[...] = got_ref[...].astype(f32).reshape(GRID, 8, GRID)
    plane_waves = wave_tables()
    overlap = jnp.zeros((1, GRID), f32)
    norm = jnp.zeros((1, GRID), f32)
    for a in range(8):
        along_y = dot_nn(turned, wide_ref[:, a, :].astype(bf16)).astype(bf16)
        coeff = coeffs_ref[a].astype(f32)
        image = kinetic_of(plane_waves, a) * coeff + dot_nn(along_y, table)
        image_ref[a] = image
        ahead_ref[a] = coeff - halved_ref[a] * image
        overlap = overlap + jnp.sum(coeff * image, axis=0, keepdims=True)
        norm = norm + jnp.sum(coeff * coeff, axis=0, keepdims=True)
    overlap = jnp.sum(overlap, axis=1, keepdims=True)
    norm = jnp.sum(norm, axis=1, keepdims=True)
    mean = overlap / jnp.maximum(norm, 1e-30)
    spread = jnp.zeros((1, GRID), f32)
    for a in range(8):
        residual = image_ref[a] - mean * coeffs_ref[a].astype(f32)
        spread = spread + jnp.sum(residual * residual, axis=0, keepdims=True)
    spread = jnp.sum(spread, axis=1, keepdims=True)
    lane = iota((1, GRID), 1)
    row = jnp.where(lane == SCALAR_LANE + 1, overlap, energy_ref[...])
    row = jnp.where(lane == SCALAR_LANE + 2, spread, row)
    out_ref[...] = force_ref[...] + row


def final_kernel(
    got_ref, ahead_ref, drawn_ref, hot_ref,
    waves_ref, force_ref, energy_ref, ratio_ref, totals_ref,
):
    got = got_ref[...]
    by_band = jnp.sum(got.reshape(SHARES, BANDS, 128), axis=0)
    column = lambda i: slice(SCALAR_LANE + i, SCALAR_LANE + i + 1)
    norms = by_band[:, column(0)]
    energies = by_band[:, column(1)] / norms
    band = iota((BANDS, 1), 0)
    own = band == lax.axis_index(GROUP)
    energy = jnp.sum(jnp.where(own, energies, 0.0), axis=0, keepdims=True)
    norm = jnp.sum(jnp.where(own, norms, 0.0), axis=0, keepdims=True)
    part_norm = got[:, column(0)]
    part_energy = got[:, column(1)] / jnp.maximum(part_norm, 1e-30)
    shift = part_energy - energy
    spread = got[:, column(2)] + part_norm * shift * shift
    own_rows = iota((OWNERS, 1), 0) % BANDS == lax.axis_index(GROUP)
    squares = jnp.sum(jnp.where(own_rows, spread, 0.0), axis=0, keepdims=True)
    energy_ref[...] = energy
    ratio_ref[...] = squares / norm
    everything = jnp.sum(by_band, axis=0, keepdims=True)
    band_energy = jnp.sum(occupancy(band) * energies, axis=0, keepdims=True) / BANDS
    totals_ref[...] = jnp.concatenate(
        [everything[:, SCALAR_LANE + 3 : SCALAR_LANE + 10], band_energy], axis=1
    )
    for a in range(8):
        waves_ref[a] = (ahead_ref[a] + energy * drawn_ref[a]).astype(bf16)
    lane = iota((8, 128), 1)
    wanted = ((lane // CAP) % 3 == iota((8, 128), 0)) & (lane < SCALAR_LANE)
    split = jnp.where(wanted, everything, 0.0)
    high, rest = halves(split)
    middle, low = halves(rest)
    pieces = jnp.concatenate([high, middle, low, jnp.zeros_like(low)], axis=0).astype(bf16)
    placed = dot_nn(pieces, hot_ref[...])
    forces = placed[0:8] + placed[8:16] + placed[16:24]
    force_ref[...] = forces[:3]


VMEM = pl.BlockSpec(memory_space=pltpu.VMEM)
SMEM = pl.BlockSpec(memory_space=pltpu.SMEM)


def call(kernel, inputs, outputs, scratch=(), cost=2000000000, specs=None, room=40):
    if specs is None:
        specs = [SMEM if x.dtype == jnp.int32 else VMEM for x in inputs]
    shapes = [jax.ShapeDtypeStruct(*out) for out in outputs]
    return pl.pallas_call(
        kernel,
        out_shape=shapes,
        in_specs=specs,
        out_specs=[VMEM] * len(shapes),
        scratch_shapes=[pltpu.VMEM(*one) if isinstance(one, tuple) else one for one in scratch],
        compiler_params=pltpu.CompilerParams(vmem_limit_bytes=room * 1024 * 1024),
        cost_estimate=pl.CostEstimate(flops=cost, bytes_accessed=1000000, transcendentals=0),
    )(*inputs)


def exchange(block, axes):
    return lax.all_to_all(block, axes, split_axis=0, concat_axis=0, tiled=True)


def per_device(coeffs, v_local, atom_pos, atom_charge, near_list, live_count):
    cosines = cosine_table()
    table, turned = jnp.asarray(cosines, bf16), jnp.asarray(cosines.T, bf16)
    coeffs = coeffs[0]
    (own,) = call(
        pick_kernel,
        [near_list.reshape(1, CAP), live_count, atom_pos, atom_charge.reshape(1, ATOMS)],
        [((SHARES, 1, 128), bf16)],
        [
            ((1, CAP), jnp.int32),
            ((3, ATOMS), f32),
            ((1, ATOMS), f32),
            pltpu.SemaphoreType.DMA((3,)),
        ],
        specs=[
            pl.BlockSpec(memory_space=pl.ANY),
            SMEM,
            pl.BlockSpec(memory_space=pl.ANY),
            pl.BlockSpec(memory_space=pl.ANY),
        ],
        room=60,
    )
    group = exchange(own, GROUP)
    (sections,) = call(
        section_kernel,
        [coeffs, table],
        [((SHARES, 80, GRID), bf16)],
        [((GRID, 8, GRID), f32)],
    )
    rows = jnp.broadcast_to(group.reshape(1, SHARES, 128), (SHARES, SHARES, 128))
    got = exchange(lax.dynamic_update_slice(sections, rows, (0, 64, 0)), "gvec")
    stats, hot, halved, drawn, local = call(
        stats_kernel,
        [near_list, live_count, coeffs, v_local],
        [
            ((1, 128), f32),
            ((128, ATOMS), bf16),
            ((8, GRID, GRID), f32),
            ((8, GRID, GRID), f32),
            ((8, GRID, GRID), f32),
        ],
        [((GRID, 8, GRID), f32)],
    )
    potential, slots, blocks = call(
        potential_kernel,
        [got],
        [((8, GRID, GRID), f32), ((8, LIVE), f32), ((OWNERS, 128), f32)],
        [((4, GRID, LIVE), f32), ((4, GRID, LIVE), bf16)],
    )
    back, density, energy = call(
        field_kernel,
        [got, local, table, turned, potential, stats],
        [
            ((SHARES, 64, GRID), bf16),
            ((8, GRID, GRID), f32),
            ((1, 128), f32),
        ],
        [((SHARES, 64, GRID), f32)],
    )
    returned = exchange(back, "gvec")
    (forces,) = call(
        force_kernel,
        [blocks, density, slots],
        [((OWNERS, 128), f32)],
        [
            ((8, GRID, GRID), bf16),
            ((4, 2, GRID, LIVE), bf16),
            ((4, GRID, LIVE), f32),
            ((4, GRID, LIVE), f32),
            ((4, 8, LIVE), f32),
            ((4, 8, LIVE), f32),
            ((8, LIVE), f32),
        ],
    )
    ahead, message = call(
        image_kernel,
        [returned, coeffs, table, turned, forces, energy, halved],
        [((8, GRID, GRID), f32), ((OWNERS, 128), f32)],
        [((GRID, 8, GRID), f32), ((8, GRID, GRID), f32)],
    )
    arrived = exchange(message.reshape(OWNERS, 1, 128), EVERY).reshape(OWNERS, 128)
    waves, atom_force, energies, ratio, totals = call(
        final_kernel,
        [arrived, ahead, drawn, hot],
        [
            ((8, GRID, GRID), bf16),
            ((3, ATOMS), f32),
            ((1, 1), f32),
            ((1, 1), f32),
            ((1, 8), f32),
        ],
    )
    return (waves[None], energies.reshape(1), ratio.reshape(1), atom_force, totals.reshape(8))


def solution(mesh):
    return jax.shard_map(
        per_device,
        mesh=mesh,
        in_specs=(
            P(("band", "dom"), "gvec", None, None),
            P(None, "gvec", None),
            P(None, ("band", "gvec", "dom")),
            P(("band", "gvec", "dom")),
            P(("band", "gvec", "dom")),
            P(("band", "gvec", "dom")),
        ),
        out_specs=(
            P(("band", "dom"), "gvec", None, None),
            P(("band", "dom")),
            P(("band", "dom")),
            P(None, ("band", "gvec", "dom")),
            P(),
        ),
        check_vma=False,
    )
```

```python
import jax
import jax.numpy as jnp
import numpy as np
from jax import lax
from jax.experimental import pallas as pl
from jax.experimental.pallas import tpu as pltpu
from jax.sharding import PartitionSpec as P

GRID = 128
CAP = 16
BANDS = 16
SHARES = 16
OWNERS = 256
LIVE = 1024
ATOMS = 1024
SIGMA_FRACTIONS = (1.0 / 32.0, 1.0 / 16.0, 1.0 / 8.0, 1.0 / 4.0)
KERNEL_WEIGHTS = (1.0, 0.5, 0.25, 0.125)
EXPONENTS = tuple(0.5 / (GRID * fraction) ** 2 for fraction in SIGMA_FRACTIONS)
FORCE_UNIT = 1.0 / 4096.0
STEP_SIZE = 0.5
WAVE_STEP = float(np.pi / GRID)
CELLS = float(GRID**3)
DEAD_MARK = 4096.0
SCALAR_LANE = 96
f32 = jnp.float32
bf16 = jnp.bfloat16
EVERY = ("gvec", "band", "dom")
GROUP = ("band", "dom")


def cosine_table():
    points = np.arange(GRID).astype(np.float32)
    angles = np.float32(np.pi) * (points[:, None] + np.float32(0.5)) * points[None, :]
    angles = (angles / np.float32(GRID)).astype(np.float32)
    scales = np.where(
        points == 0, np.sqrt(np.float32(1.0 / GRID)), np.sqrt(np.float32(2.0 / GRID))
    ).astype(np.float32)
    return np.cos(angles).astype(np.float32) * scales[None, :]


def dot_nn(a, b):
    return lax.dot_general(a, b, (((1,), (0,)), ((), ())), preferred_element_type=f32)


def dot_nt(a, b):
    return lax.dot_general(a, b, (((1,), (1,)), ((), ())), preferred_element_type=f32)


def iota(shape, dim):
    return lax.broadcasted_iota(jnp.int32, shape, dim)


def occupancy(band):
    return 2.0 / (1.0 + jnp.exp((band.astype(f32) - 0.5 * BANDS) / (0.125 * BANDS)))


def near_one_hot(near_ref):
    slot = iota((128, 128), 0) % CAP
    wanted = jnp.zeros((128, 128), jnp.int32)
    for s in range(CAP):
        wanted = jnp.where(slot == s, near_ref[s], wanted)
    lanes = iota((128, 128), 1)
    parts = [
        jnp.where(wanted == lanes + 128 * t, 1.0, 0.0).astype(bf16) for t in range(ATOMS // 128)
    ]
    return jnp.concatenate(parts, axis=1)


def halves(value):
    high = value.astype(bf16).astype(f32)
    return high, value - high


def pick_kernel(
    near_hbm, count_ref, pos_hbm, charge_hbm, out_ref, near_ref, pos_ref, charge_ref, sems
):
    moves = [
        pltpu.make_async_copy(near_hbm, near_ref, sems.at[0]),
        pltpu.make_async_copy(pos_hbm, pos_ref, sems.at[1]),
        pltpu.make_async_copy(charge_hbm, charge_ref, sems.at[2]),
    ]
    for move in moves:
        move.start()
    for move in moves:
        move.wait()
    one_hot = jnp.where(iota((ATOMS, CAP), 0) == near_ref[...], 1.0, 0.0).astype(bf16)
    high, low = halves(jnp.concatenate([pos_ref[...], charge_ref[...]], axis=0))
    both = jnp.concatenate([high, low], axis=0).astype(bf16)
    picked = dot_nn(both, one_hot).astype(bf16)
    lane = iota((8, 128), 1)
    spread = jnp.where(iota((CAP, 128), 1) % CAP == iota((CAP, 128), 0), 1.0, 0.0).astype(bf16)
    wide = dot_nn(picked, spread)
    row = jnp.sum(jnp.where(lane // CAP == iota((8, 128), 0), wide, 0.0), axis=0, keepdims=True)
    lane_row = iota((1, 128), 1)
    dead = (lane_row < CAP) & (lane_row >= count_ref[0])
    row = jnp.where(dead, DEAD_MARK, row)
    out_ref[...] = jnp.broadcast_to(row.astype(bf16)[None], out_ref.shape)


def section_kernel(coeffs_ref, table_ref, out_ref, wide_ref):
    table = table_ref[...]
    along_z = dot_nt(coeffs_ref[...].reshape(1024, GRID), table).astype(bf16)
    for a in range(8):
        wide_ref[:, a, :] = dot_nn(table, along_z[a * GRID : (a + 1) * GRID])
    out_ref[...] = wide_ref[...].reshape(SHARES, 64, GRID).astype(bf16)


def attach_kernel(sections_ref, group_ref, out_ref):
    out_ref[:, :64, :] = sections_ref[...]
    out_ref[:, 64:, :] = jnp.broadcast_to(group_ref[...][None], (SHARES, 16, 128))


def stats_kernel(
    near_ref, count_ref, coeffs_ref, local_ref,
    out_ref, hot_ref, halved_ref, drawn_ref, turned_ref, wide_ref,
):
    first = lax.axis_index("gvec") * 8
    q_wave = iota((GRID, GRID), 0).astype(f32) * WAVE_STEP
    l_wave = iota((1, GRID), 1).astype(f32) * WAVE_STEP
    sums = [jnp.zeros((1, GRID), f32) for _ in range(7)]
    for a in range(8):
        a_wave = (first + a).astype(f32) * WAVE_STEP
        value = coeffs_ref[a].astype(f32)
        square = value * value
        scaled = square * q_wave
        flat = jnp.sum(square, axis=0, keepdims=True)
        once = jnp.sum(scaled, axis=0, keepdims=True)
        twice = jnp.sum(scaled * q_wave, axis=0, keepdims=True)
        terms = (
            flat,
            a_wave * a_wave * flat,
            twice,
            l_wave * l_wave * flat,
            a_wave * once,
            a_wave * l_wave * flat,
            l_wave * once,
        )
        sums = [total + term for total, term in zip(sums, terms)]
    lane = iota((1, GRID), 1)
    weight = occupancy(jnp.full((1, 1), lax.axis_index(GROUP), jnp.int32)) / CELLS
    row = jnp.where(lane == SCALAR_LANE, jnp.sum(sums[0]), 0.0)
    for i in range(1, 7):
        value = jnp.sum(sums[i], axis=1, keepdims=True) * weight
        row = jnp.where(lane == SCALAR_LANE + 2 + i, value, row)
    out_ref[...] = row
    plane_waves = wave_tables()
    for a in range(8):
        halved = STEP_SIZE / (1.0 + kinetic_of(plane_waves, a))
        halved_ref[a] = halved
        drawn_ref[a] = halved * coeffs_ref[a].astype(f32)
    wide_ref[...] = local_ref[...].astype(f32)
    for y in range(8):
        turned_ref[y] = wide_ref[:, y, :]
    alive = iota((128, ATOMS), 0) % CAP < count_ref[0]
    hot_ref[...] = jnp.where(alive, near_one_hot(near_ref), jnp.zeros((), bf16))


def gauss_values(offset):
    wide = jnp.exp(-EXPONENTS[3] * offset * offset)
    values = [wide]
    for _ in range(3):
        square = values[0] * values[0]
        values.insert(0, square * square)
    return values


def slot_place(blocks):
    lane = iota((OWNERS, 128), 1)
    live = jnp.where((blocks < 1000.0) & (lane < CAP), 1.0, 0.0).astype(bf16)
    return live


def slot_masks(live):
    counts = dot_nn(live, jnp.ones((128, 128), bf16))
    before = jnp.where(iota((OWNERS, OWNERS), 1) < iota((OWNERS, OWNERS), 0), 1.0, 0.0).astype(bf16)
    starts = dot_nn(before, counts.astype(bf16))
    ends = starts + counts
    lane = iota((OWNERS, 128), 1).astype(f32)
    tiles = []
    for t in range(LIVE // 128):
        here = lane + (128.0 * t)
        tiles.append(jnp.where((here >= starts) & (here < ends), 1.0, 0.0).astype(bf16))
    return jnp.concatenate(tiles, axis=1), starts


def choose(held, starts, rows):
    coarse = jnp.floor(starts * 0.125)
    fine = starts - 8.0 * coarse
    left = jnp.concatenate(rows + [coarse.T[:16], fine.T[:16]], axis=0).astype(bf16)
    moved = dot_nn(left, held)
    size = moved.shape[0] - 32
    own_start = 8.0 * moved[size : size + 1] + moved[size + 16 : size + 17]
    slot = iota((1, LIVE), 1).astype(f32) - own_start
    chosen = (iota((128, LIVE), 0) % CAP).astype(f32) == slot
    return chosen, moved


def potential_kernel(
    got_ref, potential_ref, slots_ref, blocks_ref, gx_ref, depth_ref
):
    blocks = got_ref[:, 64:, :].astype(f32).reshape(OWNERS, 128)
    blocks_ref[...] = blocks
    held, starts = slot_masks(slot_place(blocks))
    chosen, moved = choose(held, starts, [blocks.T])
    pick = jnp.where(iota((8, 128), 1) // CAP == iota((8, 128), 0), 1.0, 0.0).astype(bf16)
    slots = dot_nn(pick, jnp.where(chosen, moved[:128], 0.0).astype(bf16))
    slots = slots[:4] + slots[4:]
    slots_ref[...] = jnp.concatenate([slots, slots], axis=0)
    points = iota((GRID, LIVE), 0).astype(f32)
    y_points = (lax.axis_index("gvec") * 8 + iota((8, LIVE), 0)).astype(f32)
    gx_values = gauss_values(points - slots[0:1])
    gy_values = gauss_values(y_points - slots[1:2])
    gz_values = gauss_values(points - slots[2:3])
    for k in range(4):
        gx_ref[k] = gx_values[k]
        depth_ref[k] = (gz_values[k] * (slots[3:4] * KERNEL_WEIGHTS[k])).astype(bf16)
    for k in range(4):
        plane = jnp.concatenate(
            [(gx_ref[k] * gy_values[k][y : y + 1]).astype(bf16) for y in range(8)], axis=0
        )
        part = dot_nt(plane, depth_ref[k]).reshape(8, GRID, GRID)
        potential_ref[...] = part if k == 0 else potential_ref[...] + part


def field_kernel(
    got_ref, local_ref, table_ref, turned_ref, potential_ref, stats_ref,
    back_ref, density_ref, energy_ref, back_wide,
):
    table = table_ref[...]
    got = got_ref[:, :64, :].astype(f32)
    turned = turned_ref[...]
    weight = occupancy(jnp.full((1, 1), lax.axis_index(GROUP), jnp.int32))
    energy = jnp.zeros((1, GRID), f32)
    for y in range(8):
        potential = potential_ref[y]
        mine = got[:, y * 8 : (y + 1) * 8, :].reshape(GRID, GRID).astype(bf16)
        real = dot_nn(table, mine).astype(bf16).astype(f32)
        density = weight * real * real
        density_ref[y] = density
        energy = energy + jnp.sum(density * potential, axis=0, keepdims=True)
        field = local_ref[y] + potential.astype(bf16).astype(f32)
        applied = (field * real).astype(bf16)
        back = dot_nn(turned, applied)
        back_wide[:, y * 8 : (y + 1) * 8, :] = back.reshape(SHARES, 8, GRID)
    back_ref[...] = back_wide[...].astype(bf16)
    total = jnp.sum(energy, axis=1, keepdims=True) / CELLS
    lane = iota((1, GRID), 1)
    energy_ref[...] = stats_ref[...] + jnp.where(lane == SCALAR_LANE + 9, total, 0.0)


def force_kernel(
    blocks_ref, density_ref, slots_ref, out_ref,
    turned_ref, x_ref, gz_ref, hz_ref, gy_ref, hy_ref, sum_ref,
):
    for y in range(8):
        turned_ref[y] = density_ref[y].T.astype(bf16)
    slots = slots_ref[...]
    points = iota((GRID, LIVE), 0).astype(f32)
    x_offset = points - slots[0:1]
    y_offset = (lax.axis_index("gvec") * 8 + iota((8, LIVE), 0)).astype(f32) - slots[1:2]
    z_offset = points - slots[2:3]
    gx_values = gauss_values(x_offset)
    gy_values = gauss_values(y_offset)
    gz_values = gauss_values(z_offset)
    for k in range(4):
        slope = 2.0 * EXPONENTS[k]
        x_ref[k, 0] = gx_values[k].astype(bf16)
        x_ref[k, 1] = (slope * x_offset * gx_values[k]).astype(bf16)
        gy_ref[k] = gy_values[k]
        hy_ref[k] = slope * y_offset * gy_values[k]
        scale = KERNEL_WEIGHTS[k] * slots[3:4]
        gz_ref[k] = gz_values[k] * scale
        hz_ref[k] = slope * z_offset * gz_values[k] * scale

    for chunk in range(LIVE // 128):
        lanes = pl.ds(chunk * 128, 128)
        force_x = jnp.zeros((1, 128), f32)
        force_y = jnp.zeros((1, 128), f32)
        force_z = jnp.zeros((1, 128), f32)
        for k in range(4):
            both = jnp.concatenate([x_ref[k, 0, :, lanes], x_ref[k, 1, :, lanes]], axis=1)
            value_y = gy_ref[k, :, lanes]
            slope_y = hy_ref[k, :, lanes]
            with_x = jnp.zeros((GRID, 128), f32)
            with_y = jnp.zeros((GRID, 128), f32)
            with_z = jnp.zeros((GRID, 128), f32)
            for y in range(8):
                part = dot_nn(turned_ref[y], both)
                with_x = with_x + part[:, 128:] * value_y[y : y + 1]
                with_y = with_y + part[:, :128] * slope_y[y : y + 1]
                with_z = with_z + part[:, :128] * value_y[y : y + 1]
            value_z = gz_ref[k, :, lanes]
            force_x = force_x + jnp.sum(with_x * value_z, axis=0, keepdims=True)
            force_y = force_y + jnp.sum(with_y * value_z, axis=0, keepdims=True)
            force_z = force_z + jnp.sum(with_z * hz_ref[k, :, lanes], axis=0, keepdims=True)
        sum_ref[0:1, lanes] = force_x
        sum_ref[1:2, lanes] = force_y
        sum_ref[2:3, lanes] = force_z

    forces = sum_ref[0:3, :] * -FORCE_UNIT
    high, low = halves(forces)
    stacked = jnp.concatenate(
        [jnp.broadcast_to(part[c : c + 1], (CAP, LIVE)) for part in (high, low) for c in range(3)]
        + [jnp.zeros((128 - 6 * CAP, LIVE), f32)],
        axis=0,
    )
    held, starts = slot_masks(slot_place(blocks_ref[...]))
    chosen, _ = choose(held, starts, [])
    per_slot = jnp.where(chosen, stacked, 0.0).astype(bf16)
    out_ref[...] = dot_nt(per_slot, held).T


def wave_tables():
    q_wave = iota((GRID, GRID), 0).astype(f32) * WAVE_STEP
    l_wave = iota((GRID, GRID), 1).astype(f32) * WAVE_STEP
    return q_wave * q_wave + l_wave * l_wave


def kinetic_of(plane_waves, a):
    a_wave = (lax.axis_index("gvec") * 8 + a).astype(f32) * WAVE_STEP
    return 0.5 * (a_wave * a_wave + plane_waves)


def image_kernel(
    got_ref, coeffs_ref, table_ref, turned_ref, force_ref, energy_ref, halved_ref,
    ahead_ref, out_ref, wide_ref, image_ref,
):
    table = table_ref[...]
    turned = turned_ref[...]
    wide_ref[...] = got_ref[...].astype(f32).reshape(GRID, 8, GRID)
    plane_waves = wave_tables()
    overlap = jnp.zeros((1, GRID), f32)
    norm = jnp.zeros((1, GRID), f32)
    for a in range(8):
        along_y = dot_nn(turned, wide_ref[:, a, :].astype(bf16)).astype(bf16)
        coeff = coeffs_ref[a].astype(f32)
        image = kinetic_of(plane_waves, a) * coeff + dot_nn(along_y, table)
        image_ref[a] = image
        ahead_ref[a] = coeff - halved_ref[a] * image
        overlap = overlap + jnp.sum(coeff * image, axis=0, keepdims=True)
        norm = norm + jnp.sum(coeff * coeff, axis=0, keepdims=True)
    overlap = jnp.sum(overlap, axis=1, keepdims=True)
    norm = jnp.sum(norm, axis=1, keepdims=True)
    mean = overlap / jnp.maximum(norm, 1e-30)
    spread = jnp.zeros((1, GRID), f32)
    for a in range(8):
        residual = image_ref[a] - mean * coeffs_ref[a].astype(f32)
        spread = spread + jnp.sum(residual * residual, axis=0, keepdims=True)
    spread = jnp.sum(spread, axis=1, keepdims=True)
    lane = iota((1, GRID), 1)
    row = jnp.where(lane == SCALAR_LANE + 1, overlap, energy_ref[...])
    row = jnp.where(lane == SCALAR_LANE + 2, spread, row)
    out_ref[...] = force_ref[...] + row


def final_kernel(
    got_ref, ahead_ref, drawn_ref, hot_ref,
    waves_ref, force_ref, energy_ref, ratio_ref, totals_ref,
):
    got = got_ref[...]
    by_band = jnp.sum(got.reshape(SHARES, BANDS, 128), axis=0)
    column = lambda i: slice(SCALAR_LANE + i, SCALAR_LANE + i + 1)
    norms = by_band[:, column(0)]
    energies = by_band[:, column(1)] / norms
    band = iota((BANDS, 1), 0)
    own = band == lax.axis_index(GROUP)
    energy = jnp.sum(jnp.where(own, energies, 0.0), axis=0, keepdims=True)
    norm = jnp.sum(jnp.where(own, norms, 0.0), axis=0, keepdims=True)
    part_norm = got[:, column(0)]
    part_energy = got[:, column(1)] / jnp.maximum(part_norm, 1e-30)
    shift = part_energy - energy
    spread = got[:, column(2)] + part_norm * shift * shift
    own_rows = iota((OWNERS, 1), 0) % BANDS == lax.axis_index(GROUP)
    squares = jnp.sum(jnp.where(own_rows, spread, 0.0), axis=0, keepdims=True)
    energy_ref[...] = energy
    ratio_ref[...] = squares / norm
    everything = jnp.sum(by_band, axis=0, keepdims=True)
    band_energy = jnp.sum(occupancy(band) * energies, axis=0, keepdims=True) / BANDS
    totals_ref[...] = jnp.concatenate(
        [everything[:, SCALAR_LANE + 3 : SCALAR_LANE + 10], band_energy], axis=1
    )
    for a in range(8):
        waves_ref[a] = (ahead_ref[a] + energy * drawn_ref[a]).astype(bf16)
    lane = iota((8, 128), 1)
    wanted = ((lane // CAP) % 3 == iota((8, 128), 0)) & (lane < SCALAR_LANE)
    split = jnp.where(wanted, everything, 0.0)
    high, rest = halves(split)
    middle, low = halves(rest)
    pieces = jnp.concatenate([high, middle, low, jnp.zeros_like(low)], axis=0).astype(bf16)
    placed = dot_nn(pieces, hot_ref[...])
    forces = placed[0:8] + placed[8:16] + placed[16:24]
    force_ref[...] = forces[:3]


VMEM = pl.BlockSpec(memory_space=pltpu.VMEM)
SMEM = pl.BlockSpec(memory_space=pltpu.SMEM)


def call(kernel, inputs, outputs, scratch=(), cost=2000000000, specs=None, room=40):
    if specs is None:
        specs = [SMEM if x.dtype == jnp.int32 else VMEM for x in inputs]
    shapes = [jax.ShapeDtypeStruct(*out) for out in outputs]
    return pl.pallas_call(
        kernel,
        out_shape=shapes,
        in_specs=specs,
        out_specs=[VMEM] * len(shapes),
        scratch_shapes=[pltpu.VMEM(*one) if isinstance(one, tuple) else one for one in scratch],
        compiler_params=pltpu.CompilerParams(vmem_limit_bytes=room * 1024 * 1024),
        cost_estimate=pl.CostEstimate(flops=cost, bytes_accessed=1000000, transcendentals=0),
    )(*inputs)


def exchange(block, axes):
    return lax.all_to_all(block, axes, split_axis=0, concat_axis=0, tiled=True)


def per_device(coeffs, v_local, atom_pos, atom_charge, near_list, live_count):
    cosines = cosine_table()
    table, turned = jnp.asarray(cosines, bf16), jnp.asarray(cosines.T, bf16)
    coeffs = coeffs[0]
    (own,) = call(
        pick_kernel,
        [near_list.reshape(1, CAP), live_count, atom_pos, atom_charge.reshape(1, ATOMS)],
        [((SHARES, 1, 128), bf16)],
        [
            ((1, CAP), jnp.int32),
            ((3, ATOMS), f32),
            ((1, ATOMS), f32),
            pltpu.SemaphoreType.DMA((3,)),
        ],
        specs=[
            pl.BlockSpec(memory_space=pl.ANY),
            SMEM,
            pl.BlockSpec(memory_space=pl.ANY),
            pl.BlockSpec(memory_space=pl.ANY),
        ],
        room=60,
    )
    group = exchange(own, GROUP)
    (sections,) = call(
        section_kernel,
        [coeffs, table],
        [((SHARES, 64, GRID), bf16)],
        [((GRID, 8, GRID), f32)],
    )
    (message,) = call(
        attach_kernel,
        [sections, group.reshape(SHARES, 128)],
        [((SHARES, 80, GRID), bf16)],
    )
    got = exchange(message, "gvec")
    stats, hot, halved, drawn, local = call(
        stats_kernel,
        [near_list, live_count, coeffs, v_local],
        [
            ((1, 128), f32),
            ((128, ATOMS), bf16),
            ((8, GRID, GRID), f32),
            ((8, GRID, GRID), f32),
            ((8, GRID, GRID), f32),
        ],
        [((GRID, 8, GRID), f32)],
    )
    potential, slots, blocks = call(
        potential_kernel,
        [got],
        [((8, GRID, GRID), f32), ((8, LIVE), f32), ((OWNERS, 128), f32)],
        [((4, GRID, LIVE), f32), ((4, GRID, LIVE), bf16)],
    )
    back, density, energy = call(
        field_kernel,
        [got, local, table, turned, potential, stats],
        [
            ((SHARES, 64, GRID), bf16),
            ((8, GRID, GRID), f32),
            ((1, 128), f32),
        ],
        [((SHARES, 64, GRID), f32)],
    )
    returned = exchange(back, "gvec")
    (forces,) = call(
        force_kernel,
        [blocks, density, slots],
        [((OWNERS, 128), f32)],
        [
            ((8, GRID, GRID), bf16),
            ((4, 2, GRID, LIVE), bf16),
            ((4, GRID, LIVE), f32),
            ((4, GRID, LIVE), f32),
            ((4, 8, LIVE), f32),
            ((4, 8, LIVE), f32),
            ((8, LIVE), f32),
        ],
    )
    ahead, message = call(
        image_kernel,
        [returned, coeffs, table, turned, forces, energy, halved],
        [((8, GRID, GRID), f32), ((OWNERS, 128), f32)],
        [((GRID, 8, GRID), f32), ((8, GRID, GRID), f32)],
    )
    arrived = exchange(message.reshape(OWNERS, 1, 128), EVERY).reshape(OWNERS, 128)
    waves, atom_force, energies, ratio, totals = call(
        final_kernel,
        [arrived, ahead, drawn, hot],
        [
            ((8, GRID, GRID), bf16),
            ((3, ATOMS), f32),
            ((1, 1), f32),
            ((1, 1), f32),
            ((1, 8), f32),
        ],
    )
    return (waves[None], energies.reshape(1), ratio.reshape(1), atom_force, totals.reshape(8))


def solution(mesh):
    return jax.shard_map(
        per_device,
        mesh=mesh,
        in_specs=(
            P(("band", "dom"), "gvec", None, None),
            P(None, "gvec", None),
            P(None, ("band", "gvec", "dom")),
            P(("band", "gvec", "dom")),
            P(("band", "gvec", "dom")),
            P(("band", "gvec", "dom")),
        ),
        out_specs=(
            P(("band", "dom"), "gvec", None, None),
            P(("band", "dom")),
            P(("band", "dom")),
            P(None, ("band", "gvec", "dom")),
            P(),
        ),
        check_vma=False,
    )
```
